32 devices in a mesh: dp: 4 (over y, x), seq: 8 (over z, core).
Axes of the slice: x: 2, y: 2, z: 4, core: 2. Of those that a mesh axis runs over, the one named last changes fastest.
Arguments:
- inputs: bfloat16 [4, 2048, 1024], P('dp', 'seq'), may hold values from -6 to 6
- encoder_states: bfloat16 [4, 1024, 1024], P('dp', 'seq'), may hold values from -6 to 6
- segment_ids: int32 [4, 2048], P('dp'), may hold values from 0 to 3, never falling along the last dimension, each value on 1 to 1024 neighbouring positions
- encoder_ids: int32 [4, 1024], P('dp'), may hold values from 0 to 3, never falling along the last dimension, each value on 1 to 512 neighbouring positions
- norm_gains: bfloat16 [3, 1024], replicated, may hold values from 0.5 to 1.5
- norm_shifts: bfloat16 [3, 1024], replicated, may hold values from -1 to 1
- attend_weights: bfloat16 [1024, 3072], P('dp', 'seq'), may hold values from -0.1875 to 0.1875
- attend_output: bfloat16 [1024, 1024], P('seq', 'dp'), may hold values from -3 to 3
- attend_biases: bfloat16 [3, 1024], replicated, may hold values from -0.29882812 to 0.29882812
- cross_query: bfloat16 [1024, 1024], P('dp', 'seq'), may hold values from -0.1875 to 0.1875
- cross_memory: bfloat16 [1024, 2048], P('dp', 'seq'), may hold values from -0.1875 to 0.1875
- cross_output: bfloat16 [1024, 1024], P('seq', 'dp'), may hold values from -3 to 3
- cross_biases: bfloat16 [3, 1024], replicated, may hold values from -0.29882812 to 0.29882812
- expand_weight: bfloat16 [1024, 8192], P('dp', 'seq'), may hold values from -0.1875 to 0.1875
- expand_bias: bfloat16 [8192], replicated, may hold values from -3 to 3
- shrink_weight: bfloat16 [8192, 1024], P('seq', 'dp'), may hold values from -0.0625 to 0.0625
- shrink_bias: bfloat16 [1024], replicated, may hold values from -1 to 1
- output_cotangent: bfloat16 [4, 2048, 1024], P('dp', 'seq'), may hold values from -6 to 6
Outputs:
- layer_output: bfloat16 [4, 2048, 1024], P('dp', 'seq')
- input_gradient: bfloat16 [4, 2048, 1024], P('dp', 'seq')
- encoder_gradient: bfloat16 [4, 1024, 1024], P('dp', 'seq')
- norm_gains_grad: float32 [3, 1024], replicated
- norm_shifts_grad: float32 [3, 1024], replicated
- attend_weights_grad: float32 [1024, 3072], P('dp', 'seq')
- attend_output_grad: float32 [1024, 1024], P('seq', 'dp')
- attend_biases_grad: float32 [3, 1024], replicated
- cross_query_grad: float32 [1024, 1024], P('dp', 'seq')
- cross_memory_grad: float32 [1024, 2048], P('dp', 'seq')
- cross_output_grad: float32 [1024, 1024], P('seq', 'dp')
- cross_biases_grad: float32 [3, 1024], replicated
- expand_weight_grad: float32 [1024, 8192], P('dp', 'seq')
- expand_bias_grad: float32 [8192], replicated
- shrink_weight_grad: float32 [8192, 1024], P('seq', 'dp')
- shrink_bias_grad: float32 [1024], replicated
The draws below stay inside these ranges and needn't reach their ends.
Inputs may be any that keep to these rules, and one draw needn't show every extreme that they name: `segment_ids`: in each pack the document numbers never fall; every document 0 to 3 holds 1 to 1024 tokens, and one holds exactly 1024. `encoder_ids`: in each pack the document numbers never fall; every document 0 to 3 has 1 to 512 encoder states, and one has exactly 512.
All inputs are finite; a program needn't handle non-finite values.
Results may differ from the reference program's by a relative error of at most 0.024.
Values may be sent and summed in bfloat16 or wider, within the bound.
No kernel may reach another device: no remote copies, remote signals or barrier semaphores. Data moves between devices by JAX's collectives and lax.ppermute only.
A program may use at most 256 MiB of HBM per device.

```python
import math
import jax
import jax.numpy as jnp
import numpy as np
from jax import lax

D = 1024
HEADS = 16
FF = 8192
PACK = 2048
DOCS = 4
DOC_MOST = 1024
ENC_PACK = 1024
ENC_MOST = 512
N_DP = 4


def level_of(own_key, dims, cuts, least, high):
    level, own = 1.0, jax.random.fold_in(own_key, 6)
    for dim, blocks in cuts:
        draws = jnp.exp(jax.random.uniform(jax.random.fold_in(own, dim), (blocks,), jnp.float32, least / len(cuts), high / len(cuts)))
        level = level * jnp.repeat(draws, dims[dim] // blocks).reshape([-1 if axis == dim else 1 for axis in range(len(dims))])
    return level


def profile(count, total, limit, slope):
    loads = [(1 << 20) // math.isqrt(grade ** slope) + 1 for grade in range(2, count + 1)]
    surplus, holding = total - limit - (count - 1), [1] * (count - 1)
    while surplus > 0:
        movable = [i for i in range(count - 1) if holding[i] < limit]
        pool, remaining = sum([loads[i] for i in movable]), surplus
        for i in movable:
            addition = min(limit - holding[i], max(1, remaining * loads[i] // pool), surplus)
            holding[i] = holding[i] + addition
            surplus = surplus - addition
    return np.array([limit] + holding)


def ragged_sizes(stream_key, number_of, total, bound, lean):
    if number_of == 2:
        one = jax.random.randint(stream_key, (), max(1, total - bound), min(bound, total - 1) + 1)
        return jnp.stack([one, total - one])
    tallies = jnp.asarray(profile(number_of, total, bound, lean), jnp.int32)
    couples = (number_of - 1) // 2
    donor, sink = tallies[1:1 + 2 * couples:2], tallies[2:2 + 2 * couples:2]
    slack = jnp.minimum(donor - 1, bound - sink)
    passed = jax.random.randint(jax.random.fold_in(stream_key, 1), (couples,), 0, 1 << 20) % (slack + 1)
    tallies = tallies.at[1:1 + 2 * couples:2].set(donor - passed).at[2:2 + 2 * couples:2].set(sink + passed)
    return tallies[jax.random.permutation(jax.random.fold_in(stream_key, 2), number_of)]


def normal_values(stream_key, shape, width, bound, shards=(), kind=jnp.bfloat16):
    drawn = jax.random.normal(stream_key, shape, jnp.float32) * width
    if len(shards) > 0:
        drawn = level_of(stream_key, shape, shards, -0.22, 0.18) * drawn
    return jnp.clip(drawn, min=-bound, max=bound).astype(kind)


def setup_inputs(seed: int = 0) -> dict:
    key_list = jax.random.split(jax.random.key(seed), 19)
    inputs = normal_values(key_list[0], (N_DP, PACK, D), 1.0, 6.0, ((0, 4), (1, 8)))
    encoder_states = normal_values(key_list[1], (N_DP, ENC_PACK, D), 1.0, 6.0, ((0, 4), (1, 8)))
    segment_ids = jax.vmap(lambda own: jnp.searchsorted(jnp.cumsum(ragged_sizes(own, DOCS, PACK, DOC_MOST, 1)), jnp.arange(PACK), side="right"))(jax.random.split(key_list[2], N_DP)).reshape((N_DP, PACK)).astype(jnp.int32)
    encoder_ids = jax.vmap(lambda own: jnp.searchsorted(jnp.cumsum(ragged_sizes(own, DOCS, ENC_PACK, ENC_MOST, 1)), jnp.arange(ENC_PACK), side="right"))(jax.random.split(key_list[3], N_DP)).reshape((N_DP, ENC_PACK)).astype(jnp.int32)
    norm_gains = jnp.clip(1.0 + 0.1 * jax.random.normal(key_list[4], (3, D), jnp.float32), 0.5, 1.5).astype(jnp.bfloat16)
    norm_shifts = normal_values(key_list[5], (3, D), 0.2, 1.0)
    attend_weights = normal_values(key_list[6], (D, 3 * D), D ** -0.5, 0.1875, ((0, 4), (1, 8)))
    attend_output = normal_values(key_list[7], (D, D), 4 ** -0.5, 3.0, ((0, 8), (1, 4)))
    attend_biases = normal_values(key_list[8], (3, D), 0.05, 0.29882812)
    cross_query = normal_values(key_list[9], (D, D), D ** -0.5, 0.1875, ((0, 4), (1, 8)))
    cross_memory = normal_values(key_list[10], (D, 2 * D), D ** -0.5, 0.1875, ((0, 4), (1, 8)))
    cross_output = normal_values(key_list[11], (D, D), 4 ** -0.5, 3.0, ((0, 8), (1, 4)))
    cross_biases = normal_values(key_list[12], (3, D), 0.05, 0.29882812)
    expand_weight = normal_values(key_list[13], (D, FF), D ** -0.5, 0.1875, ((0, 4), (1, 8)))
    expand_bias = normal_values(key_list[14], (FF,), 0.5, 3.0)
    shrink_weight = normal_values(key_list[15], (FF, D), FF ** -0.5, 0.0625, ((0, 8), (1, 4)))
    shrink_bias = normal_values(key_list[16], (D,), 0.2, 1.0)
    output_cotangent = normal_values(key_list[17], (N_DP, PACK, D), 1.0, 6.0, ((0, 4), (1, 8)))
    return dict(inputs=inputs, encoder_states=encoder_states, segment_ids=segment_ids, encoder_ids=encoder_ids, norm_gains=norm_gains, norm_shifts=norm_shifts, attend_weights=attend_weights, attend_output=attend_output, attend_biases=attend_biases, cross_query=cross_query, cross_memory=cross_memory, cross_output=cross_output, cross_biases=cross_biases, expand_weight=expand_weight, expand_bias=expand_bias, shrink_weight=shrink_weight, shrink_bias=shrink_bias, output_cotangent=output_cotangent)


@jax.custom_vjp
def low(v):
    return lax.optimization_barrier(v.astype(jnp.bfloat16)).astype(jnp.float32)

@jax.custom_vjp
def low_back(v):
    return v

def low_keep(v):
    return (low(v), None)

def low_pass(kept, grad):
    return (grad,)

def back_keep(v):
    return (v, None)

def back_low(kept, grad):
    return (low(grad),)
low.defvjp(low_keep, low_pass)
low_back.defvjp(back_keep, back_low)
epsilon = 1e-05
masked_score = -1e+30

def layer_norm(values, gain_row, shift_row):
    center = values - lax.optimization_barrier(jnp.mean(values, axis=-1, keepdims=True))
    spread = lax.optimization_barrier(jnp.mean(center * center, axis=-1, keepdims=True))
    return center * lax.rsqrt(spread + epsilon) * gain_row + shift_row

def matmul(former, latter):
    return jnp.dot(former, latter, precision=lax.Precision.HIGHEST)

def blocked_attention(queries, key_rows, values, query_ids, key_ids, causal, key_window):
    row_count = queries.shape[0]
    key_count = key_rows.shape[0]
    block_rows = min(512, row_count)
    scaling = 1.0 / math.sqrt(queries.shape[2])

    def one_block(block_index):
        row_start = block_index * block_rows
        key_start = jnp.clip(row_start + block_rows - key_window, 0, key_count - key_window).astype(jnp.int32)
        query_part = lax.dynamic_slice_in_dim(queries, row_start, block_rows, 0)
        key_part = lax.dynamic_slice_in_dim(key_rows, key_start, key_window, 0)
        value_part = lax.dynamic_slice_in_dim(values, key_start, key_window, 0)
        query_seg = lax.dynamic_slice_in_dim(query_ids, row_start, block_rows, 0)
        key_seg = lax.dynamic_slice_in_dim(key_ids, key_start, key_window, 0)
        allowed = query_seg[:, None] == key_seg[None, :]
        if causal:
            query_pos = row_start + jnp.arange(block_rows, dtype=jnp.int32)
            key_pos = key_start + jnp.arange(key_window, dtype=jnp.int32)
            allowed = allowed & (key_pos[None, :] <= query_pos[:, None])
        scores = jnp.einsum('qhe,khe->hqk', query_part, key_part, precision=lax.Precision.HIGHEST) * scaling
        scores = low_back(scores)
        scores = jnp.where(allowed[None], scores, masked_score)
        row_max = lax.optimization_barrier(jnp.max(scores, axis=-1, keepdims=True))
        exponent = jnp.exp(scores - row_max)
        weights = low(exponent / lax.optimization_barrier(jnp.sum(exponent, axis=-1, keepdims=True)))
        return jnp.einsum('hqk,khe->qhe', weights, value_part, precision=lax.Precision.HIGHEST)
    parts = lax.map(jax.checkpoint(one_block), jnp.arange(row_count // block_rows, dtype=jnp.int32))
    return parts.reshape(queries.shape)

def pack_forward(tokens, encoder, params, pack_ids, memory_ids):
    gains, shifts, attend_w, attend_o, attend_b, cross_q, cross_kv, cross_o, cross_b, expand_w, expand_b, shrink_w, shrink_b = params
    row_count, model_width = tokens.shape
    head_width = model_width // HEADS
    memory_rows = encoder.shape[0]
    self_window = min(row_count, min(512, row_count) + DOC_MOST)
    normed1 = low(layer_norm(tokens, gains[0], shifts[0]))
    projected = matmul(normed1, attend_w).reshape(row_count, HEADS, 3, head_width)
    query1 = low(low_back(projected[:, :, 0] + attend_b[0].reshape(HEADS, head_width)))
    key1 = low(low_back(projected[:, :, 1]))
    value1 = low(low_back(projected[:, :, 2] + attend_b[1].reshape(HEADS, head_width)))
    context1 = low(low_back(blocked_attention(query1, key1, value1, pack_ids, pack_ids, True, self_window)))
    middle = tokens + low_back(matmul(context1.reshape(row_count, model_width), attend_o) + attend_b[2])
    normed2 = low(layer_norm(middle, gains[1], shifts[1]))
    query2 = low(low_back((matmul(normed2, cross_q) + cross_b[0]).reshape(row_count, HEADS, head_width)))
    memory = matmul(encoder, cross_kv).reshape(memory_rows, HEADS, 2, head_width)
    key2 = low(low_back(memory[:, :, 0]))
    value2 = low(low_back(memory[:, :, 1] + cross_b[1].reshape(HEADS, head_width)))
    context2 = low(low_back(blocked_attention(query2, key2, value2, pack_ids, memory_ids, False, memory_rows)))
    later = middle + low_back(matmul(context2.reshape(row_count, model_width), cross_o) + cross_b[2])
    normed3 = low(layer_norm(later, gains[2], shifts[2]))
    hidden = low_back(matmul(normed3, expand_w) + expand_b)
    active = low(jax.nn.gelu(hidden))
    return later + low_back(matmul(active, shrink_w) + shrink_b)

def reference(inputs, encoder_states, segment_ids, encoder_ids, norm_gains, norm_shifts, attend_weights, attend_output, attend_biases, cross_query, cross_memory, cross_output, cross_biases, expand_weight, expand_bias, shrink_weight, shrink_bias, output_cotangent):
    params = tuple((argument.astype(jnp.float32) for argument in (norm_gains, norm_shifts, attend_weights, attend_output, attend_biases, cross_query, cross_memory, cross_output, cross_biases, expand_weight, expand_bias, shrink_weight, shrink_bias)))

    def per_pack(totals, packed):
        tokens, memory, pack_ids, memory_ids, cotangent = packed

        def forward(token_rows, memory_rows, weights):
            return pack_forward(token_rows, memory_rows, weights, pack_ids, memory_ids)
        result, pullback = jax.vjp(forward, tokens.astype(jnp.float32), memory.astype(jnp.float32), params)
        token_grad, memory_grad, param_grads = pullback(cotangent.astype(jnp.float32))
        totals = jax.tree.map(jnp.add, totals, param_grads)
        return (totals, (result.astype(jnp.bfloat16), token_grad.astype(jnp.bfloat16), memory_grad.astype(jnp.bfloat16)))
    empty_sums = jax.tree.map(jnp.zeros_like, params)
    totals, (outputs, token_grads, memory_grads) = lax.scan(per_pack, empty_sums, (inputs, encoder_states, segment_ids, encoder_ids, output_cotangent))
    return (outputs, token_grads, memory_grads) + tuple(totals)
```

```python
import functools
import math

import jax
import jax.numpy as jnp
from jax import lax
from jax.experimental import pallas as pl
from jax.experimental.pallas import tpu as pltpu
from jax.sharding import Mesh
from jax.sharding import PartitionSpec as P

HEADS = 16

epsilon = 1e-05
masked_score = -1e30
head_width = 64


def piece_slot(position, own, relative):
    return position ^ own if relative else position


def load_block(ref, core, plane, own, relative):
    parts = [
        ref[piece_slot(piece, own[0], relative), piece_slot(core, own[1], relative), plane]
        for piece in range(ref.shape[0])
    ]
    return jnp.concatenate(parts, axis=0)


def load_rows(ref, own, relative):
    parts = [ref[piece_slot(piece, own[0], relative), 0, 0] for piece in range(ref.shape[0])]
    return jnp.concatenate(parts, axis=0)


def store_rows(ref, block, own, relative):
    piece_rows = ref.shape[3]
    for piece in range(ref.shape[0]):
        ref[piece_slot(piece, own[0], relative), 0, 0] = block[
            piece * piece_rows : (piece + 1) * piece_rows
        ]


def head_columns(transposed, heads):
    if heads == 1:
        return transposed
    feature = lax.broadcasted_iota(jnp.int32, transposed.shape, 0) // head_width
    zero = jnp.zeros_like(transposed)
    return jnp.concatenate([jnp.where(feature == h, transposed, zero) for h in range(heads)], axis=1)


def head_rows(block, heads):
    if heads == 1:
        return block
    feature = lax.broadcasted_iota(jnp.int32, block.shape, 1) // head_width
    zero = jnp.zeros_like(block)
    return jnp.concatenate([jnp.where(feature == h, block, zero) for h in range(heads)], axis=0)


def flip(block):
    return jnp.transpose(block.astype(jnp.float32), (1, 0)).astype(block.dtype)


def repeat_heads(row, heads):
    return row if heads == 1 else jnp.concatenate([row] * heads, axis=1)


def forward_kernel(
    scalars, q_ref, k_ref, v_ref, first_ref, last_ref, ctx_ref, keep_ref, lse_ref, keys, flipped,
    *, heads, q_rel, kv_rel, key_block,
):
    step = pl.program_id(0)
    steps = pl.num_programs(0)
    own = (scalars[0], scalars[1])
    cores, planes = k_ref.shape[1], k_ref.shape[2]
    group = k_ref.shape[0] * k_ref.shape[3]

    @pl.when(step == 0)
    def _():
        for plane in range(planes):
            for core in range(cores):
                start = (plane * cores + core) * group
                keys[start : start + group, :] = load_block(k_ref, core, plane, own, kv_rel)
                values = load_block(v_ref, core, plane, own, kv_rel)
                offset = start % key_block
                flipped[start // key_block, :, offset : offset + group] = flip(values)

    rows = q_ref.shape[0] * q_ref.shape[3]
    query = load_rows(q_ref, own, q_rel) * jnp.asarray(1.0 / math.sqrt(head_width), jnp.bfloat16)
    columns = head_columns(flip(query), heads)
    first = repeat_heads(first_ref[0], heads)
    last = repeat_heads(last_ref[0], heads)

    def one(block, carry):
        peak, total, sums = carry
        start = pl.multiple_of(block * key_block, key_block)
        scores = jnp.dot(keys[pl.ds(start, key_block), :], columns, preferred_element_type=jnp.float32)
        place = start + lax.broadcasted_iota(jnp.int32, scores.shape, 0)
        scores = jnp.where((place >= first) & (place <= last), scores, masked_score)
        newer = jnp.maximum(peak, jnp.max(scores, axis=0, keepdims=True))
        shrink = jnp.exp(peak - newer)
        exponent = jnp.exp(scores - newer)
        total = total * shrink + jnp.sum(exponent, axis=0, keepdims=True)
        low = exponent.astype(jnp.bfloat16)
        turned = flipped[block]
        fresh = []
        for h in range(heads):
            part = jnp.dot(
                turned[h * head_width : (h + 1) * head_width],
                low[:, h * rows : (h + 1) * rows],
                preferred_element_type=jnp.float32,
            )
            fresh.append(sums[h] * shrink[:, h * rows : (h + 1) * rows] + part)
        return (newer, total, tuple(fresh))

    empty = (
        jnp.full((1, heads * rows), masked_score, jnp.float32),
        jnp.zeros((1, heads * rows), jnp.float32),
        tuple(jnp.zeros((head_width, rows), jnp.float32) for _ in range(heads)),
    )
    peak, total, sums = lax.fori_loop(scalars[2 + step], scalars[2 + steps + step] + 1, one, empty)
    context = jnp.concatenate(
        [sums[h] / total[:, h * rows : (h + 1) * rows] for h in range(heads)], axis=0
    )
    keep_ref[0] = context
    lse_ref[0] = peak + jnp.log(total)
    store_rows(ctx_ref, jnp.transpose(context, (1, 0)).astype(jnp.bfloat16), own, False)


def backward_kernel(
    scalars, q_ref, k_ref, v_ref, dc_ref, keep_ref, lse_ref, first_ref, last_ref,
    dq_ref, dkv_ref, keys, values, flipped, dkeys, dvalues,
    *, heads, q_rel, kv_rel, key_block,
):
    step = pl.program_id(0)
    steps = pl.num_programs(0)
    own = (scalars[0], scalars[1])
    pieces, cores, planes, piece_rows = k_ref.shape[:4]
    group = pieces * piece_rows
    width = heads * head_width
    scaling = 1.0 / math.sqrt(head_width)

    @pl.when(step == 0)
    def _():
        for plane in range(planes):
            for core in range(cores):
                start = (plane * cores + core) * group
                block = load_block(k_ref, core, plane, own, kv_rel)
                keys[start : start + group, :] = block
                offset = start % key_block
                flipped[start // key_block, :, offset : offset + group] = flip(block)
                values[start : start + group, :] = load_block(v_ref, core, plane, own, kv_rel)
        dkeys[...] = jnp.zeros_like(dkeys)
        dvalues[...] = jnp.zeros_like(dvalues)

    rows = q_ref.shape[0] * q_ref.shape[3]
    query = load_rows(q_ref, own, q_rel) * jnp.asarray(scaling, jnp.bfloat16)
    grad = load_rows(dc_ref, own, False)
    turned_grad = flip(grad)
    query_columns = head_columns(flip(query), heads)
    grad_columns = head_columns(turned_grad, heads)
    query_rows = head_rows(query, heads)
    grad_rows = head_rows(grad, heads)
    product = turned_grad.astype(jnp.float32) * keep_ref[0]
    center = jnp.concatenate(
        [
            jnp.sum(product[h * head_width : (h + 1) * head_width], axis=0, keepdims=True)
            for h in range(heads)
        ],
        axis=1,
    )
    first = repeat_heads(first_ref[0], heads)
    last = repeat_heads(last_ref[0], heads)
    lse = lse_ref[0]

    def one(block, sums):
        start = pl.multiple_of(block * key_block, key_block)
        here = pl.ds(start, key_block)
        scores = jnp.dot(keys[here, :], query_columns, preferred_element_type=jnp.float32)
        place = start + lax.broadcasted_iota(jnp.int32, scores.shape, 0)
        scores = jnp.where((place >= first) & (place <= last), scores, masked_score)
        weights = jnp.exp(scores - lse)
        dots = jnp.dot(values[here, :], grad_columns, preferred_element_type=jnp.float32)
        dscore = (weights * (dots - center)).astype(jnp.bfloat16)
        dvalues[here, :] += jnp.dot(
            weights.astype(jnp.bfloat16), grad_rows, preferred_element_type=jnp.float32
        )
        dkeys[here, :] += jnp.dot(dscore, query_rows, preferred_element_type=jnp.float32)
        turned = flipped[block]
        return tuple(
            sums[h]
            + jnp.dot(
                turned[h * head_width : (h + 1) * head_width],
                dscore[:, h * rows : (h + 1) * rows],
                preferred_element_type=jnp.float32,
            )
            for h in range(heads)
        )

    empty = tuple(jnp.zeros((head_width, rows), jnp.float32) for _ in range(heads))
    sums = lax.fori_loop(scalars[2 + step], scalars[2 + steps + step] + 1, one, empty)
    dquery = jnp.transpose(jnp.concatenate(sums, axis=0) * scaling, (1, 0)).astype(jnp.bfloat16)
    store_rows(dq_ref, dquery, own, q_rel)

    @pl.when(step == steps - 1)
    def _():
        for plane in range(planes):
            for core in range(cores):
                start = (plane * cores + core) * group
                dk = dkeys[start : start + group, :].astype(jnp.bfloat16)
                dv = dvalues[start : start + group, :].astype(jnp.bfloat16)
                for piece in range(pieces):
                    slot = (piece_slot(piece, own[0], kv_rel), piece_slot(core, own[1], kv_rel), plane)
                    span = slice(piece * piece_rows, (piece + 1) * piece_rows)
                    dkv_ref[slot[0], slot[1], slot[2], :, 0:width] = dk[span]
                    dkv_ref[slot[0], slot[1], slot[2], :, width : 2 * width] = dv[span]


def row_spec(shape, width, relative, column=0):
    pieces, cores, planes, piece_rows = shape[:4]

    def place(step, scalars):
        core = lax.rem(step, cores)
        return (0, core ^ scalars[1] if relative else core, lax.div(step, cores), 0, column)

    return pl.BlockSpec((pieces, 1, 1, piece_rows, width), place)


def whole_spec(shape, column=0):
    return pl.BlockSpec(shape, lambda step, scalars: (0,) * (len(shape) - 1) + (column,))


def step_spec(shape):
    return pl.BlockSpec((1,) + shape[1:], lambda step, scalars: (step, 0, 0))


def pick(array, column, width):
    if width % 128 == 0:
        return (array, column)
    return (array[..., column * width : (column + 1) * width], 0)


def attend(scalars, queries, key_rows, values, first, last, width, q_rel, kv_rel):
    heads = width // head_width
    q_array, q_column = queries
    pieces, cores, planes, q_rows = q_array.shape[:4]
    steps = cores * planes
    rows = pieces * q_rows
    key_shape = key_rows[0].shape[:4]
    key_count = math.prod(key_shape)
    key_block = min(256, key_count)
    out_shape = (
        jax.ShapeDtypeStruct((pieces, cores, planes, q_rows, width), jnp.bfloat16),
        jax.ShapeDtypeStruct((steps, width, rows), jnp.float32),
        jax.ShapeDtypeStruct((steps, 1, heads * rows), jnp.float32),
    )
    return pl.pallas_call(
        functools.partial(
            forward_kernel, heads=heads, q_rel=q_rel, kv_rel=kv_rel, key_block=key_block
        ),
        grid_spec=pltpu.PrefetchScalarGridSpec(
            num_scalar_prefetch=1,
            grid=(steps,),
            in_specs=[
                row_spec(q_array.shape, width, q_rel, q_column),
                whole_spec(key_shape + (width,), key_rows[1]),
                whole_spec(key_shape + (width,), values[1]),
                step_spec(first.shape),
                step_spec(last.shape),
            ],
            out_specs=[
                row_spec(q_array.shape, width, False),
                step_spec(out_shape[1].shape),
                step_spec(out_shape[2].shape),
            ],
            scratch_shapes=[
                pltpu.VMEM((key_count, width), jnp.bfloat16),
                pltpu.VMEM((key_count // key_block, width, key_block), jnp.bfloat16),
            ],
        ),
        out_shape=out_shape,
        compiler_params=pltpu.CompilerParams(vmem_limit_bytes=32 * 2**20),
    )(scalars, q_array, key_rows[0], values[0], first, last)


def attend_back(
    scalars, queries, key_rows, values, grad, kept, lse, first, last, width, q_rel, kv_rel
):
    heads = width // head_width
    q_array, q_column = queries
    pieces, cores, planes, q_rows = q_array.shape[:4]
    steps = cores * planes
    key_shape = key_rows[0].shape[:4]
    key_count = math.prod(key_shape)
    key_block = min(256, key_count)
    out_shape = (
        jax.ShapeDtypeStruct((pieces, cores, planes, q_rows, width), jnp.bfloat16),
        jax.ShapeDtypeStruct(key_shape + (2 * width,), jnp.bfloat16),
    )
    return pl.pallas_call(
        functools.partial(
            backward_kernel, heads=heads, q_rel=q_rel, kv_rel=kv_rel, key_block=key_block
        ),
        grid_spec=pltpu.PrefetchScalarGridSpec(
            num_scalar_prefetch=1,
            grid=(steps,),
            in_specs=[
                row_spec(q_array.shape, width, q_rel, q_column),
                whole_spec(key_shape + (width,), key_rows[1]),
                whole_spec(key_shape + (width,), values[1]),
                row_spec(q_array.shape, width, False),
                step_spec(kept.shape),
                step_spec(lse.shape),
                step_spec(first.shape),
                step_spec(last.shape),
            ],
            out_specs=[
                row_spec(q_array.shape, width, q_rel),
                whole_spec(key_shape + (2 * width,)),
            ],
            scratch_shapes=[
                pltpu.VMEM((key_count, width), jnp.bfloat16),
                pltpu.VMEM((key_count, width), jnp.bfloat16),
                pltpu.VMEM((key_count // key_block, width, key_block), jnp.bfloat16),
                pltpu.VMEM((key_count, width), jnp.float32),
                pltpu.VMEM((key_count, width), jnp.float32),
            ],
        ),
        out_shape=out_shape,
        compiler_params=pltpu.CompilerParams(vmem_limit_bytes=32 * 2**20),
    )(scalars, q_array, key_rows[0], values[0], grad, kept, lse, first, last)


def layer_norm(values, gain_row, shift_row):
    center = values - jnp.mean(values, axis=-1, keepdims=True)
    spread = jnp.mean(center * center, axis=-1, keepdims=True)
    return center * lax.rsqrt(spread + epsilon) * gain_row + shift_row


def inner_rows(former, latter):
    return lax.dot_general(
        former, latter, (((0,), (0,)), ((), ())), preferred_element_type=jnp.float32
    )


def against(former, latter):
    return lax.dot_general(
        former, latter, (((1,), (1,)), ((), ())), preferred_element_type=jnp.float32
    )


def product(former, latter):
    return jnp.dot(former, latter, preferred_element_type=jnp.float32)


def low(values):
    return values.astype(jnp.bfloat16)


def wide(values):
    return values.astype(jnp.float32)


def other(values, axis, shift):
    count = lax.axis_size(axis)
    return lax.ppermute(values, axis, [(i, i ^ shift) for i in range(count)])


def trade(values, axis, split, concat):
    return lax.all_to_all(values, axis, split_axis=split, concat_axis=concat, tiled=True)


PLANE = ("dp", "core")


def swap_in(block):
    return trade(trade(block, "dp", 0, 0), "z", 0, 0)


def swap_out(block):
    return trade(trade(block, "z", 0, 0), "dp", 0, 0)


def plane_gather(block):
    pieces = [block] + [other(block, "dp", m) for m in range(1, lax.axis_size("dp"))]
    return [jnp.stack([piece, other(piece, "core", 1)]) for piece in pieces]


def plane_reduce(parts):
    sums = [part[0] + wide(other(low(part[1]), "core", 1)) for part in parts]
    total = sums[0]
    for m in range(1, len(sums)):
        total = total + wide(other(low(sums[m]), "dp", m))
    return total


def sum_blocks(parts, axis):
    return jnp.sum(wide(trade(low(parts), axis, 0, 0)), axis=0)


def fetch_heads(weight):
    rows = weight.shape[0]
    whole = lax.all_gather(weight, "z", axis=0, tiled=True)
    return trade(whole, "dp", 0, 0)


def return_heads(grad):
    planes = lax.axis_size("z")
    mine = trade(low(grad), "dp", 0, 0)
    return sum_blocks(mine.reshape((planes, mine.shape[0] // planes, mine.shape[1])), "z")


def fetch_square(weights):
    kinds, rows, width = weights.shape
    planes, cores, pieces = lax.axis_size("z"), lax.axis_size("core"), lax.axis_size("dp")
    core, piece = lax.axis_index("core"), lax.axis_index("dp")
    part = lax.all_gather(weights, "z", axis=1, tiled=False)
    pair = jnp.zeros((kinds, planes, cores, rows, width), weights.dtype)
    for shift, block in enumerate((part, other(part, "core", 1))):
        pair = lax.dynamic_update_slice(pair, block[:, :, None], (0, 0, core ^ shift, 0, 0))
    whole = jnp.zeros((kinds, planes, cores, rows, pieces * width), weights.dtype)
    for shift in range(pieces):
        block = pair if shift == 0 else other(pair, "dp", shift)
        whole = lax.dynamic_update_slice(whole, block, (0, 0, 0, 0, (piece ^ shift) * width))
    return whole.reshape(kinds, planes * cores * rows, pieces * width)


def return_square(grads):
    planes, cores, pieces = lax.axis_size("z"), lax.axis_size("core"), lax.axis_size("dp")
    kinds, rows, width = grads.shape
    split = low(grads).reshape(
        kinds, planes, cores, rows // (planes * cores), pieces, width // pieces
    )
    split = split.transpose(2, 4, 1, 0, 3, 5)
    for axis in ("core", "dp", "z"):
        split = sum_blocks(split, axis)
    return split


def fetch_units(expand, shrink):
    width = expand.shape[0] * lax.axis_size("dp")
    former = trade(expand, "dp", 1, 0).T
    latter = trade(shrink, "dp", 0, 1)
    whole = lax.all_gather(
        jnp.concatenate([former, latter], axis=1), "z", axis=0, tiled=True
    )
    return (whole[:, :width], whole[:, width:])


def return_units(expand_grad, shrink_grad):
    width = expand_grad.shape[1]
    both = low(jnp.concatenate([expand_grad, shrink_grad], axis=1))
    mine = lax.psum_scatter(both, "z", scatter_dimension=0, tiled=True)
    former = trade(mine[:, :width].T, "dp", 0, 1)
    latter = trade(mine[:, width:], "dp", 1, 0)
    return (wide(former), wide(latter))


def sum_all(values):
    for axis in ("core", "dp", "z"):
        shift = 1
        while shift < lax.axis_size(axis):
            values = values + other(values, axis, shift)
            shift *= 2
    return values


def document_edges(ids, memory_ids, steps):
    documents = jnp.arange(4, dtype=jnp.int32)
    starts = jnp.sum((memory_ids[None] < documents[:, None]).astype(jnp.int32), axis=1)
    ends = jnp.sum((memory_ids[None] <= documents[:, None]).astype(jnp.int32), axis=1) - 1
    match = ids[None] == documents[:, None]
    first = jnp.sum(jnp.where(match, starts[:, None], 0), axis=0)
    last = jnp.sum(jnp.where(match, ends[:, None], 0), axis=0)
    return (first.reshape(steps, 1, -1), last.reshape(steps, 1, -1))


def shards(
    inputs,
    encoder_states,
    segment_ids,
    encoder_ids,
    norm_gains,
    norm_shifts,
    attend_weights,
    attend_output,
    attend_biases,
    cross_query,
    cross_memory,
    cross_output,
    cross_biases,
    expand_weight,
    expand_bias,
    shrink_weight,
    shrink_bias,
    output_cotangent,
):
    pieces, planes, cores = lax.axis_size("dp"), lax.axis_size("z"), lax.axis_size("core")
    piece, plane, core = lax.axis_index("dp"), lax.axis_index("z"), lax.axis_index("core")
    members = pieces * cores
    member = piece * cores + core
    row_count, model_width = inputs.shape[1:]
    memory_rows = encoder_states.shape[1]
    pack_rows, pack_memory = segment_ids.shape[1], encoder_ids.shape[1]
    heads = HEADS // members
    head_size = model_width // HEADS
    width = heads * head_size
    steps = planes * cores
    unit_count = expand_weight.shape[1]

    swapping = [
        ((d * planes + z) * cores + c, (z * planes + d) * cores + c)
        for d in range(pieces)
        for z in range(planes)
        for c in range(cores)
    ]
    all_ids = lax.ppermute(
        jnp.concatenate([segment_ids[0], encoder_ids[0]]), ("dp", "z", "core"), swapping
    )
    pack_ids, memory_ids = all_ids[:pack_rows], all_ids[pack_rows:]
    raw = swap_in(inputs[0])
    attend_w = fetch_heads(attend_weights)
    attend_w = (
        attend_w.reshape(model_width, heads, 3, head_size)
        .transpose(0, 2, 1, 3)
        .reshape(model_width, 3 * width)
    )
    encoder = swap_in(encoder_states[0])
    cross_kv = fetch_heads(cross_memory)
    cross_kv = (
        cross_kv.reshape(model_width, heads, 2, head_size)
        .transpose(0, 2, 1, 3)
        .reshape(model_width, 2 * width)
    )
    squares = fetch_square(jnp.stack([attend_output, cross_query.T, cross_output]))
    attend_o, cross_qt, cross_o = squares[0], squares[1], squares[2]
    upstream = swap_in(output_cotangent[0])
    expand_t, shrink_w = fetch_units(expand_weight, shrink_weight)

    own = jnp.stack([piece, core]).astype(jnp.int32)
    key_block = min(256, pack_rows)
    self_first, _ = document_edges(pack_ids, pack_ids, steps)
    self_last = jnp.arange(pack_rows, dtype=jnp.int32).reshape(steps, 1, -1)
    self_scalars = jnp.concatenate(
        [own, self_first[:, 0, 0] // key_block, self_last[:, 0, -1] // key_block]
    )
    cross_first, cross_last = document_edges(pack_ids, memory_ids, steps)
    key_block = min(256, pack_memory)
    cross_scalars = jnp.concatenate(
        [own, cross_first[:, 0, 0] // key_block, cross_last[:, 0, -1] // key_block]
    )

    gain_rows, shift_rows = wide(norm_gains), wide(norm_shifts)
    bias_self, bias_cross = wide(attend_biases), wide(cross_biases)

    def of_heads(row):
        return lax.dynamic_slice_in_dim(row, member * width, width, 0)

    zero_heads = jnp.zeros((width,), jnp.float32)
    packed_bias = jnp.concatenate([of_heads(bias_self[0]), zero_heads, of_heads(bias_self[1])])
    memory_bias = jnp.concatenate([zero_heads, of_heads(bias_cross[1])])

    tokens = wide(raw)
    normed1, norm_back1 = jax.vjp(layer_norm, tokens, gain_rows[0], shift_rows[0])
    all_one = jnp.concatenate(plane_gather(low(normed1))).reshape(pack_rows, model_width)
    packed = low(product(all_one, attend_w) + packed_bias)
    packed = packed.reshape(pieces, cores, planes, row_count // planes, 3 * width)
    self_q, self_k, self_v = (pick(packed, i, width) for i in range(3))
    context1, kept1, lse1 = attend(
        self_scalars, self_q, self_k, self_v, self_first, self_last, width, True, True
    )
    mixed1 = trade(context1.reshape(pack_rows, width), PLANE, 0, 1)
    middle = tokens + product(mixed1, attend_o) + bias_self[2]

    all_encoder = jnp.concatenate(plane_gather(encoder)).reshape(pack_memory, model_width)
    memory = low(product(all_encoder, cross_kv) + memory_bias)
    memory = memory.reshape(pieces, cores, planes, memory_rows // planes, 2 * width)
    normed2, norm_back2 = jax.vjp(layer_norm, middle, gain_rows[1], shift_rows[1])
    low_two = low(normed2)
    query2 = trade(low(against(low_two, cross_qt) + bias_cross[0]), PLANE, 1, 0)
    query2 = query2.reshape(pieces, cores, planes, row_count // planes, width)
    cross_q = (query2, 0)
    cross_k, cross_v = (pick(memory, i, width) for i in range(2))
    context2, kept2, lse2 = attend(
        cross_scalars, cross_q, cross_k, cross_v, cross_first, cross_last, width, False, True
    )
    mixed2 = trade(context2.reshape(pack_rows, width), PLANE, 0, 1)
    later = middle + product(mixed2, cross_o) + bias_cross[2]

    bias_units = wide(expand_bias).reshape(planes, cores, pieces, unit_count // pieces)
    bias_units = lax.dynamic_slice(
        bias_units, (0, core, piece, 0), (planes, 1, 1, unit_count // pieces)
    ).reshape(unit_count)
    normed3, norm_back3 = jax.vjp(layer_norm, later, gain_rows[2], shift_rows[2])
    ups = plane_gather(upstream)
    threes = plane_gather(low(normed3))
    d_threes, outs, actives, d_hiddens = [], [], [], []
    for m in range(pieces):
        up_m = ups[m].reshape(cores * row_count, model_width)
        three_m = threes[m].reshape(cores * row_count, model_width)
        d_active = against(up_m, shrink_w)
        hidden = against(three_m, expand_t) + bias_units
        active, gelu_back = jax.vjp(jax.nn.gelu, hidden)
        d_hidden = low(gelu_back(d_active)[0])
        active = low(active)
        d_threes.append(product(d_hidden, expand_t).reshape(cores, row_count, model_width))
        outs.append(product(active, shrink_w).reshape(cores, row_count, model_width))
        actives.append(active)
        d_hiddens.append(d_hidden)
    d_normed3 = plane_reduce(d_threes)
    back_three = norm_back3(d_normed3)
    d_later = wide(upstream) + back_three[0]
    all_up = jnp.concatenate(ups).reshape(pack_rows, model_width)
    all_three = jnp.concatenate(threes).reshape(pack_rows, model_width)
    all_active, all_d_hidden = jnp.concatenate(actives), jnp.concatenate(d_hiddens)
    layer_output = swap_out(low(later + plane_reduce(outs) + wide(shrink_bias)))
    expand_sum, shrink_sum = return_units(
        inner_rows(all_d_hidden, all_three), inner_rows(all_active, all_up)
    )
    unit_sums = jnp.sum(wide(all_d_hidden), axis=0).reshape(planes, 1, 1, unit_count // pieces)
    unit_sums = lax.dynamic_update_slice(
        jnp.zeros((planes, cores, pieces, unit_count // pieces), jnp.float32),
        unit_sums,
        (0, core, piece, 0),
    ).reshape(-1)
    up_sums = jnp.sum(wide(upstream), axis=0)

    def place_heads(row):
        return lax.dynamic_update_slice(
            jnp.zeros((model_width,), jnp.float32), row, (member * width,)
        )

    low_later = low(d_later)
    d_context2 = trade(low(against(low_later, cross_o)), PLANE, 1, 0)
    d_context2 = d_context2.reshape(pieces, cores, planes, row_count // planes, width)
    d_query2, d_memory = attend_back(
        cross_scalars, cross_q, cross_k, cross_v, d_context2, kept2, lse2,
        cross_first, cross_last, width, False, True,
    )
    query_flat = trade(d_query2.reshape(pack_rows, width), PLANE, 0, 1)
    memory_flat = d_memory.reshape(pack_memory, 2 * width)
    d_normed2 = product(query_flat, cross_qt)
    back_two = norm_back2(d_normed2)
    d_middle = d_later + back_two[0]
    d_encoder = against(memory_flat, cross_kv).reshape(pieces, cores, memory_rows, model_width)
    encoder_gradient = swap_out(low(plane_reduce([d_encoder[m] for m in range(pieces)])))
    cross_squares = return_square(
        jnp.stack([inner_rows(query_flat, low_two), inner_rows(mixed2, low_later)])
    )
    cross_kv_grad = (
        inner_rows(all_encoder, memory_flat)
        .reshape(model_width, 2, heads, head_size)
        .transpose(0, 2, 1, 3)
        .reshape(model_width, 2 * width)
    )
    cross_kv_sum = return_heads(cross_kv_grad)
    cross_b_grad = jnp.stack(
        [
            jnp.sum(wide(query_flat), axis=0),
            place_heads(jnp.sum(wide(memory_flat[:, width:]), axis=0)),
            jnp.sum(wide(low_later), axis=0),
        ]
    )

    low_middle = low(d_middle)
    d_context1 = trade(low(against(low_middle, attend_o)), PLANE, 1, 0)
    d_context1 = d_context1.reshape(pieces, cores, planes, row_count // planes, width)
    attend_o_sum = return_square(inner_rows(mixed1, low_middle)[None])
    d_query1, d_memory1 = attend_back(
        self_scalars, self_q, self_k, self_v, d_context1, kept1, lse1,
        self_first, self_last, width, True, True,
    )
    d_packed = jnp.concatenate(
        [d_query1.reshape(pack_rows, width), d_memory1.reshape(pack_rows, 2 * width)], axis=1
    )
    d_ones = against(d_packed, attend_w).reshape(pieces, cores, row_count, model_width)
    d_normed1 = plane_reduce([d_ones[m] for m in range(pieces)])
    back_one = norm_back1(d_normed1)
    input_gradient = swap_out(low(d_middle + back_one[0]))
    attend_w_grad = (
        inner_rows(all_one, d_packed)
        .reshape(model_width, 3, heads, head_size)
        .transpose(0, 2, 1, 3)
        .reshape(model_width, 3 * width)
    )
    attend_w_sum = return_heads(attend_w_grad)

    early = jnp.concatenate(
        [
            back_two[1],
            back_three[1],
            back_two[2],
            back_three[2],
            jnp.sum(wide(low_middle), axis=0),
            cross_b_grad.reshape(-1),
            up_sums,
            unit_sums,
        ]
    )
    early = lax.psum(early.reshape(-1, 128), ("dp", "z", "core")).reshape(-1)
    head_sums = jnp.sum(wide(d_packed), axis=0)
    late = jnp.stack(
        [
            back_one[1],
            back_one[2],
            place_heads(head_sums[:width]),
            place_heads(head_sums[2 * width :]),
        ]
    )
    late = sum_all(late)
    rows = early[: 9 * model_width].reshape(9, model_width)
    gain_grads = jnp.stack([late[0], rows[0], rows[1]])
    shift_grads = jnp.stack([late[1], rows[2], rows[3]])
    attend_b_grad = jnp.stack([late[2], late[3], rows[4]])
    return (
        layer_output[None],
        input_gradient[None],
        encoder_gradient[None],
        gain_grads,
        shift_grads,
        attend_w_sum,
        attend_o_sum[0],
        attend_b_grad,
        cross_squares[0].T,
        cross_kv_sum,
        cross_squares[1],
        rows[5:8],
        expand_sum,
        early[9 * model_width :],
        shrink_sum,
        rows[8],
    )


def solution(mesh):
    pieces, sequence = mesh.devices.shape
    planes = Mesh(mesh.devices.reshape(pieces, sequence // 2, 2), ("dp", "z", "core"))
    seq = ("z", "core")
    in_specs = (
        P("dp", seq, None),
        P("dp", seq, None),
        P("dp", None),
        P("dp", None),
        P(),
        P(),
        P("dp", seq),
        P(seq, "dp"),
        P(),
        P("dp", seq),
        P("dp", seq),
        P(seq, "dp"),
        P(),
        P("dp", seq),
        P(),
        P(seq, "dp"),
        P(),
        P("dp", seq, None),
    )
    out_specs = (
        P("dp", seq, None),
        P("dp", seq, None),
        P("dp", seq, None),
        P(),
        P(),
        P("dp", seq),
        P(seq, "dp"),
        P(),
        P("dp", seq),
        P("dp", seq),
        P(seq, "dp"),
        P(),
        P("dp", seq),
        P(),
        P(seq, "dp"),
        P(),
    )
    return jax.shard_map(
        shards, mesh=planes, in_specs=in_specs, out_specs=out_specs, check_vma=False
    )
```

```python
import functools
import math

import jax
import jax.numpy as jnp
from jax import lax
from jax.experimental import pallas as pl
from jax.experimental.pallas import tpu as pltpu
from jax.sharding import Mesh
from jax.sharding import PartitionSpec as P

HEADS = 16

epsilon = 1e-05
masked_score = -1e30
head_width = 64


def head_columns(transposed, heads):
    if heads == 1:
        return transposed
    feature = lax.broadcasted_iota(jnp.int32, transposed.shape, 0) // head_width
    zero = jnp.zeros_like(transposed)
    return jnp.concatenate([jnp.where(feature == h, transposed, zero) for h in range(heads)], axis=1)


def head_rows(block, heads):
    if heads == 1:
        return block
    feature = lax.broadcasted_iota(jnp.int32, block.shape, 1) // head_width
    zero = jnp.zeros_like(block)
    return jnp.concatenate([jnp.where(feature == h, block, zero) for h in range(heads)], axis=0)


def flip(block):
    return jnp.transpose(block.astype(jnp.float32), (1, 0)).astype(block.dtype)


def repeat_heads(row, heads):
    return row if heads == 1 else jnp.concatenate([row] * heads, axis=1)


def project(scalars, mine_ref, theirs_ref, weight_ref, bias_ref, out_refs, width):
    weight = weight_ref[...]
    bias = bias_ref[...]
    for j, source in enumerate((mine_ref, theirs_ref)):
        for m in range(source.shape[0]):
            rows = bias + lax.dot_general(
                source[m], weight, (((1,), (1,)), ((), ())), preferred_element_type=jnp.float32
            )
            rows = rows.astype(jnp.bfloat16)
            for i, out_ref in enumerate(out_refs):
                out_ref[j, m] = rows[:, i * width : (i + 1) * width]


def natural_blocks(scalars, shape, planes):
    cores, pieces, rows = shape[:3]
    part = rows // planes
    for plane in range(planes):
        for core in range(cores):
            slots = [
                ((core ^ scalars[0], piece ^ scalars[1]), plane * part) for piece in range(pieces)
            ]
            if planes == 1:
                for piece in range(pieces):
                    yield (piece * cores + core) * rows, rows, slots[piece : piece + 1]
            else:
                yield (plane * cores + core) * pieces * part, part, slots


def take_rows(ref, part, slots):
    blocks = [ref[slot[0], slot[1], first : first + part] for slot, first in slots]
    return blocks[0] if len(blocks) == 1 else jnp.concatenate(blocks, axis=0)


def query_rows_of(ref, flip_by=0):
    return jnp.concatenate([ref[0, piece ^ flip_by, 0] for piece in range(ref.shape[1])], axis=0)


def put_query_rows(ref, block, flip_by=0):
    part = ref.shape[3]
    for piece in range(ref.shape[1]):
        ref[0, piece ^ flip_by, 0] = block[piece * part : (piece + 1) * part]


def attend_rows(scalars, query, first_ref, last_ref, keys, flipped, heads, key_block):
    step = pl.program_id(0)
    steps = pl.num_programs(0)
    rows = query.shape[0]
    query = query * jnp.asarray(1.0 / math.sqrt(head_width), jnp.bfloat16)
    columns = head_columns(flip(query), heads)
    first = repeat_heads(first_ref[0], heads)
    last = repeat_heads(last_ref[0], heads)

    def one(block, carry):
        peak, total, sums = carry
        start = pl.multiple_of(block * key_block, key_block)
        scores = jnp.dot(keys[pl.ds(start, key_block), :], columns, preferred_element_type=jnp.float32)
        place = start + lax.broadcasted_iota(jnp.int32, scores.shape, 0)
        scores = jnp.where((place >= first) & (place <= last), scores, masked_score)
        newer = jnp.maximum(peak, jnp.max(scores, axis=0, keepdims=True))
        shrink = jnp.exp(peak - newer)
        exponent = jnp.exp(scores - newer)
        total = total * shrink + jnp.sum(exponent, axis=0, keepdims=True)
        low_part = exponent.astype(jnp.bfloat16)
        turned = flipped[block]
        fresh = []
        for h in range(heads):
            part = jnp.dot(
                turned[h * head_width : (h + 1) * head_width],
                low_part[:, h * rows : (h + 1) * rows],
                preferred_element_type=jnp.float32,
            )
            fresh.append(sums[h] * shrink[:, h * rows : (h + 1) * rows] + part)
        return (newer, total, tuple(fresh))

    empty = (
        jnp.full((1, heads * rows), masked_score, jnp.float32),
        jnp.zeros((1, heads * rows), jnp.float32),
        tuple(jnp.zeros((head_width, rows), jnp.float32) for _ in range(heads)),
    )
    peak, total, sums = lax.fori_loop(scalars[2 + step], scalars[2 + steps + step] + 1, one, empty)
    context = jnp.concatenate(
        [sums[h] / total[:, h * rows : (h + 1) * rows] for h in range(heads)], axis=0
    )
    return context, peak + jnp.log(total)


def prepare(scalars, k_ref, v_ref, keys, flipped, key_block, planes):
    for start, part, slots in natural_blocks(scalars, k_ref.shape, planes):
        rows = part * len(slots)
        keys[start : start + rows, :] = take_rows(k_ref, part, slots)
        offset = start % key_block
        flipped[start // key_block, :, offset : offset + rows] = flip(take_rows(v_ref, part, slots))


def finish_forward(context, lse, ctx_ref, keep_ref, lse_ref):
    keep_ref[0] = context
    lse_ref[0] = lse
    put_query_rows(ctx_ref, jnp.transpose(context, (1, 0)).astype(jnp.bfloat16))


def self_forward_kernel(
    scalars, mine_ref, theirs_ref, weight_ref, bias_ref, first_ref, last_ref,
    q_ref, k_ref, v_ref, ctx_ref, keep_ref, lse_ref, keys, flipped,
    *, heads, key_block, planes,
):
    step = pl.program_id(0)
    cores, pieces, rows = q_ref.shape[:3]
    part = rows // planes

    @pl.when(step == 0)
    def _():
        outs = (q_ref, k_ref, v_ref)
        project(scalars, mine_ref, theirs_ref, weight_ref, bias_ref, outs, heads * head_width)
        prepare(scalars, k_ref, v_ref, keys, flipped, key_block, planes)

    core = lax.rem(step, cores) ^ scalars[0]
    here = pl.ds(pl.multiple_of(lax.div(step, cores) * part, part), part)
    query = jnp.concatenate(
        [q_ref[core, piece ^ scalars[1], here, :] for piece in range(pieces)], axis=0
    )
    context, lse = attend_rows(
        scalars, query, first_ref, last_ref, keys, flipped, heads, key_block
    )
    finish_forward(context, lse, ctx_ref, keep_ref, lse_ref)


def cross_forward_kernel(
    scalars, q_ref, mine_ref, theirs_ref, weight_ref, bias_ref, first_ref, last_ref,
    k_ref, v_ref, ctx_ref, keep_ref, lse_ref, keys, flipped,
    *, heads, key_block,
):
    @pl.when(pl.program_id(0) == 0)
    def _():
        outs = (k_ref, v_ref)
        project(scalars, mine_ref, theirs_ref, weight_ref, bias_ref, outs, heads * head_width)
        prepare(scalars, k_ref, v_ref, keys, flipped, key_block, 1)

    context, lse = attend_rows(
        scalars, query_rows_of(q_ref), first_ref, last_ref, keys, flipped, heads, key_block
    )
    finish_forward(context, lse, ctx_ref, keep_ref, lse_ref)


def backward_kernel(
    scalars, q_ref, k_ref, v_ref, dc_ref, keep_ref, lse_ref, first_ref, last_ref,
    *rest, heads, key_block, planes, near,
):
    if near:
        dq_ref, dqt_ref, dkv_ref, dkvt_ref, keys, values, flipped, dkeys, dvalues = rest
    else:
        dq_ref, dkv_ref, dkvt_ref, keys, values, flipped, dkeys, dvalues = rest
    step = pl.program_id(0)
    steps = pl.num_programs(0)
    width = heads * head_width
    scaling = 1.0 / math.sqrt(head_width)

    @pl.when(step == 0)
    def _():
        prepare(scalars, k_ref, k_ref, keys, flipped, key_block, planes)
        for start, part, slots in natural_blocks(scalars, v_ref.shape, planes):
            values[start : start + part * len(slots), :] = take_rows(v_ref, part, slots)
        dkeys[...] = jnp.zeros_like(dkeys)
        dvalues[...] = jnp.zeros_like(dvalues)

    flip_by = scalars[1] if near else 0
    query = query_rows_of(q_ref, flip_by) * jnp.asarray(scaling, jnp.bfloat16)
    rows = query.shape[0]
    grad = query_rows_of(dc_ref)
    turned_grad = flip(grad)
    query_columns = head_columns(flip(query), heads)
    grad_columns = head_columns(turned_grad, heads)
    query_rows = head_rows(query, heads)
    grad_rows = head_rows(grad, heads)
    dots_kept = turned_grad.astype(jnp.float32) * keep_ref[0]
    center = jnp.concatenate(
        [
            jnp.sum(dots_kept[h * head_width : (h + 1) * head_width], axis=0, keepdims=True)
            for h in range(heads)
        ],
        axis=1,
    )
    first = repeat_heads(first_ref[0], heads)
    last = repeat_heads(last_ref[0], heads)
    lse = lse_ref[0]

    def one(block, sums):
        start = pl.multiple_of(block * key_block, key_block)
        here = pl.ds(start, key_block)
        scores = jnp.dot(keys[here, :], query_columns, preferred_element_type=jnp.float32)
        place = start + lax.broadcasted_iota(jnp.int32, scores.shape, 0)
        scores = jnp.where((place >= first) & (place <= last), scores, masked_score)
        weights = jnp.exp(scores - lse)
        dots = jnp.dot(values[here, :], grad_columns, preferred_element_type=jnp.float32)
        dscore = (weights * (dots - center)).astype(jnp.bfloat16)
        dvalues[here, :] += jnp.dot(
            weights.astype(jnp.bfloat16), grad_rows, preferred_element_type=jnp.float32
        )
        dkeys[here, :] += jnp.dot(dscore, query_rows, preferred_element_type=jnp.float32)
        turned = flipped[block]
        return tuple(
            sums[h]
            + jnp.dot(
                turned[h * head_width : (h + 1) * head_width],
                dscore[:, h * rows : (h + 1) * rows],
                preferred_element_type=jnp.float32,
            )
            for h in range(heads)
        )

    empty = tuple(jnp.zeros((head_width, rows), jnp.float32) for _ in range(heads))
    sums = lax.fori_loop(scalars[2 + step], scalars[2 + steps + step] + 1, one, empty)
    dquery = jnp.concatenate(sums, axis=0) * scaling
    dquery = jnp.transpose(dquery, (1, 0)).astype(jnp.bfloat16)
    if near:
        core = lax.rem(step, dq_ref.shape[0]) ^ scalars[0]
        plane = lax.div(step, dq_ref.shape[0])
        part = dq_ref.shape[3]
        for piece in range(dq_ref.shape[1]):
            dq_ref[core, piece ^ flip_by, plane] = dquery[piece * part : (piece + 1) * part]
    else:
        put_query_rows(dq_ref, dquery)

    @pl.when(step == steps - 1)
    def _():
        cores, pieces, key_rows = k_ref.shape[:3]
        for start, part, slots in natural_blocks(scalars, k_ref.shape, planes):
            for i, (slot, first) in enumerate(slots):
                here = slice(start + i * part, start + (i + 1) * part)
                for column, total in ((0, dkeys), (width, dvalues)):
                    dkv_ref[slot[0], slot[1], first : first + part, column : column + width] = (
                        total[here, :].astype(jnp.bfloat16)
                    )
        for j in range(cores):
            for m in range(pieces):
                place = (j * pieces + m) * key_rows
                dkvt_ref[:, place : place + key_rows] = flip(dkv_ref[j, m])
                if near:
                    block = dq_ref[j, m].reshape(key_rows, width)
                    dqt_ref[:, place : place + key_rows] = flip(block)


def whole_spec(shape, index=None):
    index = (0,) * len(shape) if index is None else index
    return pl.BlockSpec(shape, lambda step, scalars: index)


def step_spec(shape):
    return pl.BlockSpec((1,) + shape[1:], lambda step, scalars: (step, 0, 0))


def member_spec(shape, near):
    cores, pieces = shape[:2]

    def place(step, scalars):
        core = lax.rem(step, cores)
        return (core ^ scalars[0] if near else core, 0, lax.div(step, cores), 0, 0)

    return pl.BlockSpec((1, pieces, 1) + shape[3:], place)


def forward_outputs(shape):
    cores, pieces, planes, rows, width = shape
    steps = cores * planes
    heads = width // head_width
    shapes = [
        jax.ShapeDtypeStruct(shape, jnp.bfloat16),
        jax.ShapeDtypeStruct((steps, width, pieces * rows), jnp.float32),
        jax.ShapeDtypeStruct((steps, 1, heads * pieces * rows), jnp.float32),
    ]
    specs = [member_spec(shape, False), step_spec(shapes[1].shape), step_spec(shapes[2].shape)]
    return shapes, specs


def cost(microseconds):
    return pl.CostEstimate(
        flops=int(microseconds * 1.1e9), bytes_accessed=1 << 20, transcendentals=0
    )


def params():
    return pltpu.CompilerParams(vmem_limit_bytes=36 * 2**20)


def self_forward(scalars, mine, theirs, planes, weight, bias, first, last):
    pieces, rows, model_width = mine.shape
    width = weight.shape[0] // 3
    shape = (2, pieces, rows, width)
    steps = 2 * planes
    key_count = 2 * pieces * rows
    key_block = min(256, key_count)
    shapes, specs = forward_outputs((2, pieces, planes, rows // planes, width))
    full = jax.ShapeDtypeStruct(shape, jnp.bfloat16)
    return pl.pallas_call(
        functools.partial(
            self_forward_kernel, heads=width // head_width, key_block=key_block, planes=planes
        ),
        grid_spec=pltpu.PrefetchScalarGridSpec(
            num_scalar_prefetch=1,
            grid=(steps,),
            in_specs=[
                whole_spec(mine.shape),
                whole_spec(theirs.shape),
                whole_spec(weight.shape),
                whole_spec(bias.shape),
                step_spec(first.shape),
                step_spec(last.shape),
            ],
            out_specs=[whole_spec(shape)] * 3 + specs,
            scratch_shapes=[
                pltpu.VMEM((key_count, width), jnp.bfloat16),
                pltpu.VMEM((key_count // key_block, width, key_block), jnp.bfloat16),
            ],
        ),
        out_shape=[full] * 3 + shapes,
        compiler_params=params(),
        cost_estimate=cost(16),
    )(scalars, mine, theirs, weight, bias, first, last)


def cross_forward(scalars, queries, mine, theirs, weight, bias, first, last):
    cores, pieces, planes, rows, width = queries.shape
    state_rows = mine.shape[1]
    steps = cores * planes
    key_count = cores * pieces * state_rows
    key_block = min(256, key_count)
    shapes, specs = forward_outputs(queries.shape)
    key_shape = (cores, pieces, state_rows, width)
    full = jax.ShapeDtypeStruct(key_shape, jnp.bfloat16)
    return pl.pallas_call(
        functools.partial(cross_forward_kernel, heads=width // head_width, key_block=key_block),
        grid_spec=pltpu.PrefetchScalarGridSpec(
            num_scalar_prefetch=1,
            grid=(steps,),
            in_specs=[
                member_spec(queries.shape, False),
                whole_spec(mine.shape),
                whole_spec(theirs.shape),
                whole_spec(weight.shape),
                whole_spec(bias.shape),
                step_spec(first.shape),
                step_spec(last.shape),
            ],
            out_specs=[whole_spec(key_shape)] * 2 + specs,
            scratch_shapes=[
                pltpu.VMEM((key_count, width), jnp.bfloat16),
                pltpu.VMEM((key_count // key_block, width, key_block), jnp.bfloat16),
            ],
        ),
        out_shape=[full] * 2 + shapes,
        compiler_params=params(),
        cost_estimate=cost(11),
    )(scalars, queries, mine, theirs, weight, bias, first, last)


def attend_back(scalars, queries, key_rows, values, grad, kept, lse, first, last, near):
    cores, pieces, planes, rows, width = queries.shape
    steps = cores * planes
    key_shape = key_rows.shape
    key_count = cores * pieces * key_shape[2]
    key_block = min(256, key_count)
    dq_shape = jax.ShapeDtypeStruct(queries.shape, jnp.bfloat16)
    if near:
        dq_shapes = [dq_shape, jax.ShapeDtypeStruct((width, key_count), jnp.bfloat16)]
        dq_specs = [whole_spec(queries.shape), whole_spec((width, key_count))]
    else:
        dq_shapes, dq_specs = [dq_shape], [member_spec(queries.shape, False)]
    return pl.pallas_call(
        functools.partial(
            backward_kernel,
            heads=width // head_width,
            key_block=key_block,
            planes=planes if near else 1,
            near=near,
        ),
        grid_spec=pltpu.PrefetchScalarGridSpec(
            num_scalar_prefetch=1,
            grid=(steps,),
            in_specs=[
                member_spec(queries.shape, near),
                whole_spec(key_shape),
                whole_spec(key_shape),
                member_spec(grad.shape, False),
                step_spec(kept.shape),
                step_spec(lse.shape),
                step_spec(first.shape),
                step_spec(last.shape),
            ],
            out_specs=dq_specs
            + [whole_spec(key_shape[:3] + (2 * width,)), whole_spec((2 * width, key_count))],
            scratch_shapes=[
                pltpu.VMEM((key_count, width), jnp.bfloat16),
                pltpu.VMEM((key_count, width), jnp.bfloat16),
                pltpu.VMEM((key_count // key_block, width, key_block), jnp.bfloat16),
                pltpu.VMEM((key_count, width), jnp.float32),
                pltpu.VMEM((key_count, width), jnp.float32),
            ],
        ),
        out_shape=dq_shapes
        + [
            jax.ShapeDtypeStruct(key_shape[:3] + (2 * width,), jnp.bfloat16),
            jax.ShapeDtypeStruct((2 * width, key_count), jnp.bfloat16),
        ],
        compiler_params=params(),
        cost_estimate=cost(12),
    )(scalars, queries, key_rows, values, grad, kept, lse, first, last)


def single(kernel, out_shape, in_specs, scratch, *args):
    return pl.pallas_call(
        kernel,
        grid_spec=pltpu.PrefetchScalarGridSpec(
            num_scalar_prefetch=1,
            grid=(1,),
            in_specs=[
                whole_spec(value.shape) if spec is None else spec
                for spec, value in zip(in_specs, args[1:])
            ],
            out_specs=[whole_spec(value.shape) for value in out_shape],
            scratch_shapes=scratch,
        ),
        out_shape=out_shape,
        compiler_params=params(),
        cost_estimate=cost(4),
    )(*args)


def kind_spec(array, kind):
    shape = (array.shape[0], array.shape[1], 1) + array.shape[3:]
    return whole_spec(shape, (0, 0, kind, 0, 0))


def square_block(ref, m):
    block = ref[m, :, 0]
    return block.reshape(block.shape[0] * block.shape[1], block.shape[2])


def heads_of(ref, core):
    return jnp.concatenate([ref[core, piece] for piece in range(ref.shape[1])], axis=1)


def near_span(scalars, m, size):
    return pl.ds(pl.multiple_of((scalars[1] ^ m) * size, size), size)


def heads_to_model(scalars, heads_ref, mine_ref, theirs_ref, sums):
    mine, theirs = heads_of(heads_ref, scalars[0]), heads_of(heads_ref, 1 ^ scalars[0])
    size = mine_ref.shape[4]
    for m in range(mine_ref.shape[0]):
        sums[:, near_span(scalars, m, size)] = jnp.dot(
            mine, square_block(mine_ref, m), preferred_element_type=jnp.float32
        ) + jnp.dot(theirs, square_block(theirs_ref, m), preferred_element_type=jnp.float32)


def model_to_heads(scalars, rows_ref, mine_ref, theirs_ref, heads_ref, bias_ref=None):
    size = mine_ref.shape[4]
    pieces, width = heads_ref.shape[1], heads_ref.shape[3]
    for j, weight_ref in enumerate((mine_ref, theirs_ref)):
        total = 0.0
        for m in range(weight_ref.shape[0]):
            total = total + lax.dot_general(
                rows_ref[:, near_span(scalars, m, size)],
                square_block(weight_ref, m),
                (((1,), (1,)), ((), ())),
                preferred_element_type=jnp.float32,
            )
        core = scalars[0] ^ j
        for piece in range(pieces):
            block = total[:, piece * width : (piece + 1) * width]
            if bias_ref is not None:
                block = block + bias_ref[core, piece]
            heads_ref[core, piece] = block.astype(jnp.bfloat16)


def normal_parts(values):
    center = values - jnp.mean(values, axis=-1, keepdims=True)
    spread = jnp.mean(center * center, axis=-1, keepdims=True)
    scale = lax.rsqrt(spread + epsilon)
    return center * scale, scale


def norm_back(values, gain, dn):
    normal, scale = normal_parts(values)
    e = dn * gain
    dv = scale * (
        e
        - jnp.mean(e, axis=-1, keepdims=True)
        - normal * jnp.mean(e * normal, axis=-1, keepdims=True)
    )
    return (
        dv,
        jnp.sum(dn * normal, axis=0, keepdims=True),
        jnp.sum(dn, axis=0, keepdims=True),
    )


def middle_kernel(
    scalars, heads_ref, omine_ref, otheirs_ref, resid_ref, rows_ref, qmine_ref, qtheirs_ref,
    qbias_ref, sum_ref, norm_ref, q_ref,
):
    heads_to_model(scalars, heads_ref, omine_ref, otheirs_ref, sum_ref)
    total = sum_ref[...] + resid_ref[...].astype(jnp.float32) + rows_ref[0:1]
    sum_ref[...] = total
    normal, _ = normal_parts(total)
    norm_ref[...] = (normal * rows_ref[1:2] + rows_ref[2:3]).astype(jnp.bfloat16)
    model_to_heads(scalars, norm_ref, qmine_ref, qtheirs_ref, q_ref, qbias_ref)


def later_kernel(
    scalars, heads_ref, omine_ref, otheirs_ref, resid_ref, rows_ref, sum_ref, norm_ref
):
    heads_to_model(scalars, heads_ref, omine_ref, otheirs_ref, sum_ref)
    total = sum_ref[...] + resid_ref[...] + rows_ref[0:1]
    sum_ref[...] = total
    normal, _ = normal_parts(total)
    norm_ref[...] = (normal * rows_ref[1:2] + rows_ref[2:3]).astype(jnp.bfloat16)


def finish_back(scalars, values_ref, rows_ref, dn, upper, mine_ref, theirs_ref, d_ref, low_ref, heads_ref, sums_ref):
    dv, dg, db = norm_back(values_ref[...], rows_ref[0:1], dn)
    total = upper + dv
    d_ref[...] = total
    low_total = total.astype(jnp.bfloat16)
    low_ref[...] = low_total
    sums_ref[0:1] = dg
    sums_ref[1:2] = db
    sums_ref[2:3] = jnp.sum(low_total.astype(jnp.float32), axis=0, keepdims=True)
    model_to_heads(scalars, low_ref, mine_ref, theirs_ref, heads_ref)


def later_back_kernel(scalars, *refs):
    parts, (up_ref, values_ref, rows_ref, mine_ref, theirs_ref) = refs[:-9], refs[-9:-4]
    dn = parts[0][...].reshape(up_ref.shape)
    for part in parts[1:]:
        dn = dn + part[...].reshape(up_ref.shape).astype(jnp.float32)
    upper = up_ref[...].astype(jnp.float32)
    finish_back(scalars, values_ref, rows_ref, dn, upper, mine_ref, theirs_ref, *refs[-4:])


def middle_back_kernel(
    scalars, heads_ref, qmine_ref, qtheirs_ref, upper_ref, values_ref, rows_ref, mine_ref,
    theirs_ref, d_ref, low_ref, dheads_ref, sums_ref, work,
):
    heads_to_model(scalars, heads_ref, qmine_ref, qtheirs_ref, work)
    finish_back(
        scalars, values_ref, rows_ref, work[...], upper_ref[...], mine_ref, theirs_ref,
        d_ref, low_ref, dheads_ref, sums_ref,
    )


def input_back_kernel(scalars, *refs):
    parts, (upper_ref, values_ref, rows_ref, out_ref, sums_ref) = refs[:-5], refs[-5:]
    dn = parts[0][...].reshape(upper_ref.shape)
    for part in parts[1:]:
        dn = dn + part[...].reshape(upper_ref.shape).astype(jnp.float32)
    dv, dg, db = norm_back(values_ref[...].astype(jnp.float32), rows_ref[0:1], dn)
    out_ref[...] = (upper_ref[...] + dv).astype(jnp.bfloat16)
    sums_ref[0:1] = dg
    sums_ref[1:2] = db


def square_grad_kernel(scalars, *refs):
    kinds = (len(refs) - 2) // 2
    mine_ref, theirs_ref = refs[-2:]
    size = mine_ref.shape[4]
    for kind in range(kinds):
        heads_ref, rows_ref = refs[2 * kind], refs[2 * kind + 1]
        for j, out_ref in enumerate((mine_ref, theirs_ref)):
            for piece in range(heads_ref.shape[1]):
                turned = flip(heads_ref[scalars[0] ^ j, piece])
                for m in range(out_ref.shape[0]):
                    out_ref[m, piece, kind] = jnp.dot(
                        turned,
                        rows_ref[:, near_span(scalars, m, size)],
                        preferred_element_type=jnp.float32,
                    ).astype(out_ref.dtype)


def gelu_parts(u):
    root = math.sqrt(2.0 / math.pi)
    square = u * u
    bent = jnp.tanh(root * (u + 0.044715 * (square * u)))
    half = 0.5 * (1.0 + bent)
    slope = half + 0.5 * u * (1.0 - bent * bent) * (root * (1.0 + 3.0 * 0.044715 * square))
    return u * half, slope


def units_kernel(
    scalars, mine_ref, theirs_ref, upmine_ref, uptheirs_ref, expand_ref, shrink_ref, bias_ref,
    active_ref, dhidden_ref, dmine_ref, dtheirs_ref, half_count,
):
    step = pl.program_id(0)
    expand, shrink = expand_ref[...], shrink_ref[...]
    against_last = (((1,), (1,)), ((), ()))

    def one(rows, up):
        hidden = lax.dot_general(rows, expand, against_last, preferred_element_type=jnp.float32)
        dactive = lax.dot_general(up, shrink, against_last, preferred_element_type=jnp.float32)
        active, slope = gelu_parts(hidden + bias_ref[...])
        dhidden = (dactive * slope).astype(jnp.bfloat16)
        active_ref[0, 0] = active.astype(jnp.bfloat16)
        dhidden_ref[0, 0] = dhidden
        return jnp.dot(dhidden, expand, preferred_element_type=jnp.float32)

    @pl.when(step < half_count)
    def _():
        dtheirs_ref[0] = one(theirs_ref[0], uptheirs_ref[0]).astype(jnp.bfloat16)

    @pl.when(step >= half_count)
    def _():
        dmine_ref[0] = one(mine_ref[0], upmine_ref[0])


def units_group(scalars, mine, theirs, ups, start, expand_t, shrink_w, bias):
    count, rows, model_width = mine.shape
    units = expand_t.shape[0]

    def piece_spec(own, offset=0):
        if own:
            place = lambda step, scalars: (jnp.maximum(step - count, 0) + offset, 0, 0)
        else:
            place = lambda step, scalars: (jnp.minimum(step, count - 1) + offset, 0, 0)
        return pl.BlockSpec((1, rows, model_width), place)

    def table_place(step, scalars):
        return (1 - lax.div(step, count), lax.rem(step, count), 0, 0)

    table = jax.ShapeDtypeStruct((2, count, rows, units), jnp.bfloat16)
    table_spec = pl.BlockSpec((1, 1, rows, units), table_place)
    return pl.pallas_call(
        functools.partial(units_kernel, half_count=count),
        grid_spec=pltpu.PrefetchScalarGridSpec(
            num_scalar_prefetch=1,
            grid=(2 * count,),
            in_specs=[
                piece_spec(True),
                piece_spec(False),
                piece_spec(True, start),
                piece_spec(False, start),
                whole_spec(expand_t.shape),
                whole_spec(shrink_w.shape),
                whole_spec(bias.shape),
            ],
            out_specs=[table_spec, table_spec, piece_spec(True), piece_spec(False)],
        ),
        out_shape=[
            table,
            table,
            jax.ShapeDtypeStruct(mine.shape, jnp.float32),
            jax.ShapeDtypeStruct(mine.shape, jnp.bfloat16),
        ],
        compiler_params=params(),
        cost_estimate=cost(6.5 * count),
    )(scalars, mine, theirs, *ups, expand_t, shrink_w, bias)


def unit_gradients_kernel(scalars, *refs, counts):
    dhidden_refs, active_refs = refs[0:2], refs[2:4]
    row_refs, up_refs = (refs[4:6], refs[6:8]), refs[8:10]
    out_ref, expand_sum, shrink_sum = refs[10:]
    step = pl.program_id(0)
    width = expand_sum.shape[1]

    @pl.when(step == 0)
    def _():
        expand_sum[...] = jnp.zeros_like(expand_sum)
        shrink_sum[...] = jnp.zeros_like(shrink_sum)

    def add(group, core):
        for table_ref, rows_ref, total in (
            (dhidden_refs[group], row_refs[group][core], expand_sum),
            (active_refs[group], up_refs[core], shrink_sum),
        ):
            total[...] += lax.dot_general(
                table_ref[0, 0],
                rows_ref[0],
                (((0,), (0,)), ((), ())),
                preferred_element_type=jnp.float32,
            )

    first = 0
    for group, count in enumerate(counts):
        for core in range(2):
            @pl.when((step >= first) & (step < first + count))
            def _(group=group, core=core):
                add(group, core)

            first += count

    @pl.when(step == pl.num_programs(0) - 1)
    def _():
        out_ref[:, :width] = expand_sum[...].astype(jnp.bfloat16)
        out_ref[:, width:] = shrink_sum[...].astype(jnp.bfloat16)


def unit_gradients(scalars, dhiddens, actives, rows, ups):
    counts = [table.shape[1] for table in actives]
    _, _, tokens, units = actives[0].shape
    model_width = ups[0].shape[2]
    starts = [2 * sum(counts[:i]) for i in range(len(counts))]

    def table_spec(group):
        count, start = counts[group], starts[group]

        def place(step, scalars):
            here = jnp.clip(step - start, 0, 2 * count - 1)
            return (lax.div(here, count), lax.rem(here, count), 0, 0)

        return pl.BlockSpec((1, 1, tokens, units), place)

    def row_place(group, core):
        count, start = counts[group], starts[group] + core * counts[group]
        return pl.BlockSpec(
            (1, tokens, model_width),
            lambda step, scalars: (jnp.clip(step - start, 0, count - 1), 0, 0),
        )

    def up_place(core):
        def place(step, scalars):
            here = 0
            for i in range(len(counts)):
                inside = jnp.clip(step - starts[i] - core * counts[i], 0, counts[i] - 1)
                begun = (step >= starts[i] + core * counts[i]).astype(jnp.int32)
                here = jnp.where(begun == 1, sum(counts[:i]) + inside, here)
            return (here, 0, 0)

        return pl.BlockSpec((1, tokens, model_width), place)

    return pl.pallas_call(
        functools.partial(unit_gradients_kernel, counts=counts),
        grid_spec=pltpu.PrefetchScalarGridSpec(
            num_scalar_prefetch=1,
            grid=(2 * sum(counts),),
            in_specs=[table_spec(0), table_spec(1), table_spec(0), table_spec(1)]
            + [row_place(0, 0), row_place(0, 1), row_place(1, 0), row_place(1, 1)]
            + [up_place(0), up_place(1)],
            out_specs=whole_spec((units, 2 * model_width)),
            scratch_shapes=[pltpu.VMEM((units, model_width), jnp.float32)] * 2,
        ),
        out_shape=jax.ShapeDtypeStruct((units, 2 * model_width), jnp.bfloat16),
        compiler_params=params(),
        cost_estimate=cost(12),
    )(scalars, *dhiddens, *actives, *rows[0], *rows[1], *ups)


def layer_norm(values, gain_row, shift_row):
    center = values - jnp.mean(values, axis=-1, keepdims=True)
    spread = jnp.mean(center * center, axis=-1, keepdims=True)
    return center * lax.rsqrt(spread + epsilon) * gain_row + shift_row


def inner_rows(former, latter):
    return lax.dot_general(
        former, latter, (((0,), (0,)), ((), ())), preferred_element_type=jnp.float32
    )


def against(former, latter):
    return lax.dot_general(
        former, latter, (((1,), (1,)), ((), ())), preferred_element_type=jnp.float32
    )


def product(former, latter):
    return jnp.dot(former, latter, preferred_element_type=jnp.float32)


def low(values):
    return values.astype(jnp.bfloat16)


def wide(values):
    return values.astype(jnp.float32)


def other(values, axis, shift):
    count = lax.axis_size(axis)
    return lax.ppermute(values, axis, [(i, i ^ shift) for i in range(count)])


def trade(values, axis, split, concat):
    return lax.all_to_all(values, axis, split_axis=split, concat_axis=concat, tiled=True)


def after(values, *earlier):
    return lax.optimization_barrier((values, earlier))[0]


PLANE = ("core", "dp")


def chips_gather(block, axis="dp"):
    return [block] + [other(block, axis, m) for m in range(1, lax.axis_size(axis))]


def plane_gather(block):
    mine = jnp.stack(chips_gather(block))
    return mine, other(mine, "core", 1)


def plane_reduce(mine, theirs):
    sums = mine + wide(other(low(theirs), "core", 1))
    total = sums[0]
    for m in range(1, sums.shape[0]):
        total = total + wide(other(low(sums[m]), "dp", m))
    return total


def swap_planes(values, hop=0):
    pieces, planes, cores = (lax.axis_size(axis) for axis in ("dp", "z", "core"))
    pairs = [
        (((d ^ hop) * planes + z) * cores + c, (z * planes + d) * cores + c)
        for d in range(pieces)
        for z in range(planes)
        for c in range(cores)
    ]
    return lax.ppermute(values, ("dp", "z", "core"), pairs)


def swap_in(rows):
    return trade(trade(rows, "dp", 0, 0), "z", 0, 0)


def put_blocks(blocks, axis, dimension):
    size = blocks[0].shape[dimension]
    shape = list(blocks[0].shape)
    shape[dimension] = size * len(blocks)
    whole = jnp.zeros(shape, blocks[0].dtype)
    for m, block in enumerate(blocks):
        start = [0] * len(shape)
        start[dimension] = (lax.axis_index(axis) ^ m) * size
        whole = lax.dynamic_update_slice(whole, block, start)
    return whole


def sum_all(values):
    for axis in ("core", "dp", "z"):
        shift = 1
        while shift < lax.axis_size(axis):
            values = values + other(values, axis, shift)
            shift *= 2
    return values


def document_edges(ids, memory_ids, steps):
    documents = jnp.arange(4, dtype=jnp.int32)
    starts = jnp.sum((memory_ids[None] < documents[:, None]).astype(jnp.int32), axis=1)
    ends = jnp.sum((memory_ids[None] <= documents[:, None]).astype(jnp.int32), axis=1) - 1
    match = ids[None] == documents[:, None]
    first = jnp.sum(jnp.where(match, starts[:, None], 0), axis=0)
    last = jnp.sum(jnp.where(match, ends[:, None], 0), axis=0)
    return (first.reshape(steps, 1, -1), last.reshape(steps, 1, -1))


def shards(
    inputs,
    encoder_states,
    segment_ids,
    encoder_ids,
    norm_gains,
    norm_shifts,
    attend_weights,
    attend_output,
    attend_biases,
    cross_query,
    cross_memory,
    cross_output,
    cross_biases,
    expand_weight,
    expand_bias,
    shrink_weight,
    shrink_bias,
    output_cotangent,
):
    pieces, planes, cores = lax.axis_size("dp"), lax.axis_size("z"), lax.axis_size("core")
    piece, plane, core = lax.axis_index("dp"), lax.axis_index("z"), lax.axis_index("core")
    members = pieces * cores
    member = core * pieces + piece
    row_count, model_width = inputs.shape[1:]
    memory_rows = encoder_states.shape[1]
    pack_rows, pack_memory = segment_ids.shape[1], encoder_ids.shape[1]
    heads = HEADS // members
    head_size = model_width // HEADS
    width = heads * head_size
    steps = planes * cores
    unit_count = expand_weight.shape[1]
    block_units = unit_count // pieces
    block_rows = model_width // pieces

    all_ids = swap_planes(jnp.concatenate([segment_ids[0], encoder_ids[0]]))
    pack_ids, memory_ids = all_ids[:pack_rows], all_ids[pack_rows:]
    raw = swap_in(inputs[0])

    def columns_of(weight, count):
        weight = weight.reshape(pieces, heads, count, head_size, block_rows)
        return weight.transpose(2, 1, 3, 0, 4).reshape(count * width, model_width)

    near_w = jnp.concatenate(
        [attend_weights.T, cross_memory.T, attend_output, cross_query.T, cross_output]
    )
    near_w = lax.all_gather(near_w, "z", axis=0, tiled=False)
    heads_w = near_w[:, : 5 * width].reshape(planes * 5 * width, block_rows)
    upstream = swap_in(after(output_cotangent[0], raw))
    heads_w = trade(after(heads_w, upstream), "dp", 0, 0).reshape(pieces, 5 * width, block_rows)
    squares = near_w[:, 5 * width :].reshape(planes, 3, width, block_rows)
    unit_w = jnp.stack([expand_weight.T, shrink_weight], axis=1)
    unit_parts = []
    for m in range(pieces):
        part = lax.dynamic_slice_in_dim(unit_w, (piece ^ m) * block_units, block_units, 0)
        unit_parts.append(part if m == 0 else other(part, "dp", m))
    unit_w = put_blocks(unit_parts, "dp", 2).reshape(block_units, 2 * model_width)
    states = swap_planes(after(encoder_states[0], raw))
    whole_units = lax.all_gather(after(unit_w, states), "z", axis=0, tiled=True)
    expand_t, shrink_w = whole_units[:, :model_width], whole_units[:, model_width:]
    attend_w = columns_of(heads_w[:, : 3 * width], 3)
    cross_kv = columns_of(heads_w[:, 3 * width :], 2)

    own = jnp.stack([core, piece]).astype(jnp.int32)
    key_block = min(256, pack_rows)
    self_first, _ = document_edges(pack_ids, pack_ids, steps)
    self_last = jnp.arange(pack_rows, dtype=jnp.int32).reshape(steps, 1, -1)
    self_scalars = jnp.concatenate(
        [own, self_first[:, 0, 0] // key_block, self_last[:, 0, -1] // key_block]
    )
    cross_first, cross_last = document_edges(pack_ids, memory_ids, steps)
    key_block = min(256, pack_memory)
    cross_scalars = jnp.concatenate(
        [own, cross_first[:, 0, 0] // key_block, cross_last[:, 0, -1] // key_block]
    )

    gain_rows, shift_rows = wide(norm_gains), wide(norm_shifts)
    bias_self, bias_cross = wide(attend_biases), wide(cross_biases)

    def of_heads(row):
        return lax.dynamic_slice_in_dim(row, (piece * cores + core) * width, width, 0)

    def place_heads(row):
        return lax.dynamic_update_slice(
            jnp.zeros((model_width,), jnp.float32), row, ((piece * cores + core) * width,)
        )

    zero_heads = jnp.zeros((width,), jnp.float32)
    packed_bias = jnp.concatenate([of_heads(bias_self[0]), zero_heads, of_heads(bias_self[1])])
    memory_bias = jnp.concatenate([zero_heads, of_heads(bias_cross[1])])
    query_bias = bias_cross[0].reshape(pieces, cores, 1, width).transpose(1, 0, 2, 3)
    token_shape = (cores, pieces, row_count, width)
    part_shape = (cores, pieces, planes, row_count // planes, width)
    flat_shape = (row_count, model_width)
    flat_float = jax.ShapeDtypeStruct(flat_shape, jnp.float32)
    flat_low = jax.ShapeDtypeStruct(flat_shape, jnp.bfloat16)
    head_low = jax.ShapeDtypeStruct(token_shape, jnp.bfloat16)
    three_rows = jax.ShapeDtypeStruct((3, model_width), jnp.float32)

    def exchange(values):
        return trade(values.reshape(pieces * cores * row_count, width), PLANE, 0, 0).reshape(
            token_shape
        )

    low_one = low(layer_norm(wide(raw), gain_rows[0], shift_rows[0]))
    mine = jnp.stack(chips_gather(after(low_one, unit_w)))
    squares = after(squares, heads_w, mine)
    ones = (mine, other(mine, "core", 1))
    square_parts = chips_gather(squares)
    query1, key1, value1, context1, kept1, lse1 = self_forward(
        self_scalars, *ones, planes, attend_w, packed_bias[None], self_first, self_last
    )
    context1, square_parts = after((context1, square_parts))
    squares = jnp.stack(square_parts)
    squares = (squares, other(squares, "core", 1))
    mixed1 = exchange(context1)
    all_states = jnp.stack(chips_gather(after(states, mixed1)))
    all_states = (all_states, other(all_states, "core", 1))
    middle, low_two, query2 = single(
        middle_kernel,
        [flat_float, flat_low, head_low],
        [None, kind_spec(squares[0], 0), kind_spec(squares[1], 0), None, None]
        + [kind_spec(squares[0], 1), kind_spec(squares[1], 1), None],
        [],
        own, mixed1, *squares, raw,
        jnp.stack([bias_self[2], gain_rows[1], shift_rows[1]]),
        *squares, query_bias,
    )

    query2 = exchange(query2)
    query2 = query2.reshape(part_shape)
    key2, value2, context2, kept2, lse2 = cross_forward(
        cross_scalars, query2, *all_states, cross_kv, memory_bias[None],
        cross_first, cross_last,
    )
    ups = chips_gather(after(upstream, query2))
    context2, ups = after((context2, ups))
    ups = jnp.stack(ups)
    all_ups = (ups, other(ups, "core", 1))
    context2 = after(context2, whole_units)
    mixed2 = exchange(context2)
    later, low_three = single(
        later_kernel,
        [flat_float, flat_low],
        [None, kind_spec(squares[0], 2), kind_spec(squares[1], 2), None, None],
        [],
        own, mixed2, *squares, middle,
        jnp.stack([bias_cross[2], gain_rows[2], shift_rows[2]]),
    )

    bias_units = wide(expand_bias).reshape(planes, cores, pieces, block_units)
    bias_units = lax.dynamic_slice(
        bias_units, (0, core, piece, 0), (planes, 1, 1, block_units)
    ).reshape(1, unit_count)
    groups = [list(range(pieces - 1)), [pieces - 1]]
    pieces3 = chips_gather(low_three)
    threes, actives, d_hiddens, parts3, leaving = [], [], [], [], []
    for group in groups:
        mine = jnp.stack([pieces3[m] for m in group])
        if d_hiddens:
            mine = after(mine, d_hiddens[-1])
        theirs = other(mine, "core", 1)
        active, d_hidden, d_mine, d_theirs = units_group(
            own, mine, theirs, all_ups, group[0], expand_t, shrink_w, bias_units
        )
        d_sum = d_mine + wide(other(d_theirs, "core", 1))
        for i, m in enumerate(group):
            leaving.append(d_sum[i] if m == 0 else low(d_sum[i]))
            parts3.append(leaving[-1] if m == 0 else other(leaving[-1], "dp", m))
        threes.append((mine, theirs))
        actives.append(active)
        d_hiddens.append(d_hidden)
    actives, d_hiddens = after((actives, d_hiddens), leaving)

    unit_grads = unit_gradients(own, d_hiddens, actives, threes, all_ups)
    unit_grads, parts3 = after((unit_grads, parts3))
    unit_grads = lax.psum_scatter(unit_grads, "z", scatter_dimension=0, tiled=True)
    unit_sums = sum(jnp.sum(wide(d), axis=(0, 1, 2)) for d in d_hiddens)
    d_later, low_later, d_context2, sums3 = single(
        later_back_kernel,
        [flat_float, flat_low, head_low, three_rows],
        [None] * (pieces + 3) + [kind_spec(squares[0], 2), kind_spec(squares[1], 2)],
        [],
        own, *parts3, upstream, later, gain_rows[2:3], *squares,
    )

    actives = after(actives, low_later)
    outs = [
        jnp.concatenate(
            [
                product(active[j].reshape(-1, unit_count), shrink_w).reshape(
                    len(group), row_count, model_width
                )
                for group, active in zip(groups, actives)
            ]
        )
        for j in range(cores)
    ]
    outs = outs[0] + wide(other(low(outs[1]), "core", 1))

    d_context2 = exchange(d_context2)
    leaving = after([low(out) for out in outs[1:]], d_context2)
    out_parts = [other(out, "dp", m + 1) for m, out in enumerate(leaving)]
    d_query2, d_memory, d_memory_t = attend_back(
        cross_scalars, query2, key2, value2, d_context2.reshape(part_shape), kept2, lse2,
        cross_first, cross_last, False,
    )
    d_mixed2 = exchange(after(d_query2, out_parts))
    layer_rows = low(later + outs[0] + sum(wide(part) for part in out_parts) + wide(shrink_bias))
    d_middle, low_middle, d_context1, sums2 = single(
        middle_back_kernel,
        [flat_float, flat_low, head_low, three_rows],
        [None, kind_spec(squares[0], 1), kind_spec(squares[1], 1), None, None, None]
        + [kind_spec(squares[0], 0), kind_spec(squares[1], 0)],
        [pltpu.VMEM(flat_shape, jnp.float32)],
        own, d_mixed2, *squares, d_later, middle, gain_rows[1:2], *squares,
    )
    d_context1, unit_grads = after((exchange(d_context1), unit_grads))
    layer_rows = after(layer_rows, unit_grads)
    layer_first = trade(layer_rows, "z", 0, 0)
    unit_grads = unit_grads.reshape(block_units, 2, pieces, block_rows).transpose(2, 0, 1, 3)
    unit_grads = trade(unit_grads.reshape(unit_count, 2, block_rows), "dp", 0, 0)
    d_states = [
        product(part.reshape(-1, 2 * width), cross_kv).reshape(pieces, memory_rows, model_width)
        for part in after(d_memory, d_context1)
    ]
    d_states = d_states[0] + wide(other(low(d_states[1]), "core", 1))
    leaving = [low(d_states[m]) for m in range(1, pieces)]
    state_parts = [other(part, "dp", m + 1) for m, part in enumerate(leaving)]

    d_query1, d_query1_t, d_memory1, d_memory1_t = attend_back(
        self_scalars, query1.reshape(part_shape), key1, value1, d_context1.reshape(part_shape), kept1, lse1,
        self_first, self_last, True,
    )
    kinds = 3
    square_shape = (pieces, planes, kinds, width, block_rows)
    square_mine, square_theirs = single(
        square_grad_kernel,
        [
            jax.ShapeDtypeStruct(square_shape, jnp.bfloat16),
            jax.ShapeDtypeStruct(square_shape, jnp.bfloat16),
        ],
        [None] * 6,
        [],
        own, mixed1, after(low_middle, d_context1), d_mixed2, low_two, mixed2, low_later,
    )
    square_theirs = other(square_theirs, "core", 1)
    square_sums = [wide(square_mine[m]) + wide(square_theirs[m]) for m in range(pieces)]
    square_parts = [other(low(square_sums[m]), "dp", m) for m in range(1, pieces)]
    d_query1, d_query1_t, d_memory1, d_memory1_t, square_parts, state_parts = after(
        (d_query1, d_query1_t, d_memory1, d_memory1_t, square_parts, state_parts),
        layer_first,
        unit_grads,
    )
    layer_output = trade(layer_first, "dp", 0, 0)[None]
    encoder_rows = low(d_states[0] + sum(wide(part) for part in state_parts))
    encoder_gradient = swap_planes(after(encoder_rows, layer_first))[None]
    square_sum = square_sums[0] + sum(wide(part) for part in square_parts)
    d_ones = [
        (
            product(d_query1[j].reshape(-1, width), attend_w[:width])
            + product(d_memory1[j].reshape(-1, 2 * width), attend_w[width:])
        ).reshape(pieces, row_count, model_width)
        for j in range(cores)
    ]
    d_sum = d_ones[0] + wide(other(low(d_ones[1]), "core", 1))
    leaving = [low(d_sum[m]) for m in range(1, pieces)]
    parts1 = [d_sum[0]] + [other(part, "dp", m + 1) for m, part in enumerate(leaving)]
    parts1, encoder_gradient = after((parts1, encoder_gradient))
    input_gradient, sums1 = single(
        input_back_kernel,
        [flat_low, jax.ShapeDtypeStruct((2, model_width), jnp.float32)],
        [None] * (pieces + 3),
        [],
        own, *parts1, d_middle, raw, gain_rows[0:1],
    )
    input_gradient = trade(trade(input_gradient, "z", 0, 0), "dp", 0, 0)[None]

    def turned_grad(columns, rows):
        half = columns.shape[1] // cores
        return low(
            sum(
                product(columns[:, j * half : (j + 1) * half], rows[j].reshape(half, model_width))
                for j in range(cores)
            )
        )

    def to_chips(grad):
        columns = grad.shape[0]
        split = grad.reshape(columns, pieces, block_rows).transpose(1, 0, 2)
        mine = trade(split.reshape(pieces * columns, block_rows), "dp", 0, 0)
        return mine.reshape(planes, columns, block_rows)

    cross_sum = to_chips(after(turned_grad(d_memory_t, all_states), d_query1))
    attend_sum = jnp.concatenate([turned_grad(d_query1_t, ones), turned_grad(d_memory1_t, ones)])
    attend_sum = to_chips(after(attend_sum, cross_sum))
    tail = jnp.concatenate(
        [low(square_sum).reshape(planes, 3 * width, block_rows), cross_sum, attend_sum], axis=1
    )
    tail = sum(
        wide(part if m == 0 else other(part, "z", m))
        for m, part in enumerate(
            lax.dynamic_index_in_dim(tail, plane ^ m, 0, keepdims=False) for m in range(planes)
        )
    )
    square_sum = tail[: 3 * width].reshape(3, width, block_rows)
    cross_sum, attend_sum = tail[3 * width : 5 * width], tail[5 * width :]
    unit_grads = wide(unit_grads)

    def weight_order(turned, count):
        turned = turned.reshape(count, heads, head_size, block_rows).transpose(3, 1, 0, 2)
        return turned.reshape(block_rows, count * width)

    unit_sums = lax.dynamic_update_slice(
        jnp.zeros((planes, cores, pieces, block_units), jnp.float32),
        unit_sums.reshape(planes, 1, 1, block_units),
        (0, core, piece, 0),
    ).reshape(-1)
    small = jnp.concatenate(
        [
            sums2[0],
            sums3[0],
            sums2[1],
            sums3[1],
            sums2[2],
            jnp.sum(wide(d_mixed2), axis=2).transpose(1, 0, 2).reshape(-1),
            place_heads(jnp.sum(wide(d_memory_t[width:]), axis=1)),
            sums3[2],
            jnp.sum(wide(upstream), axis=0),
            unit_sums,
        ]
    )
    last = jnp.stack(
        [
            sums1[0],
            sums1[1],
            place_heads(jnp.sum(wide(d_query1_t), axis=1)),
            place_heads(jnp.sum(wide(d_memory1_t[width:]), axis=1)),
        ]
    )
    small = sum_all(jnp.concatenate([last.reshape(-1), small]).reshape(-1, 128)).reshape(-1)
    last, small = small[: 4 * model_width].reshape(4, model_width), small[4 * model_width :]
    rows = small[: 9 * model_width].reshape(9, model_width)
    return (
        layer_output,
        input_gradient,
        encoder_gradient,
        jnp.concatenate([last[0:1], rows[0:2]]),
        jnp.concatenate([last[1:2], rows[2:4]]),
        weight_order(attend_sum, 3),
        square_sum[0],
        jnp.concatenate([last[2:4], rows[4:5]]),
        square_sum[1].T,
        weight_order(cross_sum, 2),
        square_sum[2],
        rows[5:8],
        unit_grads[:, 0].T,
        small[9 * model_width :],
        unit_grads[:, 1],
        rows[8],
    )


def solution(mesh):
    pieces, sequence = mesh.devices.shape
    planes = Mesh(mesh.devices.reshape(pieces, sequence // 2, 2), ("dp", "z", "core"))
    seq = ("z", "core")
    in_specs = (
        P("dp", seq, None),
        P("dp", seq, None),
        P("dp", None),
        P("dp", None),
        P(),
        P(),
        P("dp", seq),
        P(seq, "dp"),
        P(),
        P("dp", seq),
        P("dp", seq),
        P(seq, "dp"),
        P(),
        P("dp", seq),
        P(),
        P(seq, "dp"),
        P(),
        P("dp", seq, None),
    )
    out_specs = (
        P("dp", seq, None),
        P("dp", seq, None),
        P("dp", seq, None),
        P(),
        P(),
        P("dp", seq),
        P(seq, "dp"),
        P(),
        P("dp", seq),
        P("dp", seq),
        P(seq, "dp"),
        P(),
        P("dp", seq),
        P(),
        P(seq, "dp"),
        P(),
    )
    return jax.shard_map(
        shards, mesh=planes, in_specs=in_specs, out_specs=out_specs, check_vma=False
    )
```

```python
import functools
import math

import jax
import jax.numpy as jnp
from jax import lax
from jax.experimental import pallas as pl
from jax.experimental.pallas import tpu as pltpu
from jax.sharding import Mesh
from jax.sharding import PartitionSpec as P

HEADS = 16

epsilon = 1e-05
masked_score = -1e30
head_width = 64


def head_columns(transposed, heads):
    if heads == 1:
        return transposed
    feature = lax.broadcasted_iota(jnp.int32, transposed.shape, 0) // head_width
    zero = jnp.zeros_like(transposed)
    return jnp.concatenate([jnp.where(feature == h, transposed, zero) for h in range(heads)], axis=1)


def head_rows(block, heads):
    if heads == 1:
        return block
    feature = lax.broadcasted_iota(jnp.int32, block.shape, 1) // head_width
    zero = jnp.zeros_like(block)
    return jnp.concatenate([jnp.where(feature == h, block, zero) for h in range(heads)], axis=0)


def flip(block):
    return jnp.transpose(block.astype(jnp.float32), (1, 0)).astype(block.dtype)


def repeat_heads(row, heads):
    return row if heads == 1 else jnp.concatenate([row] * heads, axis=1)


def project(scalars, mine_ref, theirs_ref, weight_ref, bias_ref, out_refs, width):
    weight = weight_ref[...]
    bias = bias_ref[...]
    for j, source in enumerate((mine_ref, theirs_ref)):
        for m in range(source.shape[0]):
            rows = bias + lax.dot_general(
                source[m], weight, (((1,), (1,)), ((), ())), preferred_element_type=jnp.float32
            )
            rows = rows.astype(jnp.bfloat16)
            for i, out_ref in enumerate(out_refs):
                out_ref[j, m] = rows[:, i * width : (i + 1) * width]


def natural_blocks(scalars, shape, planes):
    cores, pieces, rows = shape[:3]
    part = rows // planes
    for plane in range(planes):
        for core in range(cores):
            slots = [
                ((core ^ scalars[0], piece ^ scalars[1]), plane * part) for piece in range(pieces)
            ]
            if planes == 1:
                for piece in range(pieces):
                    yield (piece * cores + core) * rows, rows, slots[piece : piece + 1]
            else:
                yield (plane * cores + core) * pieces * part, part, slots


def take_rows(ref, part, slots):
    blocks = [ref[slot[0], slot[1], first : first + part] for slot, first in slots]
    return blocks[0] if len(blocks) == 1 else jnp.concatenate(blocks, axis=0)


def query_rows_of(ref, flip_by=0):
    return jnp.concatenate([ref[0, piece ^ flip_by, 0] for piece in range(ref.shape[1])], axis=0)


def put_query_rows(ref, block, flip_by=0):
    part = ref.shape[3]
    for piece in range(ref.shape[1]):
        ref[0, piece ^ flip_by, 0] = block[piece * part : (piece + 1) * part]


def attend_rows(scalars, query, first_ref, last_ref, keys, flipped, heads, key_block):
    step = pl.program_id(0)
    steps = pl.num_programs(0)
    rows = query.shape[0]
    query = query * jnp.asarray(1.0 / math.sqrt(head_width), jnp.bfloat16)
    columns = head_columns(flip(query), heads)
    first = repeat_heads(first_ref[0], heads)
    last = repeat_heads(last_ref[0], heads)

    def one(block, carry):
        peak, total, sums = carry
        start = pl.multiple_of(block * key_block, key_block)
        scores = jnp.dot(keys[pl.ds(start, key_block), :], columns, preferred_element_type=jnp.float32)
        place = start + lax.broadcasted_iota(jnp.int32, scores.shape, 0)
        scores = jnp.where((place >= first) & (place <= last), scores, masked_score)
        newer = jnp.maximum(peak, jnp.max(scores, axis=0, keepdims=True))
        shrink = jnp.exp(peak - newer)
        exponent = jnp.exp(scores - newer)
        total = total * shrink + jnp.sum(exponent, axis=0, keepdims=True)
        low_part = exponent.astype(jnp.bfloat16)
        turned = flipped[block]
        fresh = []
        for h in range(heads):
            part = jnp.dot(
                turned[h * head_width : (h + 1) * head_width],
                low_part[:, h * rows : (h + 1) * rows],
                preferred_element_type=jnp.float32,
            )
            fresh.append(sums[h] * shrink[:, h * rows : (h + 1) * rows] + part)
        return (newer, total, tuple(fresh))

    empty = (
        jnp.full((1, heads * rows), masked_score, jnp.float32),
        jnp.zeros((1, heads * rows), jnp.float32),
        tuple(jnp.zeros((head_width, rows), jnp.float32) for _ in range(heads)),
    )
    peak, total, sums = lax.fori_loop(scalars[2 + step], scalars[2 + steps + step] + 1, one, empty)
    context = jnp.concatenate(
        [sums[h] / total[:, h * rows : (h + 1) * rows] for h in range(heads)], axis=0
    )
    return context, peak + jnp.log(total)


def prepare(scalars, k_ref, v_ref, keys, flipped, key_block, planes):
    for start, part, slots in natural_blocks(scalars, k_ref.shape, planes):
        rows = part * len(slots)
        keys[start : start + rows, :] = take_rows(k_ref, part, slots)
        offset = start % key_block
        flipped[start // key_block, :, offset : offset + rows] = flip(take_rows(v_ref, part, slots))


def finish_forward(context, lse, ctx_ref, keep_ref, lse_ref):
    keep_ref[0] = context
    lse_ref[0] = lse
    put_query_rows(ctx_ref, jnp.transpose(context, (1, 0)).astype(jnp.bfloat16))


def self_forward_kernel(
    scalars, mine_ref, theirs_ref, weight_ref, bias_ref, first_ref, last_ref,
    q_ref, k_ref, v_ref, ctx_ref, keep_ref, lse_ref, keys, flipped,
    *, heads, key_block, planes,
):
    step = pl.program_id(0)
    cores, pieces, rows = q_ref.shape[:3]
    part = rows // planes

    @pl.when(step == 0)
    def _():
        outs = (q_ref, k_ref, v_ref)
        project(scalars, mine_ref, theirs_ref, weight_ref, bias_ref, outs, heads * head_width)
        prepare(scalars, k_ref, v_ref, keys, flipped, key_block, planes)

    core = lax.rem(step, cores) ^ scalars[0]
    here = pl.ds(pl.multiple_of(lax.div(step, cores) * part, part), part)
    query = jnp.concatenate(
        [q_ref[core, piece ^ scalars[1], here, :] for piece in range(pieces)], axis=0
    )
    context, lse = attend_rows(
        scalars, query, first_ref, last_ref, keys, flipped, heads, key_block
    )
    finish_forward(context, lse, ctx_ref, keep_ref, lse_ref)


def cross_forward_kernel(
    scalars, q_ref, mine_ref, theirs_ref, weight_ref, bias_ref, first_ref, last_ref,
    k_ref, v_ref, ctx_ref, keep_ref, lse_ref, keys, flipped,
    *, heads, key_block,
):
    @pl.when(pl.program_id(0) == 0)
    def _():
        outs = (k_ref, v_ref)
        project(scalars, mine_ref, theirs_ref, weight_ref, bias_ref, outs, heads * head_width)
        prepare(scalars, k_ref, v_ref, keys, flipped, key_block, 1)

    context, lse = attend_rows(
        scalars, query_rows_of(q_ref), first_ref, last_ref, keys, flipped, heads, key_block
    )
    finish_forward(context, lse, ctx_ref, keep_ref, lse_ref)


def backward_kernel(
    scalars, q_ref, k_ref, v_ref, dc_ref, keep_ref, lse_ref, first_ref, last_ref,
    *rest, heads, key_block, planes, near,
):
    if near:
        dq_ref, dqt_ref, dkv_ref, dkvt_ref, keys, values, flipped, dkeys, dvalues = rest
    else:
        dq_ref, dkv_ref, dkvt_ref, keys, values, flipped, dkeys, dvalues = rest
    step = pl.program_id(0)
    steps = pl.num_programs(0)
    width = heads * head_width
    scaling = 1.0 / math.sqrt(head_width)

    @pl.when(step == 0)
    def _():
        prepare(scalars, k_ref, k_ref, keys, flipped, key_block, planes)
        for start, part, slots in natural_blocks(scalars, v_ref.shape, planes):
            values[start : start + part * len(slots), :] = take_rows(v_ref, part, slots)
        dkeys[...] = jnp.zeros_like(dkeys)
        dvalues[...] = jnp.zeros_like(dvalues)

    flip_by = scalars[1] if near else 0
    query = query_rows_of(q_ref, flip_by) * jnp.asarray(scaling, jnp.bfloat16)
    rows = query.shape[0]
    grad = query_rows_of(dc_ref)
    turned_grad = flip(grad)
    query_columns = head_columns(flip(query), heads)
    grad_columns = head_columns(turned_grad, heads)
    query_rows = head_rows(query, heads)
    grad_rows = head_rows(grad, heads)
    dots_kept = turned_grad.astype(jnp.float32) * keep_ref[0]
    center = jnp.concatenate(
        [
            jnp.sum(dots_kept[h * head_width : (h + 1) * head_width], axis=0, keepdims=True)
            for h in range(heads)
        ],
        axis=1,
    )
    first = repeat_heads(first_ref[0], heads)
    last = repeat_heads(last_ref[0], heads)
    lse = lse_ref[0]

    def one(block, sums):
        start = pl.multiple_of(block * key_block, key_block)
        here = pl.ds(start, key_block)
        scores = jnp.dot(keys[here, :], query_columns, preferred_element_type=jnp.float32)
        place = start + lax.broadcasted_iota(jnp.int32, scores.shape, 0)
        scores = jnp.where((place >= first) & (place <= last), scores, masked_score)
        weights = jnp.exp(scores - lse)
        dots = jnp.dot(values[here, :], grad_columns, preferred_element_type=jnp.float32)
        dscore = (weights * (dots - center)).astype(jnp.bfloat16)
        dvalues[here, :] += jnp.dot(
            weights.astype(jnp.bfloat16), grad_rows, preferred_element_type=jnp.float32
        )
        dkeys[here, :] += jnp.dot(dscore, query_rows, preferred_element_type=jnp.float32)
        turned = flipped[block]
        return tuple(
            sums[h]
            + jnp.dot(
                turned[h * head_width : (h + 1) * head_width],
                dscore[:, h * rows : (h + 1) * rows],
                preferred_element_type=jnp.float32,
            )
            for h in range(heads)
        )

    empty = tuple(jnp.zeros((head_width, rows), jnp.float32) for _ in range(heads))
    sums = lax.fori_loop(scalars[2 + step], scalars[2 + steps + step] + 1, one, empty)
    dquery = jnp.concatenate(sums, axis=0) * scaling
    dquery = jnp.transpose(dquery, (1, 0)).astype(jnp.bfloat16)
    if near:
        core = lax.rem(step, dq_ref.shape[0]) ^ scalars[0]
        plane = lax.div(step, dq_ref.shape[0])
        part = dq_ref.shape[3]
        for piece in range(dq_ref.shape[1]):
            dq_ref[core, piece ^ flip_by, plane] = dquery[piece * part : (piece + 1) * part]
    else:
        put_query_rows(dq_ref, dquery)

    @pl.when(step == steps - 1)
    def _():
        cores, pieces, key_rows = k_ref.shape[:3]
        for start, part, slots in natural_blocks(scalars, k_ref.shape, planes):
            for i, (slot, first) in enumerate(slots):
                here = slice(start + i * part, start + (i + 1) * part)
                for column, total in ((0, dkeys), (width, dvalues)):
                    dkv_ref[slot[0], slot[1], first : first + part, column : column + width] = (
                        total[here, :].astype(jnp.bfloat16)
                    )
        for j in range(cores):
            for m in range(pieces):
                place = (j * pieces + m) * key_rows
                dkvt_ref[:, place : place + key_rows] = flip(dkv_ref[j, m])
                if near:
                    block = dq_ref[j, m].reshape(key_rows, width)
                    dqt_ref[:, place : place + key_rows] = flip(block)


def whole_spec(shape, index=None):
    index = (0,) * len(shape) if index is None else index
    return pl.BlockSpec(shape, lambda step, scalars: index)


def step_spec(shape):
    return pl.BlockSpec((1,) + shape[1:], lambda step, scalars: (step, 0, 0))


def member_spec(shape, near):
    cores, pieces = shape[:2]

    def place(step, scalars):
        core = lax.rem(step, cores)
        return (core ^ scalars[0] if near else core, 0, lax.div(step, cores), 0, 0)

    return pl.BlockSpec((1, pieces, 1) + shape[3:], place)


def forward_outputs(shape):
    cores, pieces, planes, rows, width = shape
    steps = cores * planes
    heads = width // head_width
    shapes = [
        jax.ShapeDtypeStruct(shape, jnp.bfloat16),
        jax.ShapeDtypeStruct((steps, width, pieces * rows), jnp.float32),
        jax.ShapeDtypeStruct((steps, 1, heads * pieces * rows), jnp.float32),
    ]
    specs = [member_spec(shape, False), step_spec(shapes[1].shape), step_spec(shapes[2].shape)]
    return shapes, specs


def cost(microseconds):
    return pl.CostEstimate(
        flops=int(microseconds * 1.1e9), bytes_accessed=1 << 20, transcendentals=0
    )


def params(mebibytes=56):
    return pltpu.CompilerParams(vmem_limit_bytes=mebibytes * 2**20)


def self_forward(scalars, mine, theirs, planes, weight, bias, first, last):
    pieces, rows, model_width = mine.shape
    width = weight.shape[0] // 3
    shape = (2, pieces, rows, width)
    steps = 2 * planes
    key_count = 2 * pieces * rows
    key_block = min(256, key_count)
    shapes, specs = forward_outputs((2, pieces, planes, rows // planes, width))
    full = jax.ShapeDtypeStruct(shape, jnp.bfloat16)
    return pl.pallas_call(
        functools.partial(
            self_forward_kernel, heads=width // head_width, key_block=key_block, planes=planes
        ),
        grid_spec=pltpu.PrefetchScalarGridSpec(
            num_scalar_prefetch=1,
            grid=(steps,),
            in_specs=[
                whole_spec(mine.shape),
                whole_spec(theirs.shape),
                whole_spec(weight.shape),
                whole_spec(bias.shape),
                step_spec(first.shape),
                step_spec(last.shape),
            ],
            out_specs=[whole_spec(shape)] * 3 + specs,
            scratch_shapes=[
                pltpu.VMEM((key_count, width), jnp.bfloat16),
                pltpu.VMEM((key_count // key_block, width, key_block), jnp.bfloat16),
            ],
        ),
        out_shape=[full] * 3 + shapes,
        compiler_params=params(),
        cost_estimate=cost(16),
    )(scalars, mine, theirs, weight, bias, first, last)


def cross_forward(scalars, queries, mine, theirs, weight, bias, first, last):
    cores, pieces, planes, rows, width = queries.shape
    state_rows = mine.shape[1]
    steps = cores * planes
    key_count = cores * pieces * state_rows
    key_block = min(256, key_count)
    shapes, specs = forward_outputs(queries.shape)
    key_shape = (cores, pieces, state_rows, width)
    full = jax.ShapeDtypeStruct(key_shape, jnp.bfloat16)
    return pl.pallas_call(
        functools.partial(cross_forward_kernel, heads=width // head_width, key_block=key_block),
        grid_spec=pltpu.PrefetchScalarGridSpec(
            num_scalar_prefetch=1,
            grid=(steps,),
            in_specs=[
                member_spec(queries.shape, False),
                whole_spec(mine.shape),
                whole_spec(theirs.shape),
                whole_spec(weight.shape),
                whole_spec(bias.shape),
                step_spec(first.shape),
                step_spec(last.shape),
            ],
            out_specs=[whole_spec(key_shape)] * 2 + specs,
            scratch_shapes=[
                pltpu.VMEM((key_count, width), jnp.bfloat16),
                pltpu.VMEM((key_count // key_block, width, key_block), jnp.bfloat16),
            ],
        ),
        out_shape=[full] * 2 + shapes,
        compiler_params=params(),
        cost_estimate=cost(11),
    )(scalars, queries, mine, theirs, weight, bias, first, last)


def attend_back(scalars, queries, key_rows, values, grad, kept, lse, first, last, near):
    cores, pieces, planes, rows, width = queries.shape
    steps = cores * planes
    key_shape = key_rows.shape
    key_count = cores * pieces * key_shape[2]
    key_block = min(256, key_count)
    dq_shape = jax.ShapeDtypeStruct(queries.shape, jnp.bfloat16)
    if near:
        dq_shapes = [dq_shape, jax.ShapeDtypeStruct((width, key_count), jnp.bfloat16)]
        dq_specs = [whole_spec(queries.shape), whole_spec((width, key_count))]
    else:
        dq_shapes, dq_specs = [dq_shape], [member_spec(queries.shape, False)]
    return pl.pallas_call(
        functools.partial(
            backward_kernel,
            heads=width // head_width,
            key_block=key_block,
            planes=planes if near else 1,
            near=near,
        ),
        grid_spec=pltpu.PrefetchScalarGridSpec(
            num_scalar_prefetch=1,
            grid=(steps,),
            in_specs=[
                member_spec(queries.shape, near),
                whole_spec(key_shape),
                whole_spec(key_shape),
                member_spec(grad.shape, False),
                step_spec(kept.shape),
                step_spec(lse.shape),
                step_spec(first.shape),
                step_spec(last.shape),
            ],
            out_specs=dq_specs
            + [whole_spec(key_shape[:3] + (2 * width,)), whole_spec((2 * width, key_count))],
            scratch_shapes=[
                pltpu.VMEM((key_count, width), jnp.bfloat16),
                pltpu.VMEM((key_count, width), jnp.bfloat16),
                pltpu.VMEM((key_count // key_block, width, key_block), jnp.bfloat16),
                pltpu.VMEM((key_count, width), jnp.float32),
                pltpu.VMEM((key_count, width), jnp.float32),
            ],
        ),
        out_shape=dq_shapes
        + [
            jax.ShapeDtypeStruct(key_shape[:3] + (2 * width,), jnp.bfloat16),
            jax.ShapeDtypeStruct((2 * width, key_count), jnp.bfloat16),
        ],
        compiler_params=params(),
        cost_estimate=cost(12),
    )(scalars, queries, key_rows, values, grad, kept, lse, first, last)


def single(kernel, out_shape, in_specs, scratch, *args):
    return pl.pallas_call(
        kernel,
        grid_spec=pltpu.PrefetchScalarGridSpec(
            num_scalar_prefetch=1,
            grid=(1,),
            in_specs=[
                whole_spec(value.shape) if spec is None else spec
                for spec, value in zip(in_specs, args[1:])
            ],
            out_specs=[whole_spec(value.shape) for value in out_shape],
            scratch_shapes=scratch,
        ),
        out_shape=out_shape,
        compiler_params=params(),
        cost_estimate=cost(4),
    )(*args)


def kind_spec(array, kind):
    shape = (array.shape[0], array.shape[1], 1) + array.shape[3:]
    return whole_spec(shape, (0, 0, kind, 0, 0))


def square_block(ref, m):
    block = ref[m, :, 0]
    return block.reshape(block.shape[0] * block.shape[1], block.shape[2])


def heads_of(ref, core):
    return jnp.concatenate([ref[core, piece] for piece in range(ref.shape[1])], axis=1)


def near_span(scalars, m, size):
    return pl.ds(pl.multiple_of((scalars[1] ^ m) * size, size), size)


def heads_to_model(scalars, heads_ref, mine_ref, theirs_ref, sums):
    mine, theirs = heads_of(heads_ref, scalars[0]), heads_of(heads_ref, 1 ^ scalars[0])
    size = mine_ref.shape[4]
    for m in range(mine_ref.shape[0]):
        sums[:, near_span(scalars, m, size)] = jnp.dot(
            mine, square_block(mine_ref, m), preferred_element_type=jnp.float32
        ) + jnp.dot(theirs, square_block(theirs_ref, m), preferred_element_type=jnp.float32)


def model_to_heads(scalars, rows_ref, mine_ref, theirs_ref, heads_ref, bias_ref=None):
    size = mine_ref.shape[4]
    pieces, width = heads_ref.shape[1], heads_ref.shape[3]
    for j, weight_ref in enumerate((mine_ref, theirs_ref)):
        total = 0.0
        for m in range(weight_ref.shape[0]):
            total = total + lax.dot_general(
                rows_ref[:, near_span(scalars, m, size)],
                square_block(weight_ref, m),
                (((1,), (1,)), ((), ())),
                preferred_element_type=jnp.float32,
            )
        core = scalars[0] ^ j
        for piece in range(pieces):
            block = total[:, piece * width : (piece + 1) * width]
            if bias_ref is not None:
                block = block + bias_ref[core, piece]
            heads_ref[core, piece] = block.astype(jnp.bfloat16)


def normal_parts(values):
    center = values - jnp.mean(values, axis=-1, keepdims=True)
    spread = jnp.mean(center * center, axis=-1, keepdims=True)
    scale = lax.rsqrt(spread + epsilon)
    return center * scale, scale


def norm_back(values, gain, dn):
    normal, scale = normal_parts(values)
    e = dn * gain
    dv = scale * (
        e
        - jnp.mean(e, axis=-1, keepdims=True)
        - normal * jnp.mean(e * normal, axis=-1, keepdims=True)
    )
    return (
        dv,
        jnp.sum(dn * normal, axis=0, keepdims=True),
        jnp.sum(dn, axis=0, keepdims=True),
    )


def middle_kernel(
    scalars, heads_ref, omine_ref, otheirs_ref, resid_ref, rows_ref, qmine_ref, qtheirs_ref,
    qbias_ref, sum_ref, norm_ref, q_ref,
):
    heads_to_model(scalars, heads_ref, omine_ref, otheirs_ref, sum_ref)
    total = sum_ref[...] + resid_ref[...].astype(jnp.float32) + rows_ref[0:1]
    sum_ref[...] = total
    normal, _ = normal_parts(total)
    norm_ref[...] = (normal * rows_ref[1:2] + rows_ref[2:3]).astype(jnp.bfloat16)
    model_to_heads(scalars, norm_ref, qmine_ref, qtheirs_ref, q_ref, qbias_ref)


def later_kernel(
    scalars, heads_ref, omine_ref, otheirs_ref, resid_ref, rows_ref, sum_ref, norm_ref
):
    heads_to_model(scalars, heads_ref, omine_ref, otheirs_ref, sum_ref)
    total = sum_ref[...] + resid_ref[...] + rows_ref[0:1]
    sum_ref[...] = total
    normal, _ = normal_parts(total)
    norm_ref[...] = (normal * rows_ref[1:2] + rows_ref[2:3]).astype(jnp.bfloat16)


def finish_back(scalars, values_ref, rows_ref, dn, upper, mine_ref, theirs_ref, d_ref, low_ref, heads_ref, sums_ref):
    dv, dg, db = norm_back(values_ref[...], rows_ref[0:1], dn)
    total = upper + dv
    d_ref[...] = total
    low_total = total.astype(jnp.bfloat16)
    low_ref[...] = low_total
    sums_ref[0:1] = dg
    sums_ref[1:2] = db
    sums_ref[2:3] = jnp.sum(low_total.astype(jnp.float32), axis=0, keepdims=True)
    model_to_heads(scalars, low_ref, mine_ref, theirs_ref, heads_ref)


def later_back_kernel(scalars, *refs):
    parts, (up_ref, values_ref, rows_ref, mine_ref, theirs_ref) = refs[:-9], refs[-9:-4]
    dn = parts[0][...].reshape(up_ref.shape)
    for part in parts[1:]:
        dn = dn + part[...].reshape(up_ref.shape).astype(jnp.float32)
    upper = up_ref[...].astype(jnp.float32)
    finish_back(scalars, values_ref, rows_ref, dn, upper, mine_ref, theirs_ref, *refs[-4:])


def middle_back_kernel(
    scalars, heads_ref, qmine_ref, qtheirs_ref, upper_ref, values_ref, rows_ref, mine_ref,
    theirs_ref, d_ref, low_ref, dheads_ref, sums_ref, work,
):
    heads_to_model(scalars, heads_ref, qmine_ref, qtheirs_ref, work)
    finish_back(
        scalars, values_ref, rows_ref, work[...], upper_ref[...], mine_ref, theirs_ref,
        d_ref, low_ref, dheads_ref, sums_ref,
    )


def input_back_kernel(scalars, *refs):
    parts, (upper_ref, values_ref, rows_ref, out_ref, sums_ref) = refs[:-5], refs[-5:]
    dn = parts[0][...].reshape(upper_ref.shape)
    for part in parts[1:]:
        dn = dn + part[...].reshape(upper_ref.shape).astype(jnp.float32)
    dv, dg, db = norm_back(values_ref[...].astype(jnp.float32), rows_ref[0:1], dn)
    out_ref[...] = (upper_ref[...] + dv).astype(jnp.bfloat16)
    sums_ref[0:1] = dg
    sums_ref[1:2] = db


def square_grad_kernel(scalars, *refs):
    kinds = (len(refs) - 2) // 2
    mine_ref, theirs_ref = refs[-2:]
    size = mine_ref.shape[4]
    for kind in range(kinds):
        heads_ref, rows_ref = refs[2 * kind], refs[2 * kind + 1]
        for j, out_ref in enumerate((mine_ref, theirs_ref)):
            for piece in range(heads_ref.shape[1]):
                turned = flip(heads_ref[scalars[0] ^ j, piece])
                for m in range(out_ref.shape[0]):
                    out_ref[m, piece, kind] = jnp.dot(
                        turned,
                        rows_ref[:, near_span(scalars, m, size)],
                        preferred_element_type=jnp.float32,
                    ).astype(out_ref.dtype)


def gelu_parts(u):
    root = math.sqrt(2.0 / math.pi)
    square = u * u
    bent = jnp.tanh(root * (u + 0.044715 * (square * u)))
    half = 0.5 * (1.0 + bent)
    slope = half + 0.5 * u * (1.0 - bent * bent) * (root * (1.0 + 3.0 * 0.044715 * square))
    return u * half, slope


def units_kernel(
    scalars, mine_ref, theirs_ref, upmine_ref, uptheirs_ref, expand_ref, shrink_ref, bias_ref,
    active_ref, dhidden_ref, dmine_ref, dtheirs_ref, outmine_ref, outtheirs_ref, half_count,
):
    step = pl.program_id(0)
    expand, shrink = expand_ref[...], shrink_ref[...]
    against_last = (((1,), (1,)), ((), ()))

    def one(rows, up):
        hidden = lax.dot_general(rows, expand, against_last, preferred_element_type=jnp.float32)
        dactive = lax.dot_general(up, shrink, against_last, preferred_element_type=jnp.float32)
        active, slope = gelu_parts(hidden + bias_ref[...])
        dhidden = (dactive * slope).astype(jnp.bfloat16)
        active = active.astype(jnp.bfloat16)
        active_ref[0, 0] = active
        dhidden_ref[0, 0] = dhidden
        return (
            jnp.dot(dhidden, expand, preferred_element_type=jnp.float32),
            jnp.dot(active, shrink, preferred_element_type=jnp.float32),
        )

    @pl.when(step < half_count)
    def _():
        dthree, out = one(theirs_ref[0], uptheirs_ref[0])
        dtheirs_ref[0] = dthree.astype(jnp.bfloat16)
        outtheirs_ref[0] = out.astype(jnp.bfloat16)

    @pl.when(step >= half_count)
    def _():
        dthree, out = one(mine_ref[0], upmine_ref[0])
        dmine_ref[0] = dthree
        outmine_ref[0] = out


def units_group(scalars, mine, theirs, ups, start, expand_t, shrink_w, bias):
    count, rows, model_width = mine.shape
    units = expand_t.shape[0]

    def piece_spec(own, offset=0):
        if own:
            place = lambda step, scalars: (jnp.maximum(step - count, 0) + offset, 0, 0)
        else:
            place = lambda step, scalars: (jnp.minimum(step, count - 1) + offset, 0, 0)
        return pl.BlockSpec((1, rows, model_width), place)

    def table_place(step, scalars):
        return (1 - lax.div(step, count), lax.rem(step, count), 0, 0)

    table = jax.ShapeDtypeStruct((2, count, rows, units), jnp.bfloat16)
    table_spec = pl.BlockSpec((1, 1, rows, units), table_place)
    return pl.pallas_call(
        functools.partial(units_kernel, half_count=count),
        grid_spec=pltpu.PrefetchScalarGridSpec(
            num_scalar_prefetch=1,
            grid=(2 * count,),
            in_specs=[
                piece_spec(True),
                piece_spec(False),
                piece_spec(True, start),
                piece_spec(False, start),
                whole_spec(expand_t.shape),
                whole_spec(shrink_w.shape),
                whole_spec(bias.shape),
            ],
            out_specs=[table_spec, table_spec] + [piece_spec(True), piece_spec(False)] * 2,
        ),
        out_shape=[
            table,
            table,
            jax.ShapeDtypeStruct(mine.shape, jnp.float32),
            jax.ShapeDtypeStruct(mine.shape, jnp.bfloat16),
        ]
        + [
            jax.ShapeDtypeStruct(mine.shape, jnp.float32),
            jax.ShapeDtypeStruct(mine.shape, jnp.bfloat16),
        ],
        compiler_params=params(32),
        cost_estimate=cost(6.5 * count),
    )(scalars, mine, theirs, *ups, expand_t, shrink_w, bias)


def unit_gradients_kernel(scalars, *refs, counts):
    dhidden_refs, active_refs = refs[0:2], refs[2:4]
    row_refs, up_refs = (refs[4:6], refs[6:8]), refs[8:10]
    out_ref, expand_sum, shrink_sum = refs[10:]
    step = pl.program_id(0)
    width = expand_sum.shape[1]

    @pl.when(step == 0)
    def _():
        expand_sum[...] = jnp.zeros_like(expand_sum)
        shrink_sum[...] = jnp.zeros_like(shrink_sum)

    def add(group, core):
        for table_ref, rows_ref, total in (
            (dhidden_refs[group], row_refs[group][core], expand_sum),
            (active_refs[group], up_refs[core], shrink_sum),
        ):
            total[...] += lax.dot_general(
                table_ref[0, 0],
                rows_ref[0],
                (((0,), (0,)), ((), ())),
                preferred_element_type=jnp.float32,
            )

    first = 0
    for group, count in enumerate(counts):
        for core in range(2):
            @pl.when((step >= first) & (step < first + count))
            def _(group=group, core=core):
                add(group, core)

            first += count

    @pl.when(step == pl.num_programs(0) - 1)
    def _():
        out_ref[:, :width] = expand_sum[...].astype(jnp.bfloat16)
        out_ref[:, width:] = shrink_sum[...].astype(jnp.bfloat16)


def unit_gradients(scalars, dhiddens, actives, rows, ups):
    counts = [table.shape[1] for table in actives]
    _, _, tokens, units = actives[0].shape
    model_width = ups[0].shape[2]
    starts = [2 * sum(counts[:i]) for i in range(len(counts))]

    def table_spec(group):
        count, start = counts[group], starts[group]

        def place(step, scalars):
            here = jnp.clip(step - start, 0, 2 * count - 1)
            return (lax.div(here, count), lax.rem(here, count), 0, 0)

        return pl.BlockSpec((1, 1, tokens, units), place)

    def row_place(group, core):
        count, start = counts[group], starts[group] + core * counts[group]
        return pl.BlockSpec(
            (1, tokens, model_width),
            lambda step, scalars: (jnp.clip(step - start, 0, count - 1), 0, 0),
        )

    def up_place(core):
        def place(step, scalars):
            here = 0
            for i in range(len(counts)):
                inside = jnp.clip(step - starts[i] - core * counts[i], 0, counts[i] - 1)
                begun = (step >= starts[i] + core * counts[i]).astype(jnp.int32)
                here = jnp.where(begun == 1, sum(counts[:i]) + inside, here)
            return (here, 0, 0)

        return pl.BlockSpec((1, tokens, model_width), place)

    return pl.pallas_call(
        functools.partial(unit_gradients_kernel, counts=counts),
        grid_spec=pltpu.PrefetchScalarGridSpec(
            num_scalar_prefetch=1,
            grid=(2 * sum(counts),),
            in_specs=[table_spec(0), table_spec(1), table_spec(0), table_spec(1)]
            + [row_place(0, 0), row_place(0, 1), row_place(1, 0), row_place(1, 1)]
            + [up_place(0), up_place(1)],
            out_specs=whole_spec((units, 2 * model_width)),
            scratch_shapes=[pltpu.VMEM((units, model_width), jnp.float32)] * 2,
        ),
        out_shape=jax.ShapeDtypeStruct((units, 2 * model_width), jnp.bfloat16),
        compiler_params=params(),
        cost_estimate=cost(12),
    )(scalars, *dhiddens, *actives, *rows[0], *rows[1], *ups)


def layer_norm(values, gain_row, shift_row):
    center = values - jnp.mean(values, axis=-1, keepdims=True)
    spread = jnp.mean(center * center, axis=-1, keepdims=True)
    return center * lax.rsqrt(spread + epsilon) * gain_row + shift_row


def inner_rows(former, latter):
    return lax.dot_general(
        former, latter, (((0,), (0,)), ((), ())), preferred_element_type=jnp.float32
    )


def against(former, latter):
    return lax.dot_general(
        former, latter, (((1,), (1,)), ((), ())), preferred_element_type=jnp.float32
    )


def product(former, latter):
    return jnp.dot(former, latter, preferred_element_type=jnp.float32)


def low(values):
    return values.astype(jnp.bfloat16)


def wide(values):
    return values.astype(jnp.float32)


def other(values, axis, shift):
    count = lax.axis_size(axis)
    return lax.ppermute(values, axis, [(i, i ^ shift) for i in range(count)])


def trade(values, axis, split, concat):
    return lax.all_to_all(values, axis, split_axis=split, concat_axis=concat, tiled=True)


def after(values, *earlier):
    return lax.optimization_barrier((values, earlier))[0]


PLANE = ("core", "dp")


def chips_gather(block, axis="dp"):
    return [block] + [other(block, axis, m) for m in range(1, lax.axis_size(axis))]


def plane_gather(block):
    mine = jnp.stack(chips_gather(block))
    return mine, other(mine, "core", 1)


def plane_reduce(mine, theirs):
    sums = mine + wide(other(low(theirs), "core", 1))
    total = sums[0]
    for m in range(1, sums.shape[0]):
        total = total + wide(other(low(sums[m]), "dp", m))
    return total


def swap_planes(values, hop=0):
    pieces, planes, cores = (lax.axis_size(axis) for axis in ("dp", "z", "core"))
    pairs = [
        (((d ^ hop) * planes + z) * cores + c, (z * planes + d) * cores + c)
        for d in range(pieces)
        for z in range(planes)
        for c in range(cores)
    ]
    return lax.ppermute(values, ("dp", "z", "core"), pairs)


def put_blocks(blocks, axis, dimension):
    size = blocks[0].shape[dimension]
    shape = list(blocks[0].shape)
    shape[dimension] = size * len(blocks)
    whole = jnp.zeros(shape, blocks[0].dtype)
    for m, block in enumerate(blocks):
        start = [0] * len(shape)
        start[dimension] = (lax.axis_index(axis) ^ m) * size
        whole = lax.dynamic_update_slice(whole, block, start)
    return whole


def sum_all(values):
    for axis in ("core", "dp", "z"):
        shift = 1
        while shift < lax.axis_size(axis):
            values = values + other(values, axis, shift)
            shift *= 2
    return values


def document_edges(ids, memory_ids, steps):
    documents = jnp.arange(4, dtype=jnp.int32)
    starts = jnp.sum((memory_ids[None] < documents[:, None]).astype(jnp.int32), axis=1)
    ends = jnp.sum((memory_ids[None] <= documents[:, None]).astype(jnp.int32), axis=1) - 1
    match = ids[None] == documents[:, None]
    first = jnp.sum(jnp.where(match, starts[:, None], 0), axis=0)
    last = jnp.sum(jnp.where(match, ends[:, None], 0), axis=0)
    return (first.reshape(steps, 1, -1), last.reshape(steps, 1, -1))


def shards(
    inputs,
    encoder_states,
    segment_ids,
    encoder_ids,
    norm_gains,
    norm_shifts,
    attend_weights,
    attend_output,
    attend_biases,
    cross_query,
    cross_memory,
    cross_output,
    cross_biases,
    expand_weight,
    expand_bias,
    shrink_weight,
    shrink_bias,
    output_cotangent,
):
    pieces, planes, cores = lax.axis_size("dp"), lax.axis_size("z"), lax.axis_size("core")
    piece, plane, core = lax.axis_index("dp"), lax.axis_index("z"), lax.axis_index("core")
    members = pieces * cores
    member = core * pieces + piece
    row_count, model_width = inputs.shape[1:]
    memory_rows = encoder_states.shape[1]
    pack_rows, pack_memory = segment_ids.shape[1], encoder_ids.shape[1]
    heads = HEADS // members
    head_size = model_width // HEADS
    width = heads * head_size
    steps = planes * cores
    unit_count = expand_weight.shape[1]
    block_units = unit_count // pieces
    block_rows = model_width // pieces

    all_ids = swap_planes(jnp.concatenate([segment_ids[0], encoder_ids[0]]))
    pack_ids, memory_ids = all_ids[:pack_rows], all_ids[pack_rows:]
    attend_at = lax.all_gather(attend_weights.T, "z", axis=0, tiled=True)
    raw = trade(after(trade(inputs[0], "dp", 0, 0), attend_at), "z", 0, 0)

    def columns_of(weight, count):
        weight = weight.reshape(pieces, heads, count, head_size, block_rows)
        return weight.transpose(2, 1, 3, 0, 4).reshape(count * width, model_width)

    near_w = jnp.concatenate([cross_memory.T, attend_output, cross_query.T, cross_output])
    near_w = lax.all_gather(after(near_w, attend_at), "z", axis=0, tiled=True)
    near_w = near_w.reshape(planes, 5 * width, block_rows)
    attend_w = trade(after(attend_at, raw), "dp", 0, 0).reshape(pieces, 3 * width, block_rows)
    upstream = trade(after(output_cotangent[0], attend_w), "dp", 0, 0)
    squares = near_w[:, 2 * width :].reshape(planes, 3, width, block_rows)
    cross_kv = near_w[:, : 2 * width].reshape(planes * 2 * width, block_rows)
    unit_w = jnp.stack([expand_weight.T, shrink_weight], axis=1)
    unit_parts = []
    for m in range(pieces):
        part = lax.dynamic_slice_in_dim(unit_w, (piece ^ m) * block_units, block_units, 0)
        unit_parts.append(part if m == 0 else other(part, "dp", m))
    unit_w = put_blocks(unit_parts, "dp", 2).reshape(block_units, 2 * model_width)
    states = swap_planes(after(encoder_states[0], raw))
    whole_units = lax.all_gather(after(unit_w, near_w), "z", axis=0, tiled=True)
    expand_t, shrink_w = whole_units[:, :model_width], whole_units[:, model_width:]
    attend_w = columns_of(attend_w, 3)

    own = jnp.stack([core, piece]).astype(jnp.int32)
    key_block = min(256, pack_rows)
    self_first, _ = document_edges(pack_ids, pack_ids, steps)
    self_last = jnp.arange(pack_rows, dtype=jnp.int32).reshape(steps, 1, -1)
    self_scalars = jnp.concatenate(
        [own, self_first[:, 0, 0] // key_block, self_last[:, 0, -1] // key_block]
    )
    cross_first, cross_last = document_edges(pack_ids, memory_ids, steps)
    key_block = min(256, pack_memory)
    cross_scalars = jnp.concatenate(
        [own, cross_first[:, 0, 0] // key_block, cross_last[:, 0, -1] // key_block]
    )

    gain_rows, shift_rows = wide(norm_gains), wide(norm_shifts)
    bias_self, bias_cross = wide(attend_biases), wide(cross_biases)

    def of_heads(row):
        return lax.dynamic_slice_in_dim(row, (piece * cores + core) * width, width, 0)

    def place_heads(row):
        return lax.dynamic_update_slice(
            jnp.zeros((model_width,), jnp.float32), row, ((piece * cores + core) * width,)
        )

    zero_heads = jnp.zeros((width,), jnp.float32)
    packed_bias = jnp.concatenate([of_heads(bias_self[0]), zero_heads, of_heads(bias_self[1])])
    memory_bias = jnp.concatenate([zero_heads, of_heads(bias_cross[1])])
    query_bias = bias_cross[0].reshape(pieces, cores, 1, width).transpose(1, 0, 2, 3)
    token_shape = (cores, pieces, row_count, width)
    part_shape = (cores, pieces, planes, row_count // planes, width)
    flat_shape = (row_count, model_width)
    flat_float = jax.ShapeDtypeStruct(flat_shape, jnp.float32)
    flat_low = jax.ShapeDtypeStruct(flat_shape, jnp.bfloat16)
    head_low = jax.ShapeDtypeStruct(token_shape, jnp.bfloat16)
    three_rows = jax.ShapeDtypeStruct((3, model_width), jnp.float32)

    def exchange(values):
        return trade(values.reshape(pieces * cores * row_count, width), PLANE, 0, 0).reshape(
            token_shape
        )

    low_one = low(layer_norm(wide(raw), gain_rows[0], shift_rows[0]))
    mine = jnp.stack(chips_gather(after(low_one, unit_w)))
    mine, states = after((mine, states), attend_w, near_w)
    squares = after(squares, mine)
    state_parts = chips_gather(after(states, mine))
    squares = after(squares, state_parts)
    ones = (mine, other(mine, "core", 1))
    square_parts = chips_gather(squares)
    query1, key1, value1, context1, kept1, lse1 = self_forward(
        self_scalars, *ones, planes, attend_w, packed_bias[None], self_first, self_last
    )
    context1, square_parts = after((context1, square_parts), upstream)
    squares = jnp.stack(square_parts)
    squares = (squares, other(squares, "core", 1))
    mixed1 = exchange(context1)
    cross_kv = trade(after(cross_kv, mixed1), "dp", 0, 0).reshape(pieces, 2 * width, block_rows)
    cross_kv = columns_of(cross_kv, 2)
    middle, low_two, query2 = single(
        middle_kernel,
        [flat_float, flat_low, head_low],
        [None, kind_spec(squares[0], 0), kind_spec(squares[1], 0), None, None]
        + [kind_spec(squares[0], 1), kind_spec(squares[1], 1), None],
        [],
        own, mixed1, *squares, raw,
        jnp.stack([bias_self[2], gain_rows[1], shift_rows[1]]),
        *squares, query_bias,
    )

    all_states = jnp.stack(state_parts)
    all_states = (all_states, other(after(all_states, mixed1), "core", 1))
    query2 = exchange(query2)
    query2 = query2.reshape(part_shape)
    key2, value2, context2, kept2, lse2 = cross_forward(
        cross_scalars, query2, *all_states, cross_kv, memory_bias[None],
        cross_first, cross_last,
    )
    upstream = trade(after(upstream, query2), "z", 0, 0)
    context2, upstream = after((context2, upstream))
    ups = jnp.stack(chips_gather(upstream))
    all_ups = (ups, other(ups, "core", 1))
    context2 = after(context2, whole_units)
    mixed2 = exchange(context2)
    later, low_three = single(
        later_kernel,
        [flat_float, flat_low],
        [None, kind_spec(squares[0], 2), kind_spec(squares[1], 2), None, None],
        [],
        own, mixed2, *squares, middle,
        jnp.stack([bias_cross[2], gain_rows[2], shift_rows[2]]),
    )

    bias_units = wide(expand_bias).reshape(planes, cores, pieces, block_units)
    bias_units = lax.dynamic_slice(
        bias_units, (0, core, piece, 0), (planes, 1, 1, block_units)
    ).reshape(1, unit_count)
    groups = [list(range(pieces - 1)), [pieces - 1]]
    pieces3 = chips_gather(low_three)
    threes, actives, d_hiddens, parts3, leaving, out_groups = [], [], [], [], [], []
    for group in groups:
        mine = jnp.stack([pieces3[m] for m in group])
        if d_hiddens:
            mine = after(mine, d_hiddens[-1])
        theirs = other(mine, "core", 1)
        active, d_hidden, d_mine, d_theirs, out_mine, out_theirs = units_group(
            own, mine, theirs, all_ups, group[0], expand_t, shrink_w, bias_units
        )
        d_sum = d_mine + wide(other(d_theirs, "core", 1))
        for i, m in enumerate(group):
            leaving.append(d_sum[i] if m == 0 else low(d_sum[i]))
            parts3.append(leaving[-1] if m == 0 else other(leaving[-1], "dp", m))
        threes.append((mine, theirs))
        out_groups.append((out_mine, out_theirs))
        actives.append(active)
        d_hiddens.append(d_hidden)
    actives, d_hiddens = after((actives, d_hiddens), leaving)

    unit_grads = unit_gradients(own, d_hiddens, actives, threes, all_ups)
    unit_grads, parts3 = after((unit_grads, parts3))
    unit_grads = lax.psum_scatter(unit_grads, "z", scatter_dimension=0, tiled=True)
    unit_sums = sum(jnp.sum(wide(d), axis=(0, 1, 2)) for d in d_hiddens)
    d_later, low_later, d_context2, sums3 = single(
        later_back_kernel,
        [flat_float, flat_low, head_low, three_rows],
        [None] * (pieces + 3) + [kind_spec(squares[0], 2), kind_spec(squares[1], 2)],
        [],
        own, *parts3, upstream, later, gain_rows[2:3], *squares,
    )

    out_groups = [
        mine + wide(other(after(theirs, low_later), "core", 1)) for mine, theirs in out_groups
    ]
    outs = [group[i] for group in out_groups for i in range(group.shape[0])]
    d_context2 = exchange(d_context2)
    leaving = after([low(out) for out in outs[1:]], d_context2)
    out_parts = [other(out, "dp", m + 1) for m, out in enumerate(leaving)]
    d_query2, d_memory, d_memory_t = attend_back(
        cross_scalars, query2, key2, value2, d_context2.reshape(part_shape), kept2, lse2,
        cross_first, cross_last, False,
    )
    d_mixed2 = exchange(after(d_query2, out_parts))
    layer_rows = low(later + outs[0] + sum(wide(part) for part in out_parts) + wide(shrink_bias))
    d_middle, low_middle, d_context1, sums2 = single(
        middle_back_kernel,
        [flat_float, flat_low, head_low, three_rows],
        [None, kind_spec(squares[0], 1), kind_spec(squares[1], 1), None, None, None]
        + [kind_spec(squares[0], 0), kind_spec(squares[1], 0)],
        [pltpu.VMEM(flat_shape, jnp.float32)],
        own, d_mixed2, *squares, d_later, middle, gain_rows[1:2], *squares,
    )
    d_context1, unit_grads = after((exchange(d_context1), unit_grads))

    def turned_grad(columns, rows):
        half = columns.shape[1] // cores
        return low(
            sum(
                product(columns[:, j * half : (j + 1) * half], rows[j].reshape(half, model_width))
                for j in range(cores)
            )
        )

    def to_chips(*grads):
        split = [grad.reshape(-1, pieces, block_rows) for grad in grads]
        return trade(jnp.concatenate(split).transpose(1, 0, 2), "dp", 0, 0)

    unit_grads = to_chips(
        unit_grads.reshape(2 * block_units, model_width),
        turned_grad(after(d_memory_t, d_context1), all_states),
    )
    d_query1, d_query1_t, d_memory1, d_memory1_t = attend_back(
        self_scalars, query1.reshape(part_shape), key1, value1, d_context1.reshape(part_shape), kept1, lse1,
        self_first, self_last, True,
    )
    d_query1, d_query1_t, d_memory1, d_memory1_t, unit_grads = after(
        (d_query1, d_query1_t, d_memory1, d_memory1_t, unit_grads)
    )
    cross_sum = unit_grads[:, 2 * block_units :]
    unit_grads = unit_grads[:, : 2 * block_units].reshape(unit_count, 2, block_rows)
    d_ones = [
        (
            product(d_query1[j].reshape(-1, width), attend_w[:width])
            + product(d_memory1[j].reshape(-1, 2 * width), attend_w[width:])
        ).reshape(pieces, row_count, model_width)
        for j in range(cores)
    ]
    d_sum = d_ones[0] + wide(other(low(d_ones[1]), "core", 1))
    leaving = [low(d_sum[m]) for m in range(1, pieces)]
    parts1 = [d_sum[0]] + [other(part, "dp", m + 1) for m, part in enumerate(leaving)]

    d_memory, low_middle_late, layer_rows, turned_late = after(
        (d_memory, low_middle, layer_rows, (d_query1_t, d_memory1_t)), leaving
    )
    layer_first = trade(layer_rows, "z", 0, 0)
    d_states = [
        product(part.reshape(-1, 2 * width), cross_kv).reshape(pieces, memory_rows, model_width)
        for part in d_memory
    ]
    d_states = d_states[0] + wide(other(low(d_states[1]), "core", 1))
    kinds = 3
    square_shape = (pieces, planes, kinds, width, block_rows)
    square_mine, square_theirs = single(
        square_grad_kernel,
        [
            jax.ShapeDtypeStruct(square_shape, jnp.bfloat16),
            jax.ShapeDtypeStruct(square_shape, jnp.bfloat16),
        ],
        [None] * 6,
        [],
        own, mixed1, low_middle_late, d_mixed2, low_two, mixed2, low_later,
    )
    attend_sum = [turned_grad(turned, ones) for turned in turned_late]
    parts1, layer_first, d_states, square_mine, square_theirs, attend_sum = after(
        (parts1, layer_first, d_states, square_mine, square_theirs, attend_sum)
    )
    attend_sum = to_chips(*attend_sum)
    state_parts = [other(low(d_states[m]), "dp", m) for m in range(1, pieces)]
    encoder_rows = low(d_states[0] + sum(wide(part) for part in state_parts))
    encoder_gradient = swap_planes(encoder_rows)[None]
    square_theirs = other(square_theirs, "core", 1)
    square_sums = [wide(square_mine[m]) + wide(square_theirs[m]) for m in range(pieces)]
    square_parts = [
        other(after(low(square_sums[m]), state_parts), "dp", m) for m in range(1, pieces)
    ]
    square_sum = square_sums[0] + sum(wide(part) for part in square_parts)
    input_gradient, sums1 = single(
        input_back_kernel,
        [flat_low, jax.ShapeDtypeStruct((2, model_width), jnp.float32)],
        [None] * (pieces + 3),
        [],
        own, *parts1, d_middle, raw, gain_rows[0:1],
    )
    input_gradient = trade(trade(after(input_gradient, attend_sum), "z", 0, 0), "dp", 0, 0)[None]
    layer_output = trade(after(layer_first, input_gradient), "dp", 0, 0)[None]

    tail = jnp.concatenate(
        [low(square_sum).reshape(planes, 3 * width, block_rows), cross_sum, attend_sum], axis=1
    )
    tail = sum(
        wide(part if m == 0 else other(part, "z", m))
        for m, part in enumerate(
            lax.dynamic_index_in_dim(tail, plane ^ m, 0, keepdims=False) for m in range(planes)
        )
    )
    square_sum = tail[: 3 * width].reshape(3, width, block_rows)
    cross_sum, attend_sum = tail[3 * width : 5 * width], tail[5 * width :]
    unit_grads = wide(unit_grads)

    def weight_order(turned, count):
        turned = turned.reshape(count, heads, head_size, block_rows).transpose(3, 1, 0, 2)
        return turned.reshape(block_rows, count * width)

    unit_sums = lax.dynamic_update_slice(
        jnp.zeros((planes, cores, pieces, block_units), jnp.float32),
        unit_sums.reshape(planes, 1, 1, block_units),
        (0, core, piece, 0),
    ).reshape(-1)
    small = jnp.concatenate(
        [
            sums2[0],
            sums3[0],
            sums2[1],
            sums3[1],
            sums2[2],
            jnp.sum(wide(d_mixed2), axis=2).transpose(1, 0, 2).reshape(-1),
            place_heads(jnp.sum(wide(d_memory_t[width:]), axis=1)),
            sums3[2],
            jnp.sum(wide(upstream), axis=0),
            unit_sums,
        ]
    )
    last = jnp.stack(
        [
            sums1[0],
            sums1[1],
            place_heads(jnp.sum(wide(d_query1_t), axis=1)),
            place_heads(jnp.sum(wide(d_memory1_t[width:]), axis=1)),
        ]
    )
    small = sum_all(jnp.concatenate([last.reshape(-1), small]).reshape(-1, 128)).reshape(-1)
    last, small = small[: 4 * model_width].reshape(4, model_width), small[4 * model_width :]
    rows = small[: 9 * model_width].reshape(9, model_width)
    return (
        layer_output,
        input_gradient,
        encoder_gradient,
        jnp.concatenate([last[0:1], rows[0:2]]),
        jnp.concatenate([last[1:2], rows[2:4]]),
        weight_order(attend_sum, 3),
        square_sum[0],
        jnp.concatenate([last[2:4], rows[4:5]]),
        square_sum[1].T,
        weight_order(cross_sum, 2),
        square_sum[2],
        rows[5:8],
        unit_grads[:, 0].T,
        small[9 * model_width :],
        unit_grads[:, 1],
        rows[8],
    )


def solution(mesh):
    pieces, sequence = mesh.devices.shape
    planes = Mesh(mesh.devices.reshape(pieces, sequence // 2, 2), ("dp", "z", "core"))
    seq = ("z", "core")
    in_specs = (
        P("dp", seq, None),
        P("dp", seq, None),
        P("dp", None),
        P("dp", None),
        P(),
        P(),
        P("dp", seq),
        P(seq, "dp"),
        P(),
        P("dp", seq),
        P("dp", seq),
        P(seq, "dp"),
        P(),
        P("dp", seq),
        P(),
        P(seq, "dp"),
        P(),
        P("dp", seq, None),
    )
    out_specs = (
        P("dp", seq, None),
        P("dp", seq, None),
        P("dp", seq, None),
        P(),
        P(),
        P("dp", seq),
        P(seq, "dp"),
        P(),
        P("dp", seq),
        P("dp", seq),
        P(seq, "dp"),
        P(),
        P("dp", seq),
        P(),
        P(seq, "dp"),
        P(),
    )
    return jax.shard_map(
        shards, mesh=planes, in_specs=in_specs, out_specs=out_specs, check_vma=False
    )
```

```python
import functools
import math

import jax
import jax.numpy as jnp
from jax import lax
from jax.experimental import pallas as pl
from jax.experimental.pallas import tpu as pltpu
from jax.sharding import Mesh
from jax.sharding import PartitionSpec as P

HEADS = 16

epsilon = 1e-05
masked_score = -1e30
head_width = 64


def head_columns(transposed, heads):
    if heads == 1:
        return transposed
    feature = lax.broadcasted_iota(jnp.int32, transposed.shape, 0) // head_width
    zero = jnp.zeros_like(transposed)
    return jnp.concatenate([jnp.where(feature == h, transposed, zero) for h in range(heads)], axis=1)


def head_rows(block, heads):
    if heads == 1:
        return block
    feature = lax.broadcasted_iota(jnp.int32, block.shape, 1) // head_width
    zero = jnp.zeros_like(block)
    return jnp.concatenate([jnp.where(feature == h, block, zero) for h in range(heads)], axis=0)


def flip(block):
    return jnp.transpose(block.astype(jnp.float32), (1, 0)).astype(block.dtype)


def repeat_heads(row, heads):
    return row if heads == 1 else jnp.concatenate([row] * heads, axis=1)


def project(scalars, mine_ref, theirs_ref, weight_ref, bias_ref, out_refs, width):
    weight = weight_ref[...]
    bias = bias_ref[...]
    for j, source in enumerate((mine_ref, theirs_ref)):
        for m in range(source.shape[0]):
            rows = bias + lax.dot_general(
                source[m], weight, (((1,), (1,)), ((), ())), preferred_element_type=jnp.float32
            )
            rows = rows.astype(jnp.bfloat16)
            for i, out_ref in enumerate(out_refs):
                out_ref[j, m] = rows[:, i * width : (i + 1) * width]


def natural_blocks(scalars, shape, planes):
    cores, pieces, rows = shape[:3]
    part = rows // planes
    for plane in range(planes):
        for core in range(cores):
            slots = [
                ((core ^ scalars[0], piece ^ scalars[1]), plane * part) for piece in range(pieces)
            ]
            if planes == 1:
                for piece in range(pieces):
                    yield (piece * cores + core) * rows, rows, slots[piece : piece + 1]
            else:
                yield (plane * cores + core) * pieces * part, part, slots


def take_rows(ref, part, slots):
    blocks = [ref[slot[0], slot[1], first : first + part] for slot, first in slots]
    return blocks[0] if len(blocks) == 1 else jnp.concatenate(blocks, axis=0)


def query_rows_of(ref, flip_by=0):
    return jnp.concatenate([ref[0, piece ^ flip_by, 0] for piece in range(ref.shape[1])], axis=0)


def put_query_rows(ref, block, flip_by=0):
    part = ref.shape[3]
    for piece in range(ref.shape[1]):
        ref[0, piece ^ flip_by, 0] = block[piece * part : (piece + 1) * part]


def attend_rows(scalars, query, first_ref, last_ref, keys, flipped, heads, key_block):
    step = pl.program_id(0)
    steps = pl.num_programs(0)
    rows = query.shape[0]
    query = query * jnp.asarray(1.0 / math.sqrt(head_width), jnp.bfloat16)
    columns = head_columns(flip(query), heads)
    first = repeat_heads(first_ref[0], heads)
    last = repeat_heads(last_ref[0], heads)

    def one(block, carry):
        peak, total, sums = carry
        start = pl.multiple_of(block * key_block, key_block)
        scores = jnp.dot(keys[pl.ds(start, key_block), :], columns, preferred_element_type=jnp.float32)
        place = start + lax.broadcasted_iota(jnp.int32, scores.shape, 0)
        scores = jnp.where((place >= first) & (place <= last), scores, masked_score)
        newer = jnp.maximum(peak, jnp.max(scores, axis=0, keepdims=True))
        shrink = jnp.exp(peak - newer)
        exponent = jnp.exp(scores - newer)
        total = total * shrink + jnp.sum(exponent, axis=0, keepdims=True)
        low_part = exponent.astype(jnp.bfloat16)
        turned = flipped[block]
        fresh = []
        for h in range(heads):
            part = jnp.dot(
                turned[h * head_width : (h + 1) * head_width],
                low_part[:, h * rows : (h + 1) * rows],
                preferred_element_type=jnp.float32,
            )
            fresh.append(sums[h] * shrink[:, h * rows : (h + 1) * rows] + part)
        return (newer, total, tuple(fresh))

    empty = (
        jnp.full((1, heads * rows), masked_score, jnp.float32),
        jnp.zeros((1, heads * rows), jnp.float32),
        tuple(jnp.zeros((head_width, rows), jnp.float32) for _ in range(heads)),
    )
    peak, total, sums = lax.fori_loop(scalars[2 + step], scalars[2 + steps + step] + 1, one, empty)
    context = jnp.concatenate(
        [sums[h] / total[:, h * rows : (h + 1) * rows] for h in range(heads)], axis=0
    )
    return context, peak + jnp.log(total)


def prepare(scalars, k_ref, v_ref, keys, flipped, key_block, planes):
    for start, part, slots in natural_blocks(scalars, k_ref.shape, planes):
        rows = part * len(slots)
        keys[start : start + rows, :] = take_rows(k_ref, part, slots)
        offset = start % key_block
        flipped[start // key_block, :, offset : offset + rows] = flip(take_rows(v_ref, part, slots))


def finish_forward(context, lse, ctx_ref, keep_ref, lse_ref):
    keep_ref[0] = context
    lse_ref[0] = lse
    put_query_rows(ctx_ref, jnp.transpose(context, (1, 0)).astype(jnp.bfloat16))


def self_forward_kernel(
    scalars, mine_ref, theirs_ref, weight_ref, bias_ref, first_ref, last_ref,
    q_ref, k_ref, v_ref, ctx_ref, keep_ref, lse_ref, keys, flipped,
    *, heads, key_block, planes,
):
    step = pl.program_id(0)
    cores, pieces, rows = q_ref.shape[:3]
    part = rows // planes

    @pl.when(step == 0)
    def _():
        outs = (q_ref, k_ref, v_ref)
        project(scalars, mine_ref, theirs_ref, weight_ref, bias_ref, outs, heads * head_width)
        prepare(scalars, k_ref, v_ref, keys, flipped, key_block, planes)

    core = lax.rem(step, cores) ^ scalars[0]
    here = pl.ds(pl.multiple_of(lax.div(step, cores) * part, part), part)
    query = jnp.concatenate(
        [q_ref[core, piece ^ scalars[1], here, :] for piece in range(pieces)], axis=0
    )
    context, lse = attend_rows(
        scalars, query, first_ref, last_ref, keys, flipped, heads, key_block
    )
    finish_forward(context, lse, ctx_ref, keep_ref, lse_ref)


def cross_forward_kernel(
    scalars, q_ref, mine_ref, theirs_ref, weight_ref, bias_ref, first_ref, last_ref,
    k_ref, v_ref, ctx_ref, keep_ref, lse_ref, keys, flipped,
    *, heads, key_block,
):
    @pl.when(pl.program_id(0) == 0)
    def _():
        outs = (k_ref, v_ref)
        project(scalars, mine_ref, theirs_ref, weight_ref, bias_ref, outs, heads * head_width)
        prepare(scalars, k_ref, v_ref, keys, flipped, key_block, 1)

    context, lse = attend_rows(
        scalars, query_rows_of(q_ref), first_ref, last_ref, keys, flipped, heads, key_block
    )
    finish_forward(context, lse, ctx_ref, keep_ref, lse_ref)


def backward_kernel(
    scalars, q_ref, k_ref, v_ref, dc_ref, keep_ref, lse_ref, first_ref, last_ref,
    *rest, heads, key_block, planes, near,
):
    if near:
        weight_ref, dmine_ref, dtheirs_ref, *rest = rest
        dq_ref, dqt_ref, dkv_ref, dkvt_ref, keys, values, flipped, dkeys, dvalues = rest
    else:
        dq_ref, dkv_ref, dkvt_ref, keys, values, flipped, dkeys, dvalues = rest
    step = pl.program_id(0)
    steps = pl.num_programs(0)
    width = heads * head_width
    scaling = 1.0 / math.sqrt(head_width)

    @pl.when(step == 0)
    def _():
        prepare(scalars, k_ref, k_ref, keys, flipped, key_block, planes)
        for start, part, slots in natural_blocks(scalars, v_ref.shape, planes):
            values[start : start + part * len(slots), :] = take_rows(v_ref, part, slots)
        dkeys[...] = jnp.zeros_like(dkeys)
        dvalues[...] = jnp.zeros_like(dvalues)

    flip_by = scalars[1] if near else 0
    query = query_rows_of(q_ref, flip_by) * jnp.asarray(scaling, jnp.bfloat16)
    rows = query.shape[0]
    grad = query_rows_of(dc_ref)
    turned_grad = flip(grad)
    query_columns = head_columns(flip(query), heads)
    grad_columns = head_columns(turned_grad, heads)
    query_rows = head_rows(query, heads)
    grad_rows = head_rows(grad, heads)
    dots_kept = turned_grad.astype(jnp.float32) * keep_ref[0]
    center = jnp.concatenate(
        [
            jnp.sum(dots_kept[h * head_width : (h + 1) * head_width], axis=0, keepdims=True)
            for h in range(heads)
        ],
        axis=1,
    )
    first = repeat_heads(first_ref[0], heads)
    last = repeat_heads(last_ref[0], heads)
    lse = lse_ref[0]

    def one(block, sums):
        start = pl.multiple_of(block * key_block, key_block)
        here = pl.ds(start, key_block)
        scores = jnp.dot(keys[here, :], query_columns, preferred_element_type=jnp.float32)
        place = start + lax.broadcasted_iota(jnp.int32, scores.shape, 0)
        scores = jnp.where((place >= first) & (place <= last), scores, masked_score)
        weights = jnp.exp(scores - lse)
        dots = jnp.dot(values[here, :], grad_columns, preferred_element_type=jnp.float32)
        dscore = (weights * (dots - center)).astype(jnp.bfloat16)
        dvalues[here, :] += jnp.dot(
            weights.astype(jnp.bfloat16), grad_rows, preferred_element_type=jnp.float32
        )
        dkeys[here, :] += jnp.dot(dscore, query_rows, preferred_element_type=jnp.float32)
        turned = flipped[block]
        return tuple(
            sums[h]
            + jnp.dot(
                turned[h * head_width : (h + 1) * head_width],
                dscore[:, h * rows : (h + 1) * rows],
                preferred_element_type=jnp.float32,
            )
            for h in range(heads)
        )

    empty = tuple(jnp.zeros((head_width, rows), jnp.float32) for _ in range(heads))
    sums = lax.fori_loop(scalars[2 + step], scalars[2 + steps + step] + 1, one, empty)
    dquery = jnp.concatenate(sums, axis=0) * scaling
    dquery = jnp.transpose(dquery, (1, 0)).astype(jnp.bfloat16)
    if near:
        core = lax.rem(step, dq_ref.shape[0]) ^ scalars[0]
        plane = lax.div(step, dq_ref.shape[0])
        part = dq_ref.shape[3]
        for piece in range(dq_ref.shape[1]):
            dq_ref[core, piece ^ flip_by, plane] = dquery[piece * part : (piece + 1) * part]
    else:
        put_query_rows(dq_ref, dquery)

    @pl.when(step == steps - 1)
    def _():
        cores, pieces, key_rows = k_ref.shape[:3]
        for start, part, slots in natural_blocks(scalars, k_ref.shape, planes):
            for i, (slot, first) in enumerate(slots):
                here = slice(start + i * part, start + (i + 1) * part)
                for column, total in ((0, dkeys), (width, dvalues)):
                    dkv_ref[slot[0], slot[1], first : first + part, column : column + width] = (
                        total[here, :].astype(jnp.bfloat16)
                    )
        for j in reversed(range(cores)):
            for m in range(pieces):
                if near:
                    rows_grad = jnp.dot(
                        dq_ref[j, m].reshape(key_rows, width),
                        weight_ref[:width],
                        preferred_element_type=jnp.float32,
                    ) + jnp.dot(
                        dkv_ref[j, m], weight_ref[width:], preferred_element_type=jnp.float32
                    )
                    if j == 0:
                        dmine_ref[m] = rows_grad
                    else:
                        dtheirs_ref[m] = rows_grad.astype(jnp.bfloat16)
                place = (j * pieces + m) * key_rows
                dkvt_ref[:, place : place + key_rows] = flip(dkv_ref[j, m])
                if near:
                    block = dq_ref[j, m].reshape(key_rows, width)
                    dqt_ref[:, place : place + key_rows] = flip(block)


def whole_spec(shape, index=None):
    index = (0,) * len(shape) if index is None else index
    return pl.BlockSpec(shape, lambda step, scalars: index)


def step_spec(shape):
    return pl.BlockSpec((1,) + shape[1:], lambda step, scalars: (step, 0, 0))


def member_spec(shape, near):
    cores, pieces = shape[:2]

    def place(step, scalars):
        core = lax.rem(step, cores)
        return (core ^ scalars[0] if near else core, 0, lax.div(step, cores), 0, 0)

    return pl.BlockSpec((1, pieces, 1) + shape[3:], place)


def forward_outputs(shape):
    cores, pieces, planes, rows, width = shape
    steps = cores * planes
    heads = width // head_width
    shapes = [
        jax.ShapeDtypeStruct(shape, jnp.bfloat16),
        jax.ShapeDtypeStruct((steps, width, pieces * rows), jnp.float32),
        jax.ShapeDtypeStruct((steps, 1, heads * pieces * rows), jnp.float32),
    ]
    specs = [member_spec(shape, False), step_spec(shapes[1].shape), step_spec(shapes[2].shape)]
    return shapes, specs


def cost(microseconds):
    return pl.CostEstimate(
        flops=int(microseconds * 1.1e9), bytes_accessed=1 << 20, transcendentals=0
    )


def params(mebibytes=56):
    return pltpu.CompilerParams(vmem_limit_bytes=mebibytes * 2**20)


def self_forward(scalars, mine, theirs, planes, weight, bias, first, last):
    pieces, rows, model_width = mine.shape
    width = weight.shape[0] // 3
    shape = (2, pieces, rows, width)
    steps = 2 * planes
    key_count = 2 * pieces * rows
    key_block = min(256, key_count)
    shapes, specs = forward_outputs((2, pieces, planes, rows // planes, width))
    full = jax.ShapeDtypeStruct(shape, jnp.bfloat16)
    return pl.pallas_call(
        functools.partial(
            self_forward_kernel, heads=width // head_width, key_block=key_block, planes=planes
        ),
        grid_spec=pltpu.PrefetchScalarGridSpec(
            num_scalar_prefetch=1,
            grid=(steps,),
            in_specs=[
                whole_spec(mine.shape),
                whole_spec(theirs.shape),
                whole_spec(weight.shape),
                whole_spec(bias.shape),
                step_spec(first.shape),
                step_spec(last.shape),
            ],
            out_specs=[whole_spec(shape)] * 3 + specs,
            scratch_shapes=[
                pltpu.VMEM((key_count, width), jnp.bfloat16),
                pltpu.VMEM((key_count // key_block, width, key_block), jnp.bfloat16),
            ],
        ),
        out_shape=[full] * 3 + shapes,
        compiler_params=params(),
        cost_estimate=cost(16),
    )(scalars, mine, theirs, weight, bias, first, last)


def cross_forward(scalars, queries, mine, theirs, weight, bias, first, last):
    cores, pieces, planes, rows, width = queries.shape
    state_rows = mine.shape[1]
    steps = cores * planes
    key_count = cores * pieces * state_rows
    key_block = min(256, key_count)
    shapes, specs = forward_outputs(queries.shape)
    key_shape = (cores, pieces, state_rows, width)
    full = jax.ShapeDtypeStruct(key_shape, jnp.bfloat16)
    return pl.pallas_call(
        functools.partial(cross_forward_kernel, heads=width // head_width, key_block=key_block),
        grid_spec=pltpu.PrefetchScalarGridSpec(
            num_scalar_prefetch=1,
            grid=(steps,),
            in_specs=[
                member_spec(queries.shape, False),
                whole_spec(mine.shape),
                whole_spec(theirs.shape),
                whole_spec(weight.shape),
                whole_spec(bias.shape),
                step_spec(first.shape),
                step_spec(last.shape),
            ],
            out_specs=[whole_spec(key_shape)] * 2 + specs,
            scratch_shapes=[
                pltpu.VMEM((key_count, width), jnp.bfloat16),
                pltpu.VMEM((key_count // key_block, width, key_block), jnp.bfloat16),
            ],
        ),
        out_shape=[full] * 2 + shapes,
        compiler_params=params(),
        cost_estimate=cost(11),
    )(scalars, queries, mine, theirs, weight, bias, first, last)


def attend_back(scalars, queries, key_rows, values, grad, kept, lse, first, last, weight=None):
    near = weight is not None
    cores, pieces, planes, rows, width = queries.shape
    steps = cores * planes
    key_shape = key_rows.shape
    key_count = cores * pieces * key_shape[2]
    key_block = min(256, key_count)
    dq_shape = jax.ShapeDtypeStruct(queries.shape, jnp.bfloat16)
    if near:
        row_shape = (pieces, planes * rows, weight.shape[1])
        dq_shapes = [
            jax.ShapeDtypeStruct(row_shape, jnp.float32),
            jax.ShapeDtypeStruct(row_shape, jnp.bfloat16),
            dq_shape,
            jax.ShapeDtypeStruct((width, key_count), jnp.bfloat16),
        ]
        dq_specs = [whole_spec(shape.shape) for shape in dq_shapes]
    else:
        dq_shapes, dq_specs = [dq_shape], [member_spec(queries.shape, False)]
    return pl.pallas_call(
        functools.partial(
            backward_kernel,
            heads=width // head_width,
            key_block=key_block,
            planes=planes if near else 1,
            near=near,
        ),
        grid_spec=pltpu.PrefetchScalarGridSpec(
            num_scalar_prefetch=1,
            grid=(steps,),
            in_specs=[
                member_spec(queries.shape, near),
                whole_spec(key_shape),
                whole_spec(key_shape),
                member_spec(grad.shape, False),
                step_spec(kept.shape),
                step_spec(lse.shape),
                step_spec(first.shape),
                step_spec(last.shape),
            ]
            + ([whole_spec(weight.shape)] if near else []),
            out_specs=dq_specs
            + [whole_spec(key_shape[:3] + (2 * width,)), whole_spec((2 * width, key_count))],
            scratch_shapes=[
                pltpu.VMEM((key_count, width), jnp.bfloat16),
                pltpu.VMEM((key_count, width), jnp.bfloat16),
                pltpu.VMEM((key_count // key_block, width, key_block), jnp.bfloat16),
                pltpu.VMEM((key_count, width), jnp.float32),
                pltpu.VMEM((key_count, width), jnp.float32),
            ],
        ),
        out_shape=dq_shapes
        + [
            jax.ShapeDtypeStruct(key_shape[:3] + (2 * width,), jnp.bfloat16),
            jax.ShapeDtypeStruct((2 * width, key_count), jnp.bfloat16),
        ],
        compiler_params=params(),
        cost_estimate=cost(12),
    )(
        scalars, queries, key_rows, values, grad, kept, lse, first, last,
        *([weight] if near else []),
    )


def single(kernel, out_shape, in_specs, scratch, *args):
    return pl.pallas_call(
        kernel,
        grid_spec=pltpu.PrefetchScalarGridSpec(
            num_scalar_prefetch=1,
            grid=(1,),
            in_specs=[
                whole_spec(value.shape) if spec is None else spec
                for spec, value in zip(in_specs, args[1:])
            ],
            out_specs=[whole_spec(value.shape) for value in out_shape],
            scratch_shapes=scratch,
        ),
        out_shape=out_shape,
        compiler_params=params(),
        cost_estimate=cost(4),
    )(*args)


def kind_spec(array, kind):
    shape = (array.shape[0], array.shape[1], 1) + array.shape[3:]
    return whole_spec(shape, (0, 0, kind, 0, 0))


def square_block(ref, m):
    block = ref[m, :, 0]
    return block.reshape(block.shape[0] * block.shape[1], block.shape[2])


def heads_of(ref, core):
    return jnp.concatenate([ref[core, piece] for piece in range(ref.shape[1])], axis=1)


def near_span(scalars, m, size):
    return pl.ds(pl.multiple_of((scalars[1] ^ m) * size, size), size)


def heads_to_model(scalars, heads_ref, mine_ref, theirs_ref, sums):
    mine, theirs = heads_of(heads_ref, scalars[0]), heads_of(heads_ref, 1 ^ scalars[0])
    size = mine_ref.shape[4]
    for m in range(mine_ref.shape[0]):
        sums[:, near_span(scalars, m, size)] = jnp.dot(
            mine, square_block(mine_ref, m), preferred_element_type=jnp.float32
        ) + jnp.dot(theirs, square_block(theirs_ref, m), preferred_element_type=jnp.float32)


def model_to_heads(scalars, rows_ref, mine_ref, theirs_ref, heads_ref, bias_ref=None):
    size = mine_ref.shape[4]
    pieces, width = heads_ref.shape[1], heads_ref.shape[3]
    for j, weight_ref in enumerate((mine_ref, theirs_ref)):
        total = 0.0
        for m in range(weight_ref.shape[0]):
            total = total + lax.dot_general(
                rows_ref[:, near_span(scalars, m, size)],
                square_block(weight_ref, m),
                (((1,), (1,)), ((), ())),
                preferred_element_type=jnp.float32,
            )
        core = scalars[0] ^ j
        for piece in range(pieces):
            block = total[:, piece * width : (piece + 1) * width]
            if bias_ref is not None:
                block = block + bias_ref[core, piece]
            heads_ref[core, piece] = block.astype(jnp.bfloat16)


def normal_parts(values):
    center = values - jnp.mean(values, axis=-1, keepdims=True)
    spread = jnp.mean(center * center, axis=-1, keepdims=True)
    scale = lax.rsqrt(spread + epsilon)
    return center * scale, scale


def norm_back(values, gain, dn):
    normal, scale = normal_parts(values)
    e = dn * gain
    dv = scale * (
        e
        - jnp.mean(e, axis=-1, keepdims=True)
        - normal * jnp.mean(e * normal, axis=-1, keepdims=True)
    )
    return (
        dv,
        jnp.sum(dn * normal, axis=0, keepdims=True),
        jnp.sum(dn, axis=0, keepdims=True),
    )


def middle_kernel(
    scalars, heads_ref, omine_ref, otheirs_ref, resid_ref, rows_ref, qmine_ref, qtheirs_ref,
    qbias_ref, sum_ref, norm_ref, q_ref,
):
    heads_to_model(scalars, heads_ref, omine_ref, otheirs_ref, sum_ref)
    total = sum_ref[...] + resid_ref[...].astype(jnp.float32) + rows_ref[0:1]
    sum_ref[...] = total
    normal, _ = normal_parts(total)
    norm_ref[...] = (normal * rows_ref[1:2] + rows_ref[2:3]).astype(jnp.bfloat16)
    model_to_heads(scalars, norm_ref, qmine_ref, qtheirs_ref, q_ref, qbias_ref)


def later_kernel(
    scalars, heads_ref, omine_ref, otheirs_ref, resid_ref, rows_ref, sum_ref, norm_ref
):
    heads_to_model(scalars, heads_ref, omine_ref, otheirs_ref, sum_ref)
    total = sum_ref[...] + resid_ref[...] + rows_ref[0:1]
    sum_ref[...] = total
    normal, _ = normal_parts(total)
    norm_ref[...] = (normal * rows_ref[1:2] + rows_ref[2:3]).astype(jnp.bfloat16)


def finish_back(scalars, values_ref, rows_ref, dn, upper, mine_ref, theirs_ref, d_ref, low_ref, heads_ref, sums_ref):
    dv, dg, db = norm_back(values_ref[...], rows_ref[0:1], dn)
    total = upper + dv
    d_ref[...] = total
    low_total = total.astype(jnp.bfloat16)
    low_ref[...] = low_total
    sums_ref[0:1] = dg
    sums_ref[1:2] = db
    sums_ref[2:3] = jnp.sum(low_total.astype(jnp.float32), axis=0, keepdims=True)
    model_to_heads(scalars, low_ref, mine_ref, theirs_ref, heads_ref)


def later_back_kernel(scalars, *refs):
    parts, (up_ref, values_ref, rows_ref, mine_ref, theirs_ref) = refs[:-9], refs[-9:-4]
    dn = parts[0][...].reshape(up_ref.shape)
    for part in parts[1:]:
        dn = dn + part[...].reshape(up_ref.shape).astype(jnp.float32)
    upper = up_ref[...].astype(jnp.float32)
    finish_back(scalars, values_ref, rows_ref, dn, upper, mine_ref, theirs_ref, *refs[-4:])


def middle_back_kernel(
    scalars, heads_ref, qmine_ref, qtheirs_ref, upper_ref, values_ref, rows_ref, mine_ref,
    theirs_ref, d_ref, low_ref, dheads_ref, sums_ref, work,
):
    heads_to_model(scalars, heads_ref, qmine_ref, qtheirs_ref, work)
    finish_back(
        scalars, values_ref, rows_ref, work[...], upper_ref[...], mine_ref, theirs_ref,
        d_ref, low_ref, dheads_ref, sums_ref,
    )


def input_back_kernel(scalars, *refs):
    parts, (upper_ref, values_ref, rows_ref, out_ref, sums_ref) = refs[:-5], refs[-5:]
    dn = parts[0][...].reshape(upper_ref.shape)
    for part in parts[1:]:
        dn = dn + part[...].reshape(upper_ref.shape).astype(jnp.float32)
    dv, dg, db = norm_back(values_ref[...].astype(jnp.float32), rows_ref[0:1], dn)
    out_ref[...] = (upper_ref[...] + dv).astype(jnp.bfloat16)
    sums_ref[0:1] = dg
    sums_ref[1:2] = db


def square_grad_kernel(scalars, *refs):
    kinds = (len(refs) - 2) // 2
    mine_ref, theirs_ref = refs[-2:]
    size = mine_ref.shape[4]
    for kind in range(kinds):
        heads_ref, rows_ref = refs[2 * kind], refs[2 * kind + 1]
        for j, out_ref in enumerate((mine_ref, theirs_ref)):
            for piece in range(heads_ref.shape[1]):
                turned = flip(heads_ref[scalars[0] ^ j, piece])
                for m in range(out_ref.shape[0]):
                    out_ref[m, piece, kind] = jnp.dot(
                        turned,
                        rows_ref[:, near_span(scalars, m, size)],
                        preferred_element_type=jnp.float32,
                    ).astype(out_ref.dtype)


def gelu_parts(u):
    root = math.sqrt(2.0 / math.pi)
    square = u * u
    bent = jnp.tanh(root * (u + 0.044715 * (square * u)))
    half = 0.5 * (1.0 + bent)
    slope = half + 0.5 * u * (1.0 - bent * bent) * (root * (1.0 + 3.0 * 0.044715 * square))
    return u * half, slope


def units_kernel(
    scalars, mine_ref, theirs_ref, upmine_ref, uptheirs_ref, expand_ref, shrink_ref, bias_ref,
    active_ref, dhidden_ref, dmine_ref, dtheirs_ref, outmine_ref, outtheirs_ref, half_count,
):
    step = pl.program_id(0)
    expand, shrink = expand_ref[...], shrink_ref[...]
    against_last = (((1,), (1,)), ((), ()))

    def one(rows, up):
        hidden = lax.dot_general(rows, expand, against_last, preferred_element_type=jnp.float32)
        dactive = lax.dot_general(up, shrink, against_last, preferred_element_type=jnp.float32)
        active, slope = gelu_parts(hidden + bias_ref[...])
        dhidden = (dactive * slope).astype(jnp.bfloat16)
        active = active.astype(jnp.bfloat16)
        active_ref[0, 0] = active
        dhidden_ref[0, 0] = dhidden
        return (
            jnp.dot(dhidden, expand, preferred_element_type=jnp.float32),
            jnp.dot(active, shrink, preferred_element_type=jnp.float32),
        )

    @pl.when(step < half_count)
    def _():
        dthree, out = one(theirs_ref[0], uptheirs_ref[0])
        dtheirs_ref[0] = dthree.astype(jnp.bfloat16)
        outtheirs_ref[0] = out.astype(jnp.bfloat16)

    @pl.when(step >= half_count)
    def _():
        dthree, out = one(mine_ref[0], upmine_ref[0])
        dmine_ref[0] = dthree
        outmine_ref[0] = out


def units_group(scalars, mine, theirs, ups, start, expand_t, shrink_w, bias):
    count, rows, model_width = mine.shape
    units = expand_t.shape[0]

    def piece_spec(own, offset=0):
        if own:
            place = lambda step, scalars: (jnp.maximum(step - count, 0) + offset, 0, 0)
        else:
            place = lambda step, scalars: (jnp.minimum(step, count - 1) + offset, 0, 0)
        return pl.BlockSpec((1, rows, model_width), place)

    def table_place(step, scalars):
        return (1 - lax.div(step, count), lax.rem(step, count), 0, 0)

    table = jax.ShapeDtypeStruct((2, count, rows, units), jnp.bfloat16)
    table_spec = pl.BlockSpec((1, 1, rows, units), table_place)
    return pl.pallas_call(
        functools.partial(units_kernel, half_count=count),
        grid_spec=pltpu.PrefetchScalarGridSpec(
            num_scalar_prefetch=1,
            grid=(2 * count,),
            in_specs=[
                piece_spec(True),
                piece_spec(False),
                piece_spec(True, start),
                piece_spec(False, start),
                whole_spec(expand_t.shape),
                whole_spec(shrink_w.shape),
                whole_spec(bias.shape),
            ],
            out_specs=[table_spec, table_spec] + [piece_spec(True), piece_spec(False)] * 2,
        ),
        out_shape=[
            table,
            table,
            jax.ShapeDtypeStruct(mine.shape, jnp.float32),
            jax.ShapeDtypeStruct(mine.shape, jnp.bfloat16),
        ]
        + [
            jax.ShapeDtypeStruct(mine.shape, jnp.float32),
            jax.ShapeDtypeStruct(mine.shape, jnp.bfloat16),
        ],
        compiler_params=params(32),
        cost_estimate=cost(6.5 * count),
    )(scalars, mine, theirs, *ups, expand_t, shrink_w, bias)


def unit_gradients_kernel(scalars, *refs, counts):
    dhidden_refs, active_refs = refs[0:2], refs[2:4]
    row_refs, up_refs = (refs[4:6], refs[6:8]), refs[8:10]
    out_ref, expand_sum, shrink_sum = refs[10:]
    step = pl.program_id(0)
    width = expand_sum.shape[1]

    @pl.when(step == 0)
    def _():
        expand_sum[...] = jnp.zeros_like(expand_sum)
        shrink_sum[...] = jnp.zeros_like(shrink_sum)

    def add(group, core):
        for table_ref, rows_ref, total in (
            (dhidden_refs[group], row_refs[group][core], expand_sum),
            (active_refs[group], up_refs[core], shrink_sum),
        ):
            total[...] += lax.dot_general(
                table_ref[0, 0],
                rows_ref[0],
                (((0,), (0,)), ((), ())),
                preferred_element_type=jnp.float32,
            )

    first = 0
    for group, count in enumerate(counts):
        for core in range(2):
            @pl.when((step >= first) & (step < first + count))
            def _(group=group, core=core):
                add(group, core)

            first += count

    @pl.when(step == pl.num_programs(0) - 1)
    def _():
        out_ref[:, :width] = expand_sum[...].astype(jnp.bfloat16)
        out_ref[:, width:] = shrink_sum[...].astype(jnp.bfloat16)


def unit_gradients(scalars, dhiddens, actives, rows, ups):
    counts = [table.shape[1] for table in actives]
    _, _, tokens, units = actives[0].shape
    model_width = ups[0].shape[2]
    starts = [2 * sum(counts[:i]) for i in range(len(counts))]

    def table_spec(group):
        count, start = counts[group], starts[group]

        def place(step, scalars):
            here = jnp.clip(step - start, 0, 2 * count - 1)
            return (lax.div(here, count), lax.rem(here, count), 0, 0)

        return pl.BlockSpec((1, 1, tokens, units), place)

    def row_place(group, core):
        count, start = counts[group], starts[group] + core * counts[group]
        return pl.BlockSpec(
            (1, tokens, model_width),
            lambda step, scalars: (jnp.clip(step - start, 0, count - 1), 0, 0),
        )

    def up_place(core):
        def place(step, scalars):
            here = 0
            for i in range(len(counts)):
                inside = jnp.clip(step - starts[i] - core * counts[i], 0, counts[i] - 1)
                begun = (step >= starts[i] + core * counts[i]).astype(jnp.int32)
                here = jnp.where(begun == 1, sum(counts[:i]) + inside, here)
            return (here, 0, 0)

        return pl.BlockSpec((1, tokens, model_width), place)

    return pl.pallas_call(
        functools.partial(unit_gradients_kernel, counts=counts),
        grid_spec=pltpu.PrefetchScalarGridSpec(
            num_scalar_prefetch=1,
            grid=(2 * sum(counts),),
            in_specs=[table_spec(0), table_spec(1), table_spec(0), table_spec(1)]
            + [row_place(0, 0), row_place(0, 1), row_place(1, 0), row_place(1, 1)]
            + [up_place(0), up_place(1)],
            out_specs=whole_spec((units, 2 * model_width)),
            scratch_shapes=[pltpu.VMEM((units, model_width), jnp.float32)] * 2,
        ),
        out_shape=jax.ShapeDtypeStruct((units, 2 * model_width), jnp.bfloat16),
        compiler_params=params(),
        cost_estimate=cost(12),
    )(scalars, *dhiddens, *actives, *rows[0], *rows[1], *ups)


def layer_norm(values, gain_row, shift_row):
    center = values - jnp.mean(values, axis=-1, keepdims=True)
    spread = jnp.mean(center * center, axis=-1, keepdims=True)
    return center * lax.rsqrt(spread + epsilon) * gain_row + shift_row


def inner_rows(former, latter):
    return lax.dot_general(
        former, latter, (((0,), (0,)), ((), ())), preferred_element_type=jnp.float32
    )


def against(former, latter):
    return lax.dot_general(
        former, latter, (((1,), (1,)), ((), ())), preferred_element_type=jnp.float32
    )


def product(former, latter):
    return jnp.dot(former, latter, preferred_element_type=jnp.float32)


def low(values):
    return values.astype(jnp.bfloat16)


def wide(values):
    return values.astype(jnp.float32)


def other(values, axis, shift):
    count = lax.axis_size(axis)
    return lax.ppermute(values, axis, [(i, i ^ shift) for i in range(count)])


def trade(values, axis, split, concat):
    return lax.all_to_all(values, axis, split_axis=split, concat_axis=concat, tiled=True)


def after(values, *earlier):
    return lax.optimization_barrier((values, earlier))[0]


PLANE = ("core", "dp")


def chips_gather(block, axis="dp"):
    return [block] + [other(block, axis, m) for m in range(1, lax.axis_size(axis))]


def plane_gather(block):
    mine = jnp.stack(chips_gather(block))
    return mine, other(mine, "core", 1)


def plane_reduce(mine, theirs):
    sums = mine + wide(other(low(theirs), "core", 1))
    total = sums[0]
    for m in range(1, sums.shape[0]):
        total = total + wide(other(low(sums[m]), "dp", m))
    return total


def swap_planes(values, hop=0):
    pieces, planes, cores = (lax.axis_size(axis) for axis in ("dp", "z", "core"))
    pairs = [
        (((d ^ hop) * planes + z) * cores + c, (z * planes + d) * cores + c)
        for d in range(pieces)
        for z in range(planes)
        for c in range(cores)
    ]
    return lax.ppermute(values, ("dp", "z", "core"), pairs)


def put_blocks(blocks, axis, dimension):
    size = blocks[0].shape[dimension]
    shape = list(blocks[0].shape)
    shape[dimension] = size * len(blocks)
    whole = jnp.zeros(shape, blocks[0].dtype)
    for m, block in enumerate(blocks):
        start = [0] * len(shape)
        start[dimension] = (lax.axis_index(axis) ^ m) * size
        whole = lax.dynamic_update_slice(whole, block, start)
    return whole


def sum_all(values):
    for axis in ("core", "dp", "z"):
        shift = 1
        while shift < lax.axis_size(axis):
            values = values + other(values, axis, shift)
            shift *= 2
    return values


def document_edges(ids, memory_ids, steps):
    documents = jnp.arange(4, dtype=jnp.int32)
    starts = jnp.sum((memory_ids[None] < documents[:, None]).astype(jnp.int32), axis=1)
    ends = jnp.sum((memory_ids[None] <= documents[:, None]).astype(jnp.int32), axis=1) - 1
    match = ids[None] == documents[:, None]
    first = jnp.sum(jnp.where(match, starts[:, None], 0), axis=0)
    last = jnp.sum(jnp.where(match, ends[:, None], 0), axis=0)
    return (first.reshape(steps, 1, -1), last.reshape(steps, 1, -1))


def shards(
    inputs,
    encoder_states,
    segment_ids,
    encoder_ids,
    norm_gains,
    norm_shifts,
    attend_weights,
    attend_output,
    attend_biases,
    cross_query,
    cross_memory,
    cross_output,
    cross_biases,
    expand_weight,
    expand_bias,
    shrink_weight,
    shrink_bias,
    output_cotangent,
):
    pieces, planes, cores = lax.axis_size("dp"), lax.axis_size("z"), lax.axis_size("core")
    piece, plane, core = lax.axis_index("dp"), lax.axis_index("z"), lax.axis_index("core")
    members = pieces * cores
    member = core * pieces + piece
    row_count, model_width = inputs.shape[1:]
    memory_rows = encoder_states.shape[1]
    pack_rows, pack_memory = segment_ids.shape[1], encoder_ids.shape[1]
    heads = HEADS // members
    head_size = model_width // HEADS
    width = heads * head_size
    steps = planes * cores
    unit_count = expand_weight.shape[1]
    block_units = unit_count // pieces
    block_rows = model_width // pieces

    all_ids = swap_planes(jnp.concatenate([segment_ids[0], encoder_ids[0]]))
    pack_ids, memory_ids = all_ids[:pack_rows], all_ids[pack_rows:]
    attend_at = lax.all_gather(attend_weights.T, "z", axis=0, tiled=True)
    raw = trade(after(trade(inputs[0], "dp", 0, 0), attend_at), "z", 0, 0)

    def columns_of(weight, count):
        weight = weight.reshape(pieces, heads, count, head_size, block_rows)
        return weight.transpose(2, 1, 3, 0, 4).reshape(count * width, model_width)

    near_w = jnp.concatenate([cross_memory.T, attend_output, cross_query.T, cross_output])
    near_w = lax.all_gather(after(near_w, attend_at), "z", axis=0, tiled=True)
    near_w = near_w.reshape(planes, 5 * width, block_rows)
    attend_w = trade(after(attend_at, raw), "dp", 0, 0).reshape(pieces, 3 * width, block_rows)
    upstream = trade(after(output_cotangent[0], attend_w), "dp", 0, 0)
    squares = near_w[:, 2 * width :].reshape(planes, 3, width, block_rows)
    cross_kv = near_w[:, : 2 * width].reshape(planes * 2 * width, block_rows)
    unit_w = jnp.stack([expand_weight.T, shrink_weight], axis=1)
    unit_parts = []
    for m in range(pieces):
        part = lax.dynamic_slice_in_dim(unit_w, (piece ^ m) * block_units, block_units, 0)
        unit_parts.append(part if m == 0 else other(part, "dp", m))
    unit_w = put_blocks(unit_parts, "dp", 2).reshape(block_units, 2 * model_width)
    states = swap_planes(after(encoder_states[0], raw))
    whole_units = lax.all_gather(after(unit_w, near_w), "z", axis=0, tiled=True)
    expand_t, shrink_w = whole_units[:, :model_width], whole_units[:, model_width:]
    attend_w = columns_of(attend_w, 3)

    own = jnp.stack([core, piece]).astype(jnp.int32)
    key_block = min(256, pack_rows)
    self_first, _ = document_edges(pack_ids, pack_ids, steps)
    self_last = jnp.arange(pack_rows, dtype=jnp.int32).reshape(steps, 1, -1)
    self_scalars = jnp.concatenate(
        [own, self_first[:, 0, 0] // key_block, self_last[:, 0, -1] // key_block]
    )
    cross_first, cross_last = document_edges(pack_ids, memory_ids, steps)
    key_block = min(256, pack_memory)
    cross_scalars = jnp.concatenate(
        [own, cross_first[:, 0, 0] // key_block, cross_last[:, 0, -1] // key_block]
    )

    gain_rows, shift_rows = wide(norm_gains), wide(norm_shifts)
    bias_self, bias_cross = wide(attend_biases), wide(cross_biases)

    def of_heads(row):
        return lax.dynamic_slice_in_dim(row, (piece * cores + core) * width, width, 0)

    def place_heads(row):
        return lax.dynamic_update_slice(
            jnp.zeros((model_width,), jnp.float32), row, ((piece * cores + core) * width,)
        )

    zero_heads = jnp.zeros((width,), jnp.float32)
    packed_bias = jnp.concatenate([of_heads(bias_self[0]), zero_heads, of_heads(bias_self[1])])
    memory_bias = jnp.concatenate([zero_heads, of_heads(bias_cross[1])])
    query_bias = bias_cross[0].reshape(pieces, cores, 1, width).transpose(1, 0, 2, 3)
    token_shape = (cores, pieces, row_count, width)
    part_shape = (cores, pieces, planes, row_count // planes, width)
    flat_shape = (row_count, model_width)
    flat_float = jax.ShapeDtypeStruct(flat_shape, jnp.float32)
    flat_low = jax.ShapeDtypeStruct(flat_shape, jnp.bfloat16)
    head_low = jax.ShapeDtypeStruct(token_shape, jnp.bfloat16)
    three_rows = jax.ShapeDtypeStruct((3, model_width), jnp.float32)

    def exchange(values):
        return trade(values.reshape(pieces * cores * row_count, width), PLANE, 0, 0).reshape(
            token_shape
        )

    low_one = low(layer_norm(wide(raw), gain_rows[0], shift_rows[0]))
    mine = jnp.stack(chips_gather(after(low_one, unit_w)))
    mine, states = after((mine, states), attend_w, near_w)
    squares = after(squares, mine)
    upstream = trade(upstream, "z", 0, 0)
    state_parts = chips_gather(after(states, mine))
    squares = after(squares, state_parts)
    ones = (mine, other(mine, "core", 1))
    square_parts = chips_gather(squares)
    query1, key1, value1, context1, kept1, lse1 = self_forward(
        self_scalars, *ones, planes, attend_w, packed_bias[None], self_first, self_last
    )
    context1, square_parts = after((context1, square_parts), upstream)
    squares = jnp.stack(square_parts)
    squares = (squares, other(squares, "core", 1))
    mixed1 = exchange(context1)
    cross_kv = trade(after(cross_kv, mixed1), "dp", 0, 0).reshape(pieces, 2 * width, block_rows)
    cross_kv = columns_of(cross_kv, 2)
    middle, low_two, query2 = single(
        middle_kernel,
        [flat_float, flat_low, head_low],
        [None, kind_spec(squares[0], 0), kind_spec(squares[1], 0), None, None]
        + [kind_spec(squares[0], 1), kind_spec(squares[1], 1), None],
        [],
        own, mixed1, *squares, raw,
        jnp.stack([bias_self[2], gain_rows[1], shift_rows[1]]),
        *squares, query_bias,
    )

    all_states = jnp.stack(state_parts)
    all_states = (all_states, other(after(all_states, mixed1), "core", 1))
    query2 = exchange(query2)
    query2 = query2.reshape(part_shape)
    key2, value2, context2, kept2, lse2 = cross_forward(
        cross_scalars, query2, *all_states, cross_kv, memory_bias[None],
        cross_first, cross_last,
    )
    ups = chips_gather(after(upstream, query2))
    context2, ups = after((context2, ups))
    ups = jnp.stack(ups)
    all_ups = (ups, other(ups, "core", 1))
    context2 = after(context2, whole_units)
    mixed2 = exchange(context2)
    later, low_three = single(
        later_kernel,
        [flat_float, flat_low],
        [None, kind_spec(squares[0], 2), kind_spec(squares[1], 2), None, None],
        [],
        own, mixed2, *squares, middle,
        jnp.stack([bias_cross[2], gain_rows[2], shift_rows[2]]),
    )

    bias_units = wide(expand_bias).reshape(planes, cores, pieces, block_units)
    bias_units = lax.dynamic_slice(
        bias_units, (0, core, piece, 0), (planes, 1, 1, block_units)
    ).reshape(1, unit_count)
    groups = [list(range(pieces - 1)), [pieces - 1]]
    pieces3 = chips_gather(low_three)
    threes, actives, d_hiddens, parts3, leaving, out_groups = [], [], [], [], [], []
    for group in groups:
        mine = jnp.stack([pieces3[m] for m in group])
        if d_hiddens:
            mine = after(mine, d_hiddens[-1])
        theirs = other(mine, "core", 1)
        active, d_hidden, d_mine, d_theirs, out_mine, out_theirs = units_group(
            own, mine, theirs, all_ups, group[0], expand_t, shrink_w, bias_units
        )
        d_sum = d_mine + wide(other(d_theirs, "core", 1))
        for i, m in enumerate(group):
            leaving.append(d_sum[i] if m == 0 else low(d_sum[i]))
            parts3.append(leaving[-1] if m == 0 else other(leaving[-1], "dp", m))
        threes.append((mine, theirs))
        out_groups.append((out_mine, out_theirs))
        actives.append(active)
        d_hiddens.append(d_hidden)
    actives, d_hiddens = after((actives, d_hiddens), leaving)

    unit_grads = unit_gradients(own, d_hiddens, actives, threes, all_ups)
    unit_grads, parts3 = after((unit_grads, parts3))
    unit_grads = lax.psum_scatter(unit_grads, "z", scatter_dimension=0, tiled=True)
    unit_sums = sum(jnp.sum(wide(d), axis=(0, 1, 2)) for d in d_hiddens)
    d_later, low_later, d_context2, sums3 = single(
        later_back_kernel,
        [flat_float, flat_low, head_low, three_rows],
        [None] * (pieces + 3) + [kind_spec(squares[0], 2), kind_spec(squares[1], 2)],
        [],
        own, *parts3, upstream, later, gain_rows[2:3], *squares,
    )

    out_groups = [
        mine + wide(other(after(theirs, low_later), "core", 1)) for mine, theirs in out_groups
    ]
    outs = [group[i] for group in out_groups for i in range(group.shape[0])]
    d_context2 = exchange(d_context2)
    leaving = after([low(out) for out in outs[1:]], d_context2)
    out_parts = [other(out, "dp", m + 1) for m, out in enumerate(leaving)]
    d_query2, d_memory, d_memory_t = attend_back(
        cross_scalars, query2, key2, value2, d_context2.reshape(part_shape), kept2, lse2,
        cross_first, cross_last,
    )
    d_mixed2 = exchange(after(d_query2, out_parts))
    layer_rows = low(later + outs[0] + sum(wide(part) for part in out_parts) + wide(shrink_bias))
    d_middle, low_middle, d_context1, sums2 = single(
        middle_back_kernel,
        [flat_float, flat_low, head_low, three_rows],
        [None, kind_spec(squares[0], 1), kind_spec(squares[1], 1), None, None, None]
        + [kind_spec(squares[0], 0), kind_spec(squares[1], 0)],
        [pltpu.VMEM(flat_shape, jnp.float32)],
        own, d_mixed2, *squares, d_later, middle, gain_rows[1:2], *squares,
    )
    d_context1, unit_grads = after((exchange(d_context1), unit_grads))

    def turned_grad(columns, rows):
        half = columns.shape[1] // cores
        return low(
            sum(
                product(columns[:, j * half : (j + 1) * half], rows[j].reshape(half, model_width))
                for j in range(cores)
            )
        )

    def to_chips(*grads):
        split = [grad.reshape(-1, pieces, block_rows) for grad in grads]
        return trade(jnp.concatenate(split).transpose(1, 0, 2), "dp", 0, 0)

    unit_grads = to_chips(
        unit_grads.reshape(2 * block_units, model_width),
        turned_grad(after(d_memory_t, d_context1), all_states),
    )
    d_mine, d_theirs, d_query1, d_query1_t, d_memory1, d_memory1_t = attend_back(
        self_scalars, query1.reshape(part_shape), key1, value1, d_context1.reshape(part_shape), kept1, lse1,
        self_first, self_last, attend_w,
    )
    d_mine, d_theirs, d_query1_t, d_memory1_t, unit_grads = after(
        (d_mine, d_theirs, d_query1_t, d_memory1_t, unit_grads)
    )
    cross_sum = unit_grads[:, 2 * block_units :]
    unit_grads = unit_grads[:, : 2 * block_units].reshape(unit_count, 2, block_rows)
    d_theirs = other(d_theirs, "core", 1)
    d_sum = [d_mine[m] + wide(d_theirs[m]) for m in range(pieces)]
    leaving = [low(d_sum[m]) for m in range(1, pieces)]
    parts1 = [d_sum[0]] + [other(part, "dp", m + 1) for m, part in enumerate(leaving)]

    d_memory, low_middle_late, layer_rows, turned_late = after(
        (d_memory, low_middle, layer_rows, (d_query1_t, d_memory1_t)), leaving
    )
    layer_first = trade(layer_rows, "z", 0, 0)
    d_states = [
        product(part.reshape(-1, 2 * width), cross_kv).reshape(pieces, memory_rows, model_width)
        for part in d_memory
    ]
    d_states = d_states[0] + wide(other(low(d_states[1]), "core", 1))
    kinds = 3
    square_shape = (pieces, planes, kinds, width, block_rows)
    square_mine, square_theirs = single(
        square_grad_kernel,
        [
            jax.ShapeDtypeStruct(square_shape, jnp.bfloat16),
            jax.ShapeDtypeStruct(square_shape, jnp.bfloat16),
        ],
        [None] * 6,
        [],
        own, mixed1, low_middle_late, d_mixed2, low_two, mixed2, low_later,
    )
    attend_sum = [turned_grad(turned, ones) for turned in turned_late]
    parts1, layer_first, d_states, square_mine, square_theirs, attend_sum = after(
        (parts1, layer_first, d_states, square_mine, square_theirs, attend_sum)
    )
    attend_sum = to_chips(*attend_sum)
    state_parts = [other(low(d_states[m]), "dp", m) for m in range(1, pieces)]
    encoder_rows = low(d_states[0] + sum(wide(part) for part in state_parts))
    encoder_gradient = swap_planes(encoder_rows)[None]
    square_theirs = other(square_theirs, "core", 1)
    square_sums = [wide(square_mine[m]) + wide(square_theirs[m]) for m in range(pieces)]
    square_parts = [
        other(after(low(square_sums[m]), state_parts), "dp", m) for m in range(1, pieces)
    ]
    square_sum = square_sums[0] + sum(wide(part) for part in square_parts)
    input_gradient, sums1 = single(
        input_back_kernel,
        [flat_low, jax.ShapeDtypeStruct((2, model_width), jnp.float32)],
        [None] * (pieces + 3),
        [],
        own, *parts1, d_middle, raw, gain_rows[0:1],
    )
    input_gradient = trade(trade(after(input_gradient, attend_sum), "z", 0, 0), "dp", 0, 0)[None]
    layer_output = trade(after(layer_first, input_gradient), "dp", 0, 0)[None]

    tail = jnp.concatenate(
        [low(square_sum).reshape(planes, 3 * width, block_rows), cross_sum, attend_sum], axis=1
    )
    tail = sum(
        wide(part if m == 0 else other(part, "z", m))
        for m, part in enumerate(
            lax.dynamic_index_in_dim(tail, plane ^ m, 0, keepdims=False) for m in range(planes)
        )
    )
    square_sum = tail[: 3 * width].reshape(3, width, block_rows)
    cross_sum, attend_sum = tail[3 * width : 5 * width], tail[5 * width :]
    unit_grads = wide(unit_grads)

    def weight_order(turned, count):
        turned = turned.reshape(count, heads, head_size, block_rows).transpose(3, 1, 0, 2)
        return turned.reshape(block_rows, count * width)

    unit_sums = lax.dynamic_update_slice(
        jnp.zeros((planes, cores, pieces, block_units), jnp.float32),
        unit_sums.reshape(planes, 1, 1, block_units),
        (0, core, piece, 0),
    ).reshape(-1)
    small = jnp.concatenate(
        [
            sums2[0],
            sums3[0],
            sums2[1],
            sums3[1],
            sums2[2],
            jnp.sum(wide(d_mixed2), axis=2).transpose(1, 0, 2).reshape(-1),
            place_heads(jnp.sum(wide(d_memory_t[width:]), axis=1)),
            sums3[2],
            jnp.sum(wide(upstream), axis=0),
            unit_sums,
        ]
    )
    last = jnp.stack(
        [
            sums1[0],
            sums1[1],
            place_heads(jnp.sum(wide(d_query1_t), axis=1)),
            place_heads(jnp.sum(wide(d_memory1_t[width:]), axis=1)),
        ]
    )
    small = sum_all(jnp.concatenate([last.reshape(-1), small]).reshape(-1, 128)).reshape(-1)
    last, small = small[: 4 * model_width].reshape(4, model_width), small[4 * model_width :]
    rows = small[: 9 * model_width].reshape(9, model_width)
    return (
        layer_output,
        input_gradient,
        encoder_gradient,
        jnp.concatenate([last[0:1], rows[0:2]]),
        jnp.concatenate([last[1:2], rows[2:4]]),
        weight_order(attend_sum, 3),
        square_sum[0],
        jnp.concatenate([last[2:4], rows[4:5]]),
        square_sum[1].T,
        weight_order(cross_sum, 2),
        square_sum[2],
        rows[5:8],
        unit_grads[:, 0].T,
        small[9 * model_width :],
        unit_grads[:, 1],
        rows[8],
    )


def solution(mesh):
    pieces, sequence = mesh.devices.shape
    planes = Mesh(mesh.devices.reshape(pieces, sequence // 2, 2), ("dp", "z", "core"))
    seq = ("z", "core")
    in_specs = (
        P("dp", seq, None),
        P("dp", seq, None),
        P("dp", None),
        P("dp", None),
        P(),
        P(),
        P("dp", seq),
        P(seq, "dp"),
        P(),
        P("dp", seq),
        P("dp", seq),
        P(seq, "dp"),
        P(),
        P("dp", seq),
        P(),
        P(seq, "dp"),
        P(),
        P("dp", seq, None),
    )
    out_specs = (
        P("dp", seq, None),
        P("dp", seq, None),
        P("dp", seq, None),
        P(),
        P(),
        P("dp", seq),
        P(seq, "dp"),
        P(),
        P("dp", seq),
        P("dp", seq),
        P(seq, "dp"),
        P(),
        P("dp", seq),
        P(),
        P(seq, "dp"),
        P(),
    )
    return jax.shard_map(
        shards, mesh=planes, in_specs=in_specs, out_specs=out_specs, check_vma=False
    )
```

```python
import functools
import math

import jax
import jax.numpy as jnp
from jax import lax
from jax.experimental import pallas as pl
from jax.experimental.pallas import tpu as pltpu
from jax.sharding import Mesh
from jax.sharding import PartitionSpec as P

HEADS = 16

epsilon = 1e-05
masked_score = -1e30
head_width = 64


def head_columns(transposed, heads):
    if heads == 1:
        return transposed
    feature = lax.broadcasted_iota(jnp.int32, transposed.shape, 0) // head_width
    zero = jnp.zeros_like(transposed)
    return jnp.concatenate([jnp.where(feature == h, transposed, zero) for h in range(heads)], axis=1)


def head_rows(block, heads):
    if heads == 1:
        return block
    feature = lax.broadcasted_iota(jnp.int32, block.shape, 1) // head_width
    zero = jnp.zeros_like(block)
    return jnp.concatenate([jnp.where(feature == h, block, zero) for h in range(heads)], axis=0)


def flip(block):
    return jnp.transpose(block.astype(jnp.float32), (1, 0)).astype(block.dtype)


def repeat_heads(row, heads):
    return row if heads == 1 else jnp.concatenate([row] * heads, axis=1)


def project(scalars, mine_ref, theirs_ref, weight_ref, bias_ref, out_refs, width):
    weight = weight_ref[...]
    bias = bias_ref[...]
    for j, source in enumerate((mine_ref, theirs_ref)):
        for m in range(source.shape[0]):
            rows = bias + lax.dot_general(
                source[m], weight, (((1,), (1,)), ((), ())), preferred_element_type=jnp.float32
            )
            rows = rows.astype(jnp.bfloat16)
            for i, out_ref in enumerate(out_refs):
                out_ref[j, m] = rows[:, i * width : (i + 1) * width]


def natural_blocks(scalars, shape, planes):
    cores, pieces, rows = shape[:3]
    part = rows // planes
    for plane in range(planes):
        for core in range(cores):
            slots = [
                ((core ^ scalars[0], piece ^ scalars[1]), plane * part) for piece in range(pieces)
            ]
            if planes == 1:
                for piece in range(pieces):
                    yield (piece * cores + core) * rows, rows, slots[piece : piece + 1]
            else:
                yield (plane * cores + core) * pieces * part, part, slots


def take_rows(ref, part, slots):
    blocks = [ref[slot[0], slot[1], first : first + part] for slot, first in slots]
    return blocks[0] if len(blocks) == 1 else jnp.concatenate(blocks, axis=0)


def query_rows_of(ref, flip_by=0):
    return jnp.concatenate([ref[0, piece ^ flip_by, 0] for piece in range(ref.shape[1])], axis=0)


def put_query_rows(ref, block, flip_by=0):
    part = ref.shape[3]
    for piece in range(ref.shape[1]):
        ref[0, piece ^ flip_by, 0] = block[piece * part : (piece + 1) * part]


def attend_rows(scalars, query, first_ref, last_ref, keys, flipped, heads, key_block):
    step = pl.program_id(0)
    steps = pl.num_programs(0)
    rows = query.shape[0]
    query = query * jnp.asarray(1.0 / math.sqrt(head_width), jnp.bfloat16)
    columns = head_columns(flip(query), heads)
    first = repeat_heads(first_ref[0], heads)
    last = repeat_heads(last_ref[0], heads)

    def one(block, carry):
        peak, total, sums = carry
        start = pl.multiple_of(block * key_block, key_block)
        scores = jnp.dot(keys[pl.ds(start, key_block), :], columns, preferred_element_type=jnp.float32)
        place = start + lax.broadcasted_iota(jnp.int32, scores.shape, 0)
        scores = jnp.where((place >= first) & (place <= last), scores, masked_score)
        newer = jnp.maximum(peak, jnp.max(scores, axis=0, keepdims=True))
        shrink = jnp.exp(peak - newer)
        exponent = jnp.exp(scores - newer)
        total = total * shrink + jnp.sum(exponent, axis=0, keepdims=True)
        low_part = exponent.astype(jnp.bfloat16)
        turned = flipped[block]
        fresh = []
        for h in range(heads):
            part = jnp.dot(
                turned[h * head_width : (h + 1) * head_width],
                low_part[:, h * rows : (h + 1) * rows],
                preferred_element_type=jnp.float32,
            )
            fresh.append(sums[h] * shrink[:, h * rows : (h + 1) * rows] + part)
        return (newer, total, tuple(fresh))

    empty = (
        jnp.full((1, heads * rows), masked_score, jnp.float32),
        jnp.zeros((1, heads * rows), jnp.float32),
        tuple(jnp.zeros((head_width, rows), jnp.float32) for _ in range(heads)),
    )
    peak, total, sums = lax.fori_loop(scalars[2 + step], scalars[2 + steps + step] + 1, one, empty)
    context = jnp.concatenate(
        [sums[h] / total[:, h * rows : (h + 1) * rows] for h in range(heads)], axis=0
    )
    return context, peak + jnp.log(total)


def prepare(scalars, k_ref, v_ref, keys, flipped, key_block, planes):
    for start, part, slots in natural_blocks(scalars, k_ref.shape, planes):
        rows = part * len(slots)
        keys[start : start + rows, :] = take_rows(k_ref, part, slots)
        offset = start % key_block
        flipped[start // key_block, :, offset : offset + rows] = flip(take_rows(v_ref, part, slots))


def finish_forward(context, lse, ctx_ref, keep_ref, lse_ref):
    keep_ref[0] = context
    lse_ref[0] = lse
    put_query_rows(ctx_ref, jnp.transpose(context, (1, 0)).astype(jnp.bfloat16))


def self_forward_kernel(
    scalars, mine_ref, theirs_ref, weight_ref, bias_ref, first_ref, last_ref,
    q_ref, k_ref, v_ref, ctx_ref, keep_ref, lse_ref, keys, flipped,
    *, heads, key_block, planes,
):
    step = pl.program_id(0)
    cores, pieces, rows = q_ref.shape[:3]
    part = rows // planes

    @pl.when(step == 0)
    def _():
        outs = (q_ref, k_ref, v_ref)
        project(scalars, mine_ref, theirs_ref, weight_ref, bias_ref, outs, heads * head_width)
        prepare(scalars, k_ref, v_ref, keys, flipped, key_block, planes)

    core = lax.rem(step, cores) ^ scalars[0]
    here = pl.ds(pl.multiple_of(lax.div(step, cores) * part, part), part)
    query = jnp.concatenate(
        [q_ref[core, piece ^ scalars[1], here, :] for piece in range(pieces)], axis=0
    )
    context, lse = attend_rows(
        scalars, query, first_ref, last_ref, keys, flipped, heads, key_block
    )
    finish_forward(context, lse, ctx_ref, keep_ref, lse_ref)


def cross_forward_kernel(
    scalars, q_ref, mine_ref, theirs_ref, weight_ref, bias_ref, first_ref, last_ref,
    k_ref, v_ref, ctx_ref, keep_ref, lse_ref, keys, flipped,
    *, heads, key_block,
):
    @pl.when(pl.program_id(0) == 0)
    def _():
        outs = (k_ref, v_ref)
        project(scalars, mine_ref, theirs_ref, weight_ref, bias_ref, outs, heads * head_width)
        prepare(scalars, k_ref, v_ref, keys, flipped, key_block, 1)

    context, lse = attend_rows(
        scalars, query_rows_of(q_ref), first_ref, last_ref, keys, flipped, heads, key_block
    )
    finish_forward(context, lse, ctx_ref, keep_ref, lse_ref)


def backward_kernel(
    scalars, q_ref, k_ref, v_ref, dc_ref, keep_ref, lse_ref, first_ref, last_ref,
    *rest, heads, key_block, planes, near,
):
    if near:
        weight_ref, dmine_ref, dtheirs_ref, *rest = rest
        dq_ref, dqt_ref, dkv_ref, dkvt_ref, keys, values, flipped, dkeys, dvalues = rest
    else:
        dq_ref, dkv_ref, dkvt_ref, keys, values, flipped, dkeys, dvalues = rest
    step = pl.program_id(0)
    steps = pl.num_programs(0)
    width = heads * head_width
    scaling = 1.0 / math.sqrt(head_width)

    @pl.when(step == 0)
    def _():
        prepare(scalars, k_ref, k_ref, keys, flipped, key_block, planes)
        for start, part, slots in natural_blocks(scalars, v_ref.shape, planes):
            values[start : start + part * len(slots), :] = take_rows(v_ref, part, slots)
        dkeys[...] = jnp.zeros_like(dkeys)
        dvalues[...] = jnp.zeros_like(dvalues)

    flip_by = scalars[1] if near else 0
    query = query_rows_of(q_ref, flip_by) * jnp.asarray(scaling, jnp.bfloat16)
    rows = query.shape[0]
    grad = query_rows_of(dc_ref)
    turned_grad = flip(grad)
    query_columns = head_columns(flip(query), heads)
    grad_columns = head_columns(turned_grad, heads)
    query_rows = head_rows(query, heads)
    grad_rows = head_rows(grad, heads)
    dots_kept = turned_grad.astype(jnp.float32) * keep_ref[0]
    center = jnp.concatenate(
        [
            jnp.sum(dots_kept[h * head_width : (h + 1) * head_width], axis=0, keepdims=True)
            for h in range(heads)
        ],
        axis=1,
    )
    first = repeat_heads(first_ref[0], heads)
    last = repeat_heads(last_ref[0], heads)
    lse = lse_ref[0]

    def one(block, sums):
        start = pl.multiple_of(block * key_block, key_block)
        here = pl.ds(start, key_block)
        scores = jnp.dot(keys[here, :], query_columns, preferred_element_type=jnp.float32)
        place = start + lax.broadcasted_iota(jnp.int32, scores.shape, 0)
        scores = jnp.where((place >= first) & (place <= last), scores, masked_score)
        weights = jnp.exp(scores - lse)
        dots = jnp.dot(values[here, :], grad_columns, preferred_element_type=jnp.float32)
        dscore = (weights * (dots - center)).astype(jnp.bfloat16)
        dvalues[here, :] += jnp.dot(
            weights.astype(jnp.bfloat16), grad_rows, preferred_element_type=jnp.float32
        )
        dkeys[here, :] += jnp.dot(dscore, query_rows, preferred_element_type=jnp.float32)
        turned = flipped[block]
        return tuple(
            sums[h]
            + jnp.dot(
                turned[h * head_width : (h + 1) * head_width],
                dscore[:, h * rows : (h + 1) * rows],
                preferred_element_type=jnp.float32,
            )
            for h in range(heads)
        )

    empty = tuple(jnp.zeros((head_width, rows), jnp.float32) for _ in range(heads))
    sums = lax.fori_loop(scalars[2 + step], scalars[2 + steps + step] + 1, one, empty)
    dquery = jnp.concatenate(sums, axis=0) * scaling
    dquery = jnp.transpose(dquery, (1, 0)).astype(jnp.bfloat16)
    if near:
        core = lax.rem(step, dq_ref.shape[0]) ^ scalars[0]
        plane = lax.div(step, dq_ref.shape[0])
        part = dq_ref.shape[3]
        for piece in range(dq_ref.shape[1]):
            dq_ref[core, piece ^ flip_by, plane] = dquery[piece * part : (piece + 1) * part]
    else:
        put_query_rows(dq_ref, dquery)

    @pl.when(step == steps - 1)
    def _():
        cores, pieces, key_rows = k_ref.shape[:3]
        for start, part, slots in natural_blocks(scalars, k_ref.shape, planes):
            for i, (slot, first) in enumerate(slots):
                here = slice(start + i * part, start + (i + 1) * part)
                for column, total in ((0, dkeys), (width, dvalues)):
                    dkv_ref[slot[0], slot[1], first : first + part, column : column + width] = (
                        total[here, :].astype(jnp.bfloat16)
                    )
        for j in reversed(range(cores)):
            for m in range(pieces):
                if near:
                    rows_grad = jnp.dot(
                        dq_ref[j, m].reshape(key_rows, width),
                        weight_ref[:width],
                        preferred_element_type=jnp.float32,
                    ) + jnp.dot(
                        dkv_ref[j, m], weight_ref[width:], preferred_element_type=jnp.float32
                    )
                    if j == 0:
                        dmine_ref[m] = rows_grad
                    else:
                        dtheirs_ref[m] = rows_grad.astype(jnp.bfloat16)
                place = (j * pieces + m) * key_rows
                dkvt_ref[:, place : place + key_rows] = flip(dkv_ref[j, m])
                if near:
                    block = dq_ref[j, m].reshape(key_rows, width)
                    dqt_ref[:, place : place + key_rows] = flip(block)


def whole_spec(shape, index=None):
    index = (0,) * len(shape) if index is None else index
    return pl.BlockSpec(shape, lambda step, scalars: index)


def step_spec(shape):
    return pl.BlockSpec((1,) + shape[1:], lambda step, scalars: (step, 0, 0))


def member_spec(shape, near):
    cores, pieces = shape[:2]

    def place(step, scalars):
        core = lax.rem(step, cores)
        return (core ^ scalars[0] if near else core, 0, lax.div(step, cores), 0, 0)

    return pl.BlockSpec((1, pieces, 1) + shape[3:], place)


def forward_outputs(shape):
    cores, pieces, planes, rows, width = shape
    steps = cores * planes
    heads = width // head_width
    shapes = [
        jax.ShapeDtypeStruct(shape, jnp.bfloat16),
        jax.ShapeDtypeStruct((steps, width, pieces * rows), jnp.float32),
        jax.ShapeDtypeStruct((steps, 1, heads * pieces * rows), jnp.float32),
    ]
    specs = [member_spec(shape, False), step_spec(shapes[1].shape), step_spec(shapes[2].shape)]
    return shapes, specs


def cost(microseconds):
    return pl.CostEstimate(
        flops=int(microseconds * 1.1e9), bytes_accessed=1 << 20, transcendentals=0
    )


def params(mebibytes=56):
    return pltpu.CompilerParams(vmem_limit_bytes=mebibytes * 2**20)


def self_forward(scalars, mine, theirs, planes, weight, bias, first, last):
    pieces, rows, model_width = mine.shape
    width = weight.shape[0] // 3
    shape = (2, pieces, rows, width)
    steps = 2 * planes
    key_count = 2 * pieces * rows
    key_block = min(256, key_count)
    shapes, specs = forward_outputs((2, pieces, planes, rows // planes, width))
    full = jax.ShapeDtypeStruct(shape, jnp.bfloat16)
    return pl.pallas_call(
        functools.partial(
            self_forward_kernel, heads=width // head_width, key_block=key_block, planes=planes
        ),
        grid_spec=pltpu.PrefetchScalarGridSpec(
            num_scalar_prefetch=1,
            grid=(steps,),
            in_specs=[
                whole_spec(mine.shape),
                whole_spec(theirs.shape),
                whole_spec(weight.shape),
                whole_spec(bias.shape),
                step_spec(first.shape),
                step_spec(last.shape),
            ],
            out_specs=[whole_spec(shape)] * 3 + specs,
            scratch_shapes=[
                pltpu.VMEM((key_count, width), jnp.bfloat16),
                pltpu.VMEM((key_count // key_block, width, key_block), jnp.bfloat16),
            ],
        ),
        out_shape=[full] * 3 + shapes,
        compiler_params=params(),
        cost_estimate=cost(16),
    )(scalars, mine, theirs, weight, bias, first, last)


def cross_forward(scalars, queries, mine, theirs, weight, bias, first, last):
    cores, pieces, planes, rows, width = queries.shape
    state_rows = mine.shape[1]
    steps = cores * planes
    key_count = cores * pieces * state_rows
    key_block = min(256, key_count)
    shapes, specs = forward_outputs(queries.shape)
    key_shape = (cores, pieces, state_rows, width)
    full = jax.ShapeDtypeStruct(key_shape, jnp.bfloat16)
    return pl.pallas_call(
        functools.partial(cross_forward_kernel, heads=width // head_width, key_block=key_block),
        grid_spec=pltpu.PrefetchScalarGridSpec(
            num_scalar_prefetch=1,
            grid=(steps,),
            in_specs=[
                member_spec(queries.shape, False),
                whole_spec(mine.shape),
                whole_spec(theirs.shape),
                whole_spec(weight.shape),
                whole_spec(bias.shape),
                step_spec(first.shape),
                step_spec(last.shape),
            ],
            out_specs=[whole_spec(key_shape)] * 2 + specs,
            scratch_shapes=[
                pltpu.VMEM((key_count, width), jnp.bfloat16),
                pltpu.VMEM((key_count // key_block, width, key_block), jnp.bfloat16),
            ],
        ),
        out_shape=[full] * 2 + shapes,
        compiler_params=params(),
        cost_estimate=cost(11),
    )(scalars, queries, mine, theirs, weight, bias, first, last)


def attend_back(scalars, queries, key_rows, values, grad, kept, lse, first, last, weight=None):
    near = weight is not None
    cores, pieces, planes, rows, width = queries.shape
    steps = cores * planes
    key_shape = key_rows.shape
    key_count = cores * pieces * key_shape[2]
    key_block = min(256, key_count)
    dq_shape = jax.ShapeDtypeStruct(queries.shape, jnp.bfloat16)
    if near:
        row_shape = (pieces, planes * rows, weight.shape[1])
        dq_shapes = [
            jax.ShapeDtypeStruct(row_shape, jnp.float32),
            jax.ShapeDtypeStruct(row_shape, jnp.bfloat16),
            dq_shape,
            jax.ShapeDtypeStruct((width, key_count), jnp.bfloat16),
        ]
        dq_specs = [whole_spec(shape.shape) for shape in dq_shapes]
    else:
        dq_shapes, dq_specs = [dq_shape], [member_spec(queries.shape, False)]
    return pl.pallas_call(
        functools.partial(
            backward_kernel,
            heads=width // head_width,
            key_block=key_block,
            planes=planes if near else 1,
            near=near,
        ),
        grid_spec=pltpu.PrefetchScalarGridSpec(
            num_scalar_prefetch=1,
            grid=(steps,),
            in_specs=[
                member_spec(queries.shape, near),
                whole_spec(key_shape),
                whole_spec(key_shape),
                member_spec(grad.shape, False),
                step_spec(kept.shape),
                step_spec(lse.shape),
                step_spec(first.shape),
                step_spec(last.shape),
            ]
            + ([whole_spec(weight.shape)] if near else []),
            out_specs=dq_specs
            + [whole_spec(key_shape[:3] + (2 * width,)), whole_spec((2 * width, key_count))],
            scratch_shapes=[
                pltpu.VMEM((key_count, width), jnp.bfloat16),
                pltpu.VMEM((key_count, width), jnp.bfloat16),
                pltpu.VMEM((key_count // key_block, width, key_block), jnp.bfloat16),
                pltpu.VMEM((key_count, width), jnp.float32),
                pltpu.VMEM((key_count, width), jnp.float32),
            ],
        ),
        out_shape=dq_shapes
        + [
            jax.ShapeDtypeStruct(key_shape[:3] + (2 * width,), jnp.bfloat16),
            jax.ShapeDtypeStruct((2 * width, key_count), jnp.bfloat16),
        ],
        compiler_params=params(),
        cost_estimate=cost(12),
    )(
        scalars, queries, key_rows, values, grad, kept, lse, first, last,
        *([weight] if near else []),
    )


def single(kernel, out_shape, in_specs, scratch, *args):
    return pl.pallas_call(
        kernel,
        grid_spec=pltpu.PrefetchScalarGridSpec(
            num_scalar_prefetch=1,
            grid=(1,),
            in_specs=[
                whole_spec(value.shape) if spec is None else spec
                for spec, value in zip(in_specs, args[1:])
            ],
            out_specs=[whole_spec(value.shape) for value in out_shape],
            scratch_shapes=scratch,
        ),
        out_shape=out_shape,
        compiler_params=params(),
        cost_estimate=cost(4),
    )(*args)


def kind_spec(array, kind):
    shape = (array.shape[0], array.shape[1], 1) + array.shape[3:]
    return whole_spec(shape, (0, 0, kind, 0, 0))


def square_block(ref, m):
    block = ref[m, :, 0]
    return block.reshape(block.shape[0] * block.shape[1], block.shape[2])


def heads_of(ref, core):
    return jnp.concatenate([ref[core, piece] for piece in range(ref.shape[1])], axis=1)


def near_span(scalars, m, size):
    return pl.ds(pl.multiple_of((scalars[1] ^ m) * size, size), size)


def heads_to_model(scalars, heads_ref, mine_ref, theirs_ref, sums):
    mine, theirs = heads_of(heads_ref, scalars[0]), heads_of(heads_ref, 1 ^ scalars[0])
    size = mine_ref.shape[4]
    for m in range(mine_ref.shape[0]):
        sums[:, near_span(scalars, m, size)] = jnp.dot(
            mine, square_block(mine_ref, m), preferred_element_type=jnp.float32
        ) + jnp.dot(theirs, square_block(theirs_ref, m), preferred_element_type=jnp.float32)


def model_to_heads(scalars, rows_ref, mine_ref, theirs_ref, heads_ref, bias_ref=None):
    size = mine_ref.shape[4]
    pieces, width = heads_ref.shape[1], heads_ref.shape[3]
    for j, weight_ref in enumerate((mine_ref, theirs_ref)):
        total = 0.0
        for m in range(weight_ref.shape[0]):
            total = total + lax.dot_general(
                rows_ref[:, near_span(scalars, m, size)],
                square_block(weight_ref, m),
                (((1,), (1,)), ((), ())),
                preferred_element_type=jnp.float32,
            )
        core = scalars[0] ^ j
        for piece in range(pieces):
            block = total[:, piece * width : (piece + 1) * width]
            if bias_ref is not None:
                block = block + bias_ref[core, piece]
            heads_ref[core, piece] = block.astype(jnp.bfloat16)


def normal_parts(values):
    center = values - jnp.mean(values, axis=-1, keepdims=True)
    spread = jnp.mean(center * center, axis=-1, keepdims=True)
    scale = lax.rsqrt(spread + epsilon)
    return center * scale, scale


def norm_back(values, gain, dn):
    normal, scale = normal_parts(values)
    e = dn * gain
    dv = scale * (
        e
        - jnp.mean(e, axis=-1, keepdims=True)
        - normal * jnp.mean(e * normal, axis=-1, keepdims=True)
    )
    return (
        dv,
        jnp.sum(dn * normal, axis=0, keepdims=True),
        jnp.sum(dn, axis=0, keepdims=True),
    )


def middle_kernel(
    scalars, heads_ref, omine_ref, otheirs_ref, resid_ref, rows_ref, qmine_ref, qtheirs_ref,
    qbias_ref, sum_ref, norm_ref, q_ref,
):
    heads_to_model(scalars, heads_ref, omine_ref, otheirs_ref, sum_ref)
    total = sum_ref[...] + resid_ref[...].astype(jnp.float32) + rows_ref[0:1]
    sum_ref[...] = total
    normal, _ = normal_parts(total)
    norm_ref[...] = (normal * rows_ref[1:2] + rows_ref[2:3]).astype(jnp.bfloat16)
    model_to_heads(scalars, norm_ref, qmine_ref, qtheirs_ref, q_ref, qbias_ref)


def later_kernel(
    scalars, heads_ref, omine_ref, otheirs_ref, resid_ref, rows_ref, sum_ref, norm_ref
):
    heads_to_model(scalars, heads_ref, omine_ref, otheirs_ref, sum_ref)
    total = sum_ref[...] + resid_ref[...] + rows_ref[0:1]
    sum_ref[...] = total
    normal, _ = normal_parts(total)
    norm_ref[...] = (normal * rows_ref[1:2] + rows_ref[2:3]).astype(jnp.bfloat16)


def finish_back(scalars, values_ref, rows_ref, dn, upper, mine_ref, theirs_ref, d_ref, low_ref, heads_ref, sums_ref):
    dv, dg, db = norm_back(values_ref[...], rows_ref[0:1], dn)
    total = upper + dv
    d_ref[...] = total
    low_total = total.astype(jnp.bfloat16)
    low_ref[...] = low_total
    sums_ref[0:1] = dg
    sums_ref[1:2] = db
    sums_ref[2:3] = jnp.sum(low_total.astype(jnp.float32), axis=0, keepdims=True)
    model_to_heads(scalars, low_ref, mine_ref, theirs_ref, heads_ref)


def later_back_kernel(scalars, *refs):
    parts, (up_ref, values_ref, rows_ref, mine_ref, theirs_ref) = refs[:-9], refs[-9:-4]
    dn = parts[0][...].reshape(up_ref.shape)
    for part in parts[1:]:
        dn = dn + part[...].reshape(up_ref.shape).astype(jnp.float32)
    upper = up_ref[...].astype(jnp.float32)
    finish_back(scalars, values_ref, rows_ref, dn, upper, mine_ref, theirs_ref, *refs[-4:])


def middle_back_kernel(
    scalars, heads_ref, qmine_ref, qtheirs_ref, upper_ref, values_ref, rows_ref, mine_ref,
    theirs_ref, d_ref, low_ref, dheads_ref, sums_ref, work,
):
    heads_to_model(scalars, heads_ref, qmine_ref, qtheirs_ref, work)
    finish_back(
        scalars, values_ref, rows_ref, work[...], upper_ref[...], mine_ref, theirs_ref,
        d_ref, low_ref, dheads_ref, sums_ref,
    )


def input_back_kernel(scalars, *refs):
    parts, (upper_ref, values_ref, rows_ref, out_ref, sums_ref) = refs[:-5], refs[-5:]
    dn = parts[0][...].reshape(upper_ref.shape)
    for part in parts[1:]:
        dn = dn + part[...].reshape(upper_ref.shape).astype(jnp.float32)
    dv, dg, db = norm_back(values_ref[...].astype(jnp.float32), rows_ref[0:1], dn)
    out_ref[...] = (upper_ref[...] + dv).astype(jnp.bfloat16)
    sums_ref[0:1] = dg
    sums_ref[1:2] = db


def square_grad_kernel(scalars, *refs):
    kinds = (len(refs) - 2) // 2
    mine_ref, theirs_ref = refs[-2:]
    size = mine_ref.shape[4]
    for kind in range(kinds):
        heads_ref, rows_ref = refs[2 * kind], refs[2 * kind + 1]
        for j, out_ref in enumerate((mine_ref, theirs_ref)):
            for piece in range(heads_ref.shape[1]):
                turned = flip(heads_ref[scalars[0] ^ j, piece])
                for m in range(out_ref.shape[0]):
                    out_ref[m, piece, kind] = jnp.dot(
                        turned,
                        rows_ref[:, near_span(scalars, m, size)],
                        preferred_element_type=jnp.float32,
                    ).astype(out_ref.dtype)


def gelu_parts(u):
    root = math.sqrt(2.0 / math.pi)
    square = u * u
    bent = jnp.tanh(root * (u + 0.044715 * (square * u)))
    half = 0.5 * (1.0 + bent)
    slope = half + 0.5 * u * (1.0 - bent * bent) * (root * (1.0 + 3.0 * 0.044715 * square))
    return u * half, slope


def units_kernel(
    scalars, mine_ref, theirs_ref, upmine_ref, uptheirs_ref, expand_ref, shrink_ref, bias_ref,
    active_ref, dhidden_ref, dmine_ref, dtheirs_ref, outmine_ref, outtheirs_ref, half_count,
):
    step = pl.program_id(0)
    expand, shrink = expand_ref[...], shrink_ref[...]
    against_last = (((1,), (1,)), ((), ()))

    def one(rows, up):
        hidden = lax.dot_general(rows, expand, against_last, preferred_element_type=jnp.float32)
        dactive = lax.dot_general(up, shrink, against_last, preferred_element_type=jnp.float32)
        active, slope = gelu_parts(hidden + bias_ref[...])
        dhidden = (dactive * slope).astype(jnp.bfloat16)
        active = active.astype(jnp.bfloat16)
        active_ref[0, 0] = active
        dhidden_ref[0, 0] = dhidden
        return (
            jnp.dot(dhidden, expand, preferred_element_type=jnp.float32),
            jnp.dot(active, shrink, preferred_element_type=jnp.float32),
        )

    @pl.when(step < half_count)
    def _():
        dthree, out = one(theirs_ref[0], uptheirs_ref[0])
        dtheirs_ref[0] = dthree.astype(jnp.bfloat16)
        outtheirs_ref[0] = out.astype(jnp.bfloat16)

    @pl.when(step >= half_count)
    def _():
        dthree, out = one(mine_ref[0], upmine_ref[0])
        dmine_ref[0] = dthree
        outmine_ref[0] = out


def units_group(scalars, mine, theirs, ups, start, expand_t, shrink_w, bias):
    count, rows, model_width = mine.shape
    units = expand_t.shape[0]

    def piece_spec(own, offset=0):
        if own:
            place = lambda step, scalars: (jnp.maximum(step - count, 0) + offset, 0, 0)
        else:
            place = lambda step, scalars: (jnp.minimum(step, count - 1) + offset, 0, 0)
        return pl.BlockSpec((1, rows, model_width), place)

    def table_place(step, scalars):
        return (1 - lax.div(step, count), lax.rem(step, count), 0, 0)

    table = jax.ShapeDtypeStruct((2, count, rows, units), jnp.bfloat16)
    table_spec = pl.BlockSpec((1, 1, rows, units), table_place)
    return pl.pallas_call(
        functools.partial(units_kernel, half_count=count),
        grid_spec=pltpu.PrefetchScalarGridSpec(
            num_scalar_prefetch=1,
            grid=(2 * count,),
            in_specs=[
                piece_spec(True),
                piece_spec(False),
                piece_spec(True, start),
                piece_spec(False, start),
                whole_spec(expand_t.shape),
                whole_spec(shrink_w.shape),
                whole_spec(bias.shape),
            ],
            out_specs=[table_spec, table_spec] + [piece_spec(True), piece_spec(False)] * 2,
        ),
        out_shape=[
            table,
            table,
            jax.ShapeDtypeStruct(mine.shape, jnp.float32),
            jax.ShapeDtypeStruct(mine.shape, jnp.bfloat16),
        ]
        + [
            jax.ShapeDtypeStruct(mine.shape, jnp.float32),
            jax.ShapeDtypeStruct(mine.shape, jnp.bfloat16),
        ],
        compiler_params=params(32),
        cost_estimate=cost(6.5 * count),
    )(scalars, mine, theirs, *ups, expand_t, shrink_w, bias)


def unit_gradients_kernel(scalars, *refs, counts):
    dhidden_refs, active_refs = refs[0:2], refs[2:4]
    row_refs, up_refs = (refs[4:6], refs[6:8]), refs[8:10]
    out_ref, expand_sum, shrink_sum = refs[10:]
    step = pl.program_id(0)
    width = expand_sum.shape[1]

    @pl.when(step == 0)
    def _():
        expand_sum[...] = jnp.zeros_like(expand_sum)
        shrink_sum[...] = jnp.zeros_like(shrink_sum)

    def add(group, core):
        for table_ref, rows_ref, total in (
            (dhidden_refs[group], row_refs[group][core], expand_sum),
            (active_refs[group], up_refs[core], shrink_sum),
        ):
            total[...] += lax.dot_general(
                table_ref[0, 0],
                rows_ref[0],
                (((0,), (0,)), ((), ())),
                preferred_element_type=jnp.float32,
            )

    first = 0
    for group, count in enumerate(counts):
        for core in range(2):
            @pl.when((step >= first) & (step < first + count))
            def _(group=group, core=core):
                add(group, core)

            first += count

    @pl.when(step == pl.num_programs(0) - 1)
    def _():
        out_ref[:, :width] = expand_sum[...].astype(jnp.bfloat16)
        out_ref[:, width:] = shrink_sum[...].astype(jnp.bfloat16)


def unit_gradients(scalars, dhiddens, actives, rows, ups):
    counts = [table.shape[1] for table in actives]
    _, _, tokens, units = actives[0].shape
    model_width = ups[0].shape[2]
    starts = [2 * sum(counts[:i]) for i in range(len(counts))]

    def table_spec(group):
        count, start = counts[group], starts[group]

        def place(step, scalars):
            here = jnp.clip(step - start, 0, 2 * count - 1)
            return (lax.div(here, count), lax.rem(here, count), 0, 0)

        return pl.BlockSpec((1, 1, tokens, units), place)

    def row_place(group, core):
        count, start = counts[group], starts[group] + core * counts[group]
        return pl.BlockSpec(
            (1, tokens, model_width),
            lambda step, scalars: (jnp.clip(step - start, 0, count - 1), 0, 0),
        )

    def up_place(core):
        def place(step, scalars):
            here = 0
            for i in range(len(counts)):
                inside = jnp.clip(step - starts[i] - core * counts[i], 0, counts[i] - 1)
                begun = (step >= starts[i] + core * counts[i]).astype(jnp.int32)
                here = jnp.where(begun == 1, sum(counts[:i]) + inside, here)
            return (here, 0, 0)

        return pl.BlockSpec((1, tokens, model_width), place)

    return pl.pallas_call(
        functools.partial(unit_gradients_kernel, counts=counts),
        grid_spec=pltpu.PrefetchScalarGridSpec(
            num_scalar_prefetch=1,
            grid=(2 * sum(counts),),
            in_specs=[table_spec(0), table_spec(1), table_spec(0), table_spec(1)]
            + [row_place(0, 0), row_place(0, 1), row_place(1, 0), row_place(1, 1)]
            + [up_place(0), up_place(1)],
            out_specs=whole_spec((units, 2 * model_width)),
            scratch_shapes=[pltpu.VMEM((units, model_width), jnp.float32)] * 2,
        ),
        out_shape=jax.ShapeDtypeStruct((units, 2 * model_width), jnp.bfloat16),
        compiler_params=params(),
        cost_estimate=cost(12),
    )(scalars, *dhiddens, *actives, *rows[0], *rows[1], *ups)


def layer_norm(values, gain_row, shift_row):
    center = values - jnp.mean(values, axis=-1, keepdims=True)
    spread = jnp.mean(center * center, axis=-1, keepdims=True)
    return center * lax.rsqrt(spread + epsilon) * gain_row + shift_row


def inner_rows(former, latter):
    return lax.dot_general(
        former, latter, (((0,), (0,)), ((), ())), preferred_element_type=jnp.float32
    )


def against(former, latter):
    return lax.dot_general(
        former, latter, (((1,), (1,)), ((), ())), preferred_element_type=jnp.float32
    )


def product(former, latter):
    return jnp.dot(former, latter, preferred_element_type=jnp.float32)


def low(values):
    return values.astype(jnp.bfloat16)


def wide(values):
    return values.astype(jnp.float32)


def other(values, axis, shift):
    count = lax.axis_size(axis)
    return lax.ppermute(values, axis, [(i, i ^ shift) for i in range(count)])


def trade(values, axis, split, concat):
    return lax.all_to_all(values, axis, split_axis=split, concat_axis=concat, tiled=True)


def after(values, *earlier):
    return lax.optimization_barrier((values, earlier))[0]


PLANE = ("core", "dp")


def chips_gather(block, axis="dp"):
    return [block] + [other(block, axis, m) for m in range(1, lax.axis_size(axis))]


def plane_gather(block):
    mine = jnp.stack(chips_gather(block))
    return mine, other(mine, "core", 1)


def plane_reduce(mine, theirs):
    sums = mine + wide(other(low(theirs), "core", 1))
    total = sums[0]
    for m in range(1, sums.shape[0]):
        total = total + wide(other(low(sums[m]), "dp", m))
    return total


def swap_planes(values, hop=0):
    pieces, planes, cores = (lax.axis_size(axis) for axis in ("dp", "z", "core"))
    pairs = [
        (((d ^ hop) * planes + z) * cores + c, (z * planes + d) * cores + c)
        for d in range(pieces)
        for z in range(planes)
        for c in range(cores)
    ]
    return lax.ppermute(values, ("dp", "z", "core"), pairs)


def put_blocks(blocks, axis, dimension):
    size = blocks[0].shape[dimension]
    shape = list(blocks[0].shape)
    shape[dimension] = size * len(blocks)
    whole = jnp.zeros(shape, blocks[0].dtype)
    for m, block in enumerate(blocks):
        start = [0] * len(shape)
        start[dimension] = (lax.axis_index(axis) ^ m) * size
        whole = lax.dynamic_update_slice(whole, block, start)
    return whole


def sum_all(values):
    for axis in ("core", "dp", "z"):
        shift = 1
        while shift < lax.axis_size(axis):
            values = values + other(values, axis, shift)
            shift *= 2
    return values


def document_edges(ids, memory_ids, steps):
    documents = jnp.arange(4, dtype=jnp.int32)
    starts = jnp.sum((memory_ids[None] < documents[:, None]).astype(jnp.int32), axis=1)
    ends = jnp.sum((memory_ids[None] <= documents[:, None]).astype(jnp.int32), axis=1) - 1
    match = ids[None] == documents[:, None]
    first = jnp.sum(jnp.where(match, starts[:, None], 0), axis=0)
    last = jnp.sum(jnp.where(match, ends[:, None], 0), axis=0)
    return (first.reshape(steps, 1, -1), last.reshape(steps, 1, -1))


def shards(
    inputs,
    encoder_states,
    segment_ids,
    encoder_ids,
    norm_gains,
    norm_shifts,
    attend_weights,
    attend_output,
    attend_biases,
    cross_query,
    cross_memory,
    cross_output,
    cross_biases,
    expand_weight,
    expand_bias,
    shrink_weight,
    shrink_bias,
    output_cotangent,
):
    pieces, planes, cores = lax.axis_size("dp"), lax.axis_size("z"), lax.axis_size("core")
    piece, plane, core = lax.axis_index("dp"), lax.axis_index("z"), lax.axis_index("core")
    members = pieces * cores
    member = core * pieces + piece
    row_count, model_width = inputs.shape[1:]
    memory_rows = encoder_states.shape[1]
    pack_rows, pack_memory = segment_ids.shape[1], encoder_ids.shape[1]
    heads = HEADS // members
    head_size = model_width // HEADS
    width = heads * head_size
    steps = planes * cores
    unit_count = expand_weight.shape[1]
    block_units = unit_count // pieces
    block_rows = model_width // pieces

    all_ids = swap_planes(jnp.concatenate([segment_ids[0], encoder_ids[0]]))
    pack_ids, memory_ids = all_ids[:pack_rows], all_ids[pack_rows:]
    attend_at = lax.all_gather(attend_weights.T, "z", axis=0, tiled=True)
    raw = trade(after(trade(inputs[0], "dp", 0, 0), attend_at), "z", 0, 0)

    def columns_of(weight, count):
        weight = weight.reshape(pieces, heads, count, head_size, block_rows)
        return weight.transpose(2, 1, 3, 0, 4).reshape(count * width, model_width)

    near_w = jnp.concatenate([cross_memory.T, attend_output, cross_query.T, cross_output])
    near_w = lax.all_gather(after(near_w, attend_at), "z", axis=0, tiled=True)
    near_w = near_w.reshape(planes, 5 * width, block_rows)
    attend_w = trade(after(attend_at, raw), "dp", 0, 0).reshape(pieces, 3 * width, block_rows)
    upstream = trade(after(output_cotangent[0], attend_w), "dp", 0, 0)
    squares = near_w[:, 2 * width :].reshape(planes, 3, width, block_rows)
    cross_kv = near_w[:, : 2 * width].reshape(planes * 2 * width, block_rows)
    unit_w = jnp.stack([expand_weight.T, shrink_weight], axis=1)
    unit_parts = []
    for m in range(pieces):
        part = lax.dynamic_slice_in_dim(unit_w, (piece ^ m) * block_units, block_units, 0)
        unit_parts.append(part if m == 0 else other(part, "dp", m))
    unit_w = put_blocks(unit_parts, "dp", 2).reshape(block_units, 2 * model_width)
    states = swap_planes(after(encoder_states[0], raw))
    whole_units = lax.all_gather(after(unit_w, near_w), "z", axis=0, tiled=True)
    expand_t, shrink_w = whole_units[:, :model_width], whole_units[:, model_width:]
    attend_w = columns_of(attend_w, 3)

    own = jnp.stack([core, piece]).astype(jnp.int32)
    key_block = min(256, pack_rows)
    self_first, _ = document_edges(pack_ids, pack_ids, steps)
    self_last = jnp.arange(pack_rows, dtype=jnp.int32).reshape(steps, 1, -1)
    self_scalars = jnp.concatenate(
        [own, self_first[:, 0, 0] // key_block, self_last[:, 0, -1] // key_block]
    )
    cross_first, cross_last = document_edges(pack_ids, memory_ids, steps)
    key_block = min(256, pack_memory)
    cross_scalars = jnp.concatenate(
        [own, cross_first[:, 0, 0] // key_block, cross_last[:, 0, -1] // key_block]
    )

    gain_rows, shift_rows = wide(norm_gains), wide(norm_shifts)
    bias_self, bias_cross = wide(attend_biases), wide(cross_biases)

    def of_heads(row):
        return lax.dynamic_slice_in_dim(row, (piece * cores + core) * width, width, 0)

    def place_heads(row):
        return lax.dynamic_update_slice(
            jnp.zeros((model_width,), jnp.float32), row, ((piece * cores + core) * width,)
        )

    zero_heads = jnp.zeros((width,), jnp.float32)
    packed_bias = jnp.concatenate([of_heads(bias_self[0]), zero_heads, of_heads(bias_self[1])])
    memory_bias = jnp.concatenate([zero_heads, of_heads(bias_cross[1])])
    query_bias = bias_cross[0].reshape(pieces, cores, 1, width).transpose(1, 0, 2, 3)
    token_shape = (cores, pieces, row_count, width)
    part_shape = (cores, pieces, planes, row_count // planes, width)
    flat_shape = (row_count, model_width)
    flat_float = jax.ShapeDtypeStruct(flat_shape, jnp.float32)
    flat_low = jax.ShapeDtypeStruct(flat_shape, jnp.bfloat16)
    head_low = jax.ShapeDtypeStruct(token_shape, jnp.bfloat16)
    three_rows = jax.ShapeDtypeStruct((3, model_width), jnp.float32)

    def exchange(values):
        return trade(values.reshape(pieces * cores * row_count, width), PLANE, 0, 0).reshape(
            token_shape
        )

    low_one = low(layer_norm(wide(raw), gain_rows[0], shift_rows[0]))
    mine = jnp.stack(chips_gather(after(low_one, unit_w)))
    mine, states = after((mine, states), attend_w, near_w)
    squares = after(squares, mine)
    upstream = trade(upstream, "z", 0, 0)
    state_parts = chips_gather(after(states, mine))
    squares = after(squares, state_parts)
    ones = (mine, other(mine, "core", 1))
    square_parts = chips_gather(squares)
    query1, key1, value1, context1, kept1, lse1 = self_forward(
        self_scalars, *ones, planes, attend_w, packed_bias[None], self_first, self_last
    )
    context1, square_parts = after((context1, square_parts), upstream)
    squares = jnp.stack(square_parts)
    squares = (squares, other(squares, "core", 1))
    mixed1 = exchange(context1)
    cross_kv = trade(after(cross_kv, mixed1), "dp", 0, 0).reshape(pieces, 2 * width, block_rows)
    cross_kv = columns_of(cross_kv, 2)
    middle, low_two, query2 = single(
        middle_kernel,
        [flat_float, flat_low, head_low],
        [None, kind_spec(squares[0], 0), kind_spec(squares[1], 0), None, None]
        + [kind_spec(squares[0], 1), kind_spec(squares[1], 1), None],
        [],
        own, mixed1, *squares, raw,
        jnp.stack([bias_self[2], gain_rows[1], shift_rows[1]]),
        *squares, query_bias,
    )

    all_states = jnp.stack(state_parts)
    all_states = (all_states, other(after(all_states, mixed1), "core", 1))
    query2 = exchange(query2)
    query2 = query2.reshape(part_shape)
    key2, value2, context2, kept2, lse2 = cross_forward(
        cross_scalars, query2, *all_states, cross_kv, memory_bias[None],
        cross_first, cross_last,
    )
    ups = chips_gather(after(upstream, query2))
    context2, ups = after((context2, ups))
    ups = jnp.stack(ups)
    all_ups = (ups, other(ups, "core", 1))
    context2 = after(context2, whole_units)
    mixed2 = exchange(context2)
    later, low_three = single(
        later_kernel,
        [flat_float, flat_low],
        [None, kind_spec(squares[0], 2), kind_spec(squares[1], 2), None, None],
        [],
        own, mixed2, *squares, middle,
        jnp.stack([bias_cross[2], gain_rows[2], shift_rows[2]]),
    )

    bias_units = wide(expand_bias).reshape(planes, cores, pieces, block_units)
    bias_units = lax.dynamic_slice(
        bias_units, (0, core, piece, 0), (planes, 1, 1, block_units)
    ).reshape(1, unit_count)
    groups = [list(range(pieces - 1)), [pieces - 1]]
    pieces3 = chips_gather(low_three)
    threes, actives, d_hiddens, parts3, leaving, out_groups = [], [], [], [], [], []
    for group in groups:
        mine = jnp.stack([pieces3[m] for m in group])
        if d_hiddens:
            mine = after(mine, d_hiddens[-1])
        theirs = other(mine, "core", 1)
        active, d_hidden, d_mine, d_theirs, out_mine, out_theirs = units_group(
            own, mine, theirs, all_ups, group[0], expand_t, shrink_w, bias_units
        )
        d_sum = d_mine + wide(other(d_theirs, "core", 1))
        for i, m in enumerate(group):
            leaving.append(d_sum[i] if m == 0 else low(d_sum[i]))
            parts3.append(leaving[-1] if m == 0 else other(leaving[-1], "dp", m))
        threes.append((mine, theirs))
        out_groups.append((out_mine, out_theirs))
        actives.append(active)
        d_hiddens.append(d_hidden)
    actives, d_hiddens = after((actives, d_hiddens), leaving)

    unit_grads = unit_gradients(own, d_hiddens, actives, threes, all_ups)
    unit_grads, parts3 = after((unit_grads, parts3))
    unit_grads = lax.psum_scatter(unit_grads, "z", scatter_dimension=0, tiled=True)
    unit_sums = sum(jnp.sum(wide(d), axis=(0, 1, 2)) for d in d_hiddens)
    d_later, low_later, d_context2, sums3 = single(
        later_back_kernel,
        [flat_float, flat_low, head_low, three_rows],
        [None] * (pieces + 3) + [kind_spec(squares[0], 2), kind_spec(squares[1], 2)],
        [],
        own, *parts3, upstream, later, gain_rows[2:3], *squares,
    )

    out_groups = [
        mine + wide(other(after(theirs, low_later), "core", 1)) for mine, theirs in out_groups
    ]
    outs = [group[i] for group in out_groups for i in range(group.shape[0])]
    d_context2 = exchange(d_context2)
    leaving = after([low(out) for out in outs[1:]], d_context2)
    out_parts = [other(out, "dp", m + 1) for m, out in enumerate(leaving)]
    d_query2, d_memory, d_memory_t = attend_back(
        cross_scalars, query2, key2, value2, d_context2.reshape(part_shape), kept2, lse2,
        cross_first, cross_last,
    )
    d_mixed2 = exchange(after(d_query2, out_parts))
    layer_rows = low(later + outs[0] + sum(wide(part) for part in out_parts) + wide(shrink_bias))
    d_middle, low_middle, d_context1, sums2 = single(
        middle_back_kernel,
        [flat_float, flat_low, head_low, three_rows],
        [None, kind_spec(squares[0], 1), kind_spec(squares[1], 1), None, None, None]
        + [kind_spec(squares[0], 0), kind_spec(squares[1], 0)],
        [pltpu.VMEM(flat_shape, jnp.float32)],
        own, d_mixed2, *squares, d_later, middle, gain_rows[1:2], *squares,
    )
    d_context1, unit_grads = after((exchange(d_context1), unit_grads))

    def turned_grad(columns, rows):
        half = columns.shape[1] // cores
        return low(
            sum(
                product(columns[:, j * half : (j + 1) * half], rows[j].reshape(half, model_width))
                for j in range(cores)
            )
        )

    def to_chips(*grads):
        split = [grad.reshape(-1, pieces, block_rows) for grad in grads]
        return trade(jnp.concatenate(split).transpose(1, 0, 2), "dp", 0, 0)

    unit_grads = to_chips(
        unit_grads.reshape(2 * block_units, model_width),
        turned_grad(after(d_memory_t, d_context1), all_states),
    )
    d_mine, d_theirs, d_query1, d_query1_t, d_memory1, d_memory1_t = attend_back(
        self_scalars, query1.reshape(part_shape), key1, value1, d_context1.reshape(part_shape), kept1, lse1,
        self_first, self_last, attend_w,
    )
    d_mine, d_theirs, d_query1_t, d_memory1_t, unit_grads = after(
        (d_mine, d_theirs, d_query1_t, d_memory1_t, unit_grads)
    )
    cross_sum = unit_grads[:, 2 * block_units :]
    unit_grads = unit_grads[:, : 2 * block_units].reshape(unit_count, 2, block_rows)
    d_theirs = other(d_theirs, "core", 1)
    d_sum = [d_mine[m] + wide(d_theirs[m]) for m in range(pieces)]
    leaving = [low(d_sum[m]) for m in range(1, pieces)]
    parts1 = [d_sum[0]] + [other(part, "dp", m + 1) for m, part in enumerate(leaving)]

    d_memory, low_middle_late, layer_rows, turned_late = after(
        (d_memory, low_middle, layer_rows, (d_query1_t, d_memory1_t)), leaving
    )
    layer_first = trade(layer_rows, "z", 0, 0)
    d_states = [
        product(part.reshape(-1, 2 * width), cross_kv).reshape(pieces, memory_rows, model_width)
        for part in d_memory
    ]
    d_states = d_states[0] + wide(other(low(d_states[1]), "core", 1))
    kinds = 3
    square_shape = (pieces, planes, kinds, width, block_rows)
    square_mine, square_theirs = single(
        square_grad_kernel,
        [
            jax.ShapeDtypeStruct(square_shape, jnp.bfloat16),
            jax.ShapeDtypeStruct(square_shape, jnp.bfloat16),
        ],
        [None] * 6,
        [],
        own, mixed1, low_middle_late, d_mixed2, low_two, mixed2, low_later,
    )
    attend_sum = [turned_grad(turned, ones) for turned in turned_late]
    parts1, layer_first, d_states, square_mine, square_theirs, attend_sum = after(
        (parts1, layer_first, d_states, square_mine, square_theirs, attend_sum)
    )
    attend_sum = to_chips(*attend_sum)
    square_theirs = other(square_theirs, "core", 1)
    square_sums = [wide(square_mine[m]) + wide(square_theirs[m]) for m in range(pieces)]
    square_parts = [other(low(square_sums[m]), "dp", m) for m in range(1, pieces)]
    state_parts = [
        other(after(low(d_states[m]), square_parts), "dp", m) for m in range(1, pieces)
    ]
    encoder_rows = low(d_states[0] + sum(wide(part) for part in state_parts))
    encoder_gradient = swap_planes(encoder_rows)[None]
    square_sum = square_sums[0] + sum(wide(part) for part in square_parts)
    input_gradient, sums1 = single(
        input_back_kernel,
        [flat_low, jax.ShapeDtypeStruct((2, model_width), jnp.float32)],
        [None] * (pieces + 3),
        [],
        own, *parts1, d_middle, raw, gain_rows[0:1],
    )
    input_gradient = trade(trade(after(input_gradient, attend_sum), "z", 0, 0), "dp", 0, 0)[None]
    layer_output = trade(after(layer_first, input_gradient), "dp", 0, 0)[None]

    tail = jnp.concatenate(
        [low(square_sum).reshape(planes, 3 * width, block_rows), cross_sum, attend_sum], axis=1
    )
    tail = sum(
        wide(part if m == 0 else other(part, "z", m))
        for m, part in enumerate(
            lax.dynamic_index_in_dim(tail, plane ^ m, 0, keepdims=False) for m in range(planes)
        )
    )
    square_sum = tail[: 3 * width].reshape(3, width, block_rows)
    cross_sum, attend_sum = tail[3 * width : 5 * width], tail[5 * width :]
    unit_grads = wide(unit_grads)

    def weight_order(turned, count):
        turned = turned.reshape(count, heads, head_size, block_rows).transpose(3, 1, 0, 2)
        return turned.reshape(block_rows, count * width)

    unit_sums = lax.dynamic_update_slice(
        jnp.zeros((planes, cores, pieces, block_units), jnp.float32),
        unit_sums.reshape(planes, 1, 1, block_units),
        (0, core, piece, 0),
    ).reshape(-1)
    small = jnp.concatenate(
        [
            sums2[0],
            sums3[0],
            sums2[1],
            sums3[1],
            sums2[2],
            jnp.sum(wide(d_mixed2), axis=2).transpose(1, 0, 2).reshape(-1),
            place_heads(jnp.sum(wide(d_memory_t[width:]), axis=1)),
            sums3[2],
            jnp.sum(wide(upstream), axis=0),
            unit_sums,
        ]
    )
    last = jnp.stack(
        [
            sums1[0],
            sums1[1],
            place_heads(jnp.sum(wide(d_query1_t), axis=1)),
            place_heads(jnp.sum(wide(d_memory1_t[width:]), axis=1)),
        ]
    )
    small = sum_all(jnp.concatenate([last.reshape(-1), small]).reshape(-1, 128)).reshape(-1)
    last, small = small[: 4 * model_width].reshape(4, model_width), small[4 * model_width :]
    rows = small[: 9 * model_width].reshape(9, model_width)
    return (
        layer_output,
        input_gradient,
        encoder_gradient,
        jnp.concatenate([last[0:1], rows[0:2]]),
        jnp.concatenate([last[1:2], rows[2:4]]),
        weight_order(attend_sum, 3),
        square_sum[0],
        jnp.concatenate([last[2:4], rows[4:5]]),
        square_sum[1].T,
        weight_order(cross_sum, 2),
        square_sum[2],
        rows[5:8],
        unit_grads[:, 0].T,
        small[9 * model_width :],
        unit_grads[:, 1],
        rows[8],
    )


def solution(mesh):
    pieces, sequence = mesh.devices.shape
    planes = Mesh(mesh.devices.reshape(pieces, sequence // 2, 2), ("dp", "z", "core"))
    seq = ("z", "core")
    in_specs = (
        P("dp", seq, None),
        P("dp", seq, None),
        P("dp", None),
        P("dp", None),
        P(),
        P(),
        P("dp", seq),
        P(seq, "dp"),
        P(),
        P("dp", seq),
        P("dp", seq),
        P(seq, "dp"),
        P(),
        P("dp", seq),
        P(),
        P(seq, "dp"),
        P(),
        P("dp", seq, None),
    )
    out_specs = (
        P("dp", seq, None),
        P("dp", seq, None),
        P("dp", seq, None),
        P(),
        P(),
        P("dp", seq),
        P(seq, "dp"),
        P(),
        P("dp", seq),
        P("dp", seq),
        P(seq, "dp"),
        P(),
        P("dp", seq),
        P(),
        P(seq, "dp"),
        P(),
    )
    return jax.shard_map(
        shards, mesh=planes, in_specs=in_specs, out_specs=out_specs, check_vma=False
    )
```
